32 devices in a mesh: exp: 8 (over z, x), tp: 4 (over y, core).
Axes of the slice: x: 2, y: 2, z: 4, core: 2. Of those that a mesh axis runs over, the one named last changes fastest.
Arguments:
- tokens: bfloat16 [4096, 2048], P('exp'), may hold values from -6 to 6
- cotangent: bfloat16 [4096, 2048], P('exp'), may hold values from -6 to 6
- lengths: int32 [1], replicated, may hold values from 1024 to 4096, as said below
- routes: int32 [4096, 4], P('exp'), may hold values from 0 to 15, all different within a row; in each aligned block of 512 rows (0 to 511, 512 to 1023, ...) at most 256 rows name the same one
- w_query: bfloat16 [2048, 2048], P('exp', 'tp'), may hold values from -0.125 to 0.125
- w_key: bfloat16 [2048, 2048], P('exp', 'tp'), may hold values from -0.125 to 0.125
- w_value: bfloat16 [2048, 2048], P('exp', 'tp'), may hold values from -0.125 to 0.125
- w_out: bfloat16 [2048, 2048], P('tp', 'exp'), may hold values from -0.75 to 0.75
- b_query: bfloat16 [2048], P(('tp', 'exp')), may hold values from -3 to 3
- b_key: bfloat16 [2048], P(('tp', 'exp')), may hold values from -3 to 3
- b_value: bfloat16 [2048], P(('tp', 'exp')), may hold values from -3 to 3
- gain_attention: bfloat16 [2048], P('exp'), may hold values from 0.5 to 1.5
- gain_experts: bfloat16 [2048], P('exp'), may hold values from 0.5 to 1.5
- w_router: bfloat16 [2048, 16], P('exp'), may hold values from -0.0625 to 0.0625
- w_shared_gate: bfloat16 [2048], P('exp'), may hold values from -0.125 to 0.125
- shared_gate: bfloat16 [2048, 5632], P('exp', 'tp'), may hold values from -0.125 to 0.125
- shared_up: bfloat16 [2048, 5632], P('exp', 'tp'), may hold values from -0.125 to 0.125
- shared_down: bfloat16 [5632, 2048], P('tp', 'exp'), may hold values from -0.15625 to 0.15625
- expert_gate: bfloat16 [16, 2048, 1408], P('exp', None, 'tp'), may hold values from -0.125 to 0.125
- expert_up: bfloat16 [16, 2048, 1408], P('exp', None, 'tp'), may hold values from -0.125 to 0.125
- expert_down: bfloat16 [16, 1408, 2048], P('exp', 'tp'), may hold values from -0.625 to 0.625
Outputs:
- mixed: bfloat16 [4096, 2048], P('exp')
- grad_tokens: bfloat16 [4096, 2048], P('exp')
- grad_w_query: float32 [2048, 2048], P('exp', 'tp')
- grad_w_key: float32 [2048, 2048], P('exp', 'tp')
- grad_w_value: float32 [2048, 2048], P('exp', 'tp')
- grad_w_out: float32 [2048, 2048], P('tp', 'exp')
- grad_b_query: float32 [2048], P(('tp', 'exp'))
- grad_b_key: float32 [2048], P(('tp', 'exp'))
- grad_b_value: float32 [2048], P(('tp', 'exp'))
- grad_gain_attention: float32 [2048], P('exp')
- grad_gain_experts: float32 [2048], P('exp')
- grad_w_router: float32 [2048, 16], P('exp')
- grad_w_shared_gate: float32 [2048], P('exp')
- grad_shared_gate: float32 [2048, 5632], P('exp', 'tp')
- grad_shared_up: float32 [2048, 5632], P('exp', 'tp')
- grad_shared_down: float32 [5632, 2048], P('tp', 'exp')
- grad_expert_gate: float32 [16, 2048, 1408], P('exp', None, 'tp')
- grad_expert_up: float32 [16, 2048, 1408], P('exp', None, 'tp')
- grad_expert_down: float32 [16, 1408, 2048], P('exp', 'tp')
- rms_output: float32 [], replicated
- rms_grad: float32 [], replicated
The draws below stay inside these ranges and needn't reach their ends.
Inputs may be any that keep to these rules, and one draw needn't show every extreme that they name: `lengths`: every sequence's length; one sequence, drawn from the seed, fills all 4096 slots. `routes`: within the 512 rows of one index of exp no expert is named by more than 256 rows, a bound that some block reaches.
All inputs are finite; a program needn't handle non-finite values.
Results may differ from the reference program's by a relative error of at most 0.034.
Values may be sent and summed in bfloat16 or wider, within the bound.
A program may use at most 384 MiB of HBM per device.

```python
import math
import jax
import jax.numpy as jnp
import numpy as np
from jax import lax

D = 2048
HEADS = 16
HEAD_DIM = 128
EXP_FF = 1408
SHARED_FF = 5632
TOPK = 4
TOK_DEV = 512
SLOT = 4096
MIN_LEN = 1024
EXPERTS = 16
CAP = 256
TOKENS = 4096
SEQS = 1
N_EXP = 8


def draw_lengths(key, part):
    key = jax.random.fold_in(key, 11)
    first_key, second_key = jax.random.split(key)
    drawn = jax.random.randint(first_key, (SEQS,), MIN_LEN, SLOT + 1)
    longest = jax.random.randint(second_key, (), 0, SEQS)
    return jnp.where(jnp.arange(SEQS) == longest, SLOT, drawn).astype(jnp.int32)


def block_scale(key, shape, shards, least, largest):
    def one(position, blocks):
        heights = jax.random.uniform(jax.random.fold_in(jax.random.fold_in(key, 6), position), (blocks,), jnp.float32, least / len(shards), largest / len(shards))
        return jnp.repeat(jnp.exp(heights), shape[position] // blocks).reshape((-1,) + (1,) * (len(shape) - position - 1))

    loudness = one(*shards[0])
    for cut in shards[1:]:
        loudness = loudness * one(*cut)
    return loudness


def routed_block(stream_key, own, number, rows, count, top, bound, lean):
    sequence = jax.random.permutation(stream_key, count)
    heavy_load, usual = shares(count, rows * top, bound, lean, True), shares(count, rows * top, bound, lean, False)
    places = jnp.arange(count)

    def named(sizes, turn):
        used = int((sizes > 0).sum())
        fixed = max(1, used // 4)
        shifted = fixed + (places - fixed + turn * (used - fixed)) % max(1, count - fixed)
        return jnp.zeros((count,), jnp.int32).at[sequence[jnp.where(places < fixed, places, shifted)]].set(jnp.asarray(sizes, jnp.int32))

    sizes = jnp.where(number % 4 == 0, named(heavy_load, number // 4), named(usual, number - number // 4 - 1))
    mixed = jax.random.permutation(jax.random.fold_in(own, 3), count)
    donor, receiver = mixed[0:count // 2 * 2:2], mixed[1:count // 2 * 2:2]
    slack = jnp.minimum(sizes[donor] - 1, bound - sizes[receiver]) // 2
    slack = jnp.where((donor == sequence[0]) | (receiver == sequence[0]) | (sizes[receiver] == 0), 0, jnp.maximum(slack, 0))
    shifted = jax.random.randint(jax.random.fold_in(own, 4), (count // 2,), 0, 1 << 20) % (slack + 1)
    sizes = sizes.at[donor].add(-shifted).at[receiver].add(shifted)
    labels = jnp.searchsorted(jnp.cumsum(sizes), jnp.arange(rows * top), side="right").astype(jnp.int32)
    grid = labels.reshape(top, rows).T
    grid = grid[jax.random.permutation(jax.random.fold_in(own, 1), rows)]
    turn = jax.random.randint(jax.random.fold_in(own, 2), (rows, 1), 0, top)
    return jnp.take_along_axis(grid, (jnp.arange(top)[None, :] + turn) % top, axis=1)


def shares(number_of, total, bound, slope, full):
    loads = [(1 << 20) // math.isqrt(grade ** slope) + 1 for grade in range(1, number_of + 1)]
    largest = bound if full else min(bound, max(-(-total // number_of), total * loads[0] // sum(loads)))
    least = 1 if total - largest >= number_of - 1 else 0
    counts, surplus = [largest] + [least] * (number_of - 1), total - largest - least * (number_of - 1)
    while surplus > 0:
        candidates = [i for i in range(1, number_of) if counts[i] < largest] or [i for i in range(1, number_of) if counts[i] < bound]
        whole, left = sum([loads[i] for i in candidates]), surplus
        for i in candidates:
            extra = min(bound - counts[i], max(1, left * loads[i] // whole), surplus)
            counts[i] = counts[i] + extra
            surplus = surplus - extra
    return np.array(counts)


def normal_values(key, dims, width, limit, cuts=(), held_as=jnp.bfloat16):
    values = width * jax.random.normal(key, dims, jnp.float32)
    if cuts:
        values = values * block_scale(key, dims, cuts, -0.22, 0.18)
    return jnp.clip(values, -limit, limit).astype(held_as)


def setup_inputs(seed: int = 0) -> dict:
    key_list = jax.random.split(jax.random.key(seed), 22)
    tokens = normal_values(key_list[0], (TOKENS, D), 1.0, 6.0, ((0, 8),))
    cotangent = normal_values(key_list[1], (TOKENS, D), 1.0, 6.0, ((0, 8),))
    lengths = draw_lengths(jax.random.fold_in(key_list[21], 71), 0)
    routes_keys = jax.random.split(jax.random.fold_in(key_list[3], 1), TOKENS // TOK_DEV)
    routes_turns = jax.random.permutation(jax.random.fold_in(key_list[3], 3), TOKENS // TOK_DEV)
    routes = jax.vmap(lambda own, number: routed_block(jax.random.fold_in(key_list[3], 2), own, number, TOK_DEV, EXPERTS, TOPK, CAP, 1))(routes_keys, routes_turns).reshape((TOKENS, TOPK))
    w_query = normal_values(key_list[4], (D, D), D ** -0.5, 0.125, ((0, 8), (1, 4)))
    w_key = normal_values(key_list[5], (D, D), D ** -0.5, 0.125, ((0, 8), (1, 4)))
    w_value = normal_values(key_list[6], (D, D), D ** -0.5, 0.125, ((0, 8), (1, 4)))
    w_out = normal_values(key_list[7], (D, D), (D // 32) ** -0.5, 0.75, ((0, 4), (1, 8)))
    b_query = normal_values(key_list[8], (D,), 0.5, 3.0, ((0, 32),))
    b_key = normal_values(key_list[9], (D,), 0.5, 3.0, ((0, 32),))
    b_value = normal_values(key_list[10], (D,), 0.5, 3.0, ((0, 32),))
    gain_attention = jnp.clip(1.0 + 0.1 * jax.random.normal(key_list[11], (D,), jnp.float32), 0.5, 1.5).astype(jnp.bfloat16)
    gain_experts = jnp.clip(1.0 + 0.1 * jax.random.normal(key_list[12], (D,), jnp.float32), 0.5, 1.5).astype(jnp.bfloat16)
    w_router = normal_values(key_list[13], (D, EXPERTS), (4 * D) ** -0.5, 0.0625, ((0, 8),))
    w_shared_gate = normal_values(key_list[14], (D,), D ** -0.5, 0.125, ((0, 8),))
    shared_gate = normal_values(key_list[15], (D, SHARED_FF), D ** -0.5, 0.125, ((0, 8), (1, 4)))
    shared_up = normal_values(key_list[16], (D, SHARED_FF), D ** -0.5, 0.125, ((0, 8), (1, 4)))
    shared_down = normal_values(key_list[17], (SHARED_FF, D), (SHARED_FF // 4) ** -0.5, 0.15625, ((0, 4), (1, 8)))
    expert_gate = normal_values(key_list[18], (EXPERTS, D, EXP_FF), D ** -0.5, 0.125, ((0, 8), (2, 4)))
    expert_up = normal_values(key_list[19], (EXPERTS, D, EXP_FF), D ** -0.5, 0.125, ((0, 8), (2, 4)))
    expert_down = normal_values(key_list[20], (EXPERTS, EXP_FF, D), (max(1, EXP_FF * TOPK * TOPK // (EXPERTS * EXPERTS))) ** -0.5, 0.625, ((0, 8), (1, 4)))
    return dict(tokens=tokens, cotangent=cotangent, lengths=lengths, routes=routes, w_query=w_query, w_key=w_key, w_value=w_value, w_out=w_out, b_query=b_query, b_key=b_key, b_value=b_value, gain_attention=gain_attention, gain_experts=gain_experts, w_router=w_router, w_shared_gate=w_shared_gate, shared_gate=shared_gate, shared_up=shared_up, shared_down=shared_down, expert_gate=expert_gate, expert_up=expert_up, expert_down=expert_down)


EPSILON = 1e-06
ROPE_BASE = 1000000.0
MASKED = -1e+30
PRECISE = lax.Precision.HIGHEST

@jax.custom_vjp
def low(v):
    return lax.optimization_barrier(v.astype(jnp.bfloat16)).astype(jnp.float32)

@jax.custom_vjp
def low_back(v):
    return v

def low_keep(v):
    return (low(v), None)

def low_pass(kept, grad):
    return (grad,)

def back_keep(v):
    return (v, None)

def back_low(kept, grad):
    return (low(grad),)
low.defvjp(low_keep, low_pass)
low_back.defvjp(back_keep, back_low)

def rope_tables(positions, head_dim):
    half_dim = head_dim // 2
    frequency = ROPE_BASE ** (-(jnp.arange(half_dim, dtype=jnp.float32) * 2.0) / head_dim)
    angles = positions.astype(jnp.float32)[:, None] * frequency[None, :]
    cosine = jnp.concatenate([jnp.cos(angles), jnp.cos(angles)], axis=1)
    sine_table = jnp.concatenate([jnp.sin(angles), jnp.sin(angles)], axis=1)
    return (cosine, sine_table)

def rotate(values, cosine, sine_table):
    half_dim = values.shape[-1] // 2
    turned = jnp.concatenate([-values[..., half_dim:], values[..., :half_dim]], axis=-1)
    return values * cosine[:, None, :] + turned * sine_table[:, None, :]

def rms_norm(values, gain):
    inverse = lax.rsqrt(lax.optimization_barrier(jnp.mean(values * values, axis=1, keepdims=True)) + EPSILON)
    return values * inverse * gain

def attend_block(query, keys, values, query_pos, length):
    key_pos = jnp.arange(keys.shape[0], dtype=jnp.int32)
    scores = jnp.einsum('qhd,khd->hqk', query, keys, precision=PRECISE) * (1.0 / HEAD_DIM ** 0.5)
    scores = low_back(scores)
    allowed = (key_pos[None, :] <= query_pos[:, None]) & (key_pos[None, :] < length)
    scores = jnp.where(allowed[None, :, :], scores, MASKED)
    peak_score = lax.optimization_barrier(jnp.max(scores, axis=2, keepdims=True))
    weights = jnp.exp(scores - peak_score)
    probabilities = low(weights / lax.optimization_barrier(jnp.sum(weights, axis=2, keepdims=True)))
    return jnp.einsum('hqk,khd->qhd', probabilities, values, precision=PRECISE)

def attend_sequence(sequence_pack):
    query, keys, values, length = sequence_pack
    block_rows = min(512, SLOT)
    block_count = SLOT // block_rows
    query_blocks = query.reshape(block_count, block_rows, HEADS, HEAD_DIM)
    position_blocks = jnp.arange(SLOT, dtype=jnp.int32).reshape(block_count, block_rows)

    def one_block(inputs_pair):
        return attend_block(inputs_pair[0], keys, values, inputs_pair[1], length)
    attended = lax.map(jax.checkpoint(one_block), (query_blocks, position_blocks))
    return attended.reshape(SLOT, HEADS, HEAD_DIM)

def reference(tokens, cotangent, lengths, routes, w_query, w_key, w_value, w_out, b_query, b_key, b_value, gain_attention, gain_experts, w_router, w_shared_gate, shared_gate, shared_up, shared_down, expert_gate, expert_up, expert_down):
    token_index = jnp.arange(TOKENS, dtype=jnp.int32)
    positions = token_index % SLOT
    sequence_of = token_index // SLOT
    valid_rows = (positions < lengths[sequence_of]).astype(jnp.float32)
    cosine, sine_table = rope_tables(positions, HEAD_DIM)
    flat_routes = routes.reshape(-1).astype(jnp.int32)
    pick_table = (flat_routes[:, None] == jnp.arange(EXPERTS, dtype=jnp.int32)[None, :]).astype(jnp.int32)
    rank_in_expert = lax.optimization_barrier(jnp.sum((jnp.cumsum(pick_table, axis=0) - 1) * pick_table, axis=1)).astype(jnp.int32)
    slot_room = CAP * N_EXP
    pair_count = TOKENS * TOPK
    slot_table = jnp.full((EXPERTS * slot_room,), pair_count, jnp.int32)
    slot_table = slot_table.at[flat_routes * slot_room + rank_in_expert].set(jnp.arange(pair_count, dtype=jnp.int32))
    slot_table = slot_table.reshape(EXPERTS, slot_room)
    token_of = jnp.where(slot_table < pair_count, slot_table // TOPK, TOKENS).astype(jnp.int32)

    def layer(input_rows, query_weight, key_weight, value_weight, out_weight, query_bias, key_bias, value_bias, attn_gain, ffn_gain, router_weight, share_vector, share_gate_weight, share_up_weight, share_down_weight, gate_stack, up_stack, down_stack):
        normed_first = low(rms_norm(input_rows, attn_gain))
        query_lin = low_back(jnp.dot(normed_first, query_weight, precision=PRECISE) + query_bias)
        key_lin = low_back(jnp.dot(normed_first, key_weight, precision=PRECISE) + key_bias)
        value_lin = low_back(jnp.dot(normed_first, value_weight, precision=PRECISE) + value_bias)
        query_rot = low(rotate(query_lin.reshape(TOKENS, HEADS, HEAD_DIM), cosine, sine_table))
        key_rot = low(rotate(key_lin.reshape(TOKENS, HEADS, HEAD_DIM), cosine, sine_table))
        value_low = low(value_lin.reshape(TOKENS, HEADS, HEAD_DIM))
        attended = lax.map(attend_sequence, (query_rot.reshape(SEQS, SLOT, HEADS, HEAD_DIM), key_rot.reshape(SEQS, SLOT, HEADS, HEAD_DIM), value_low.reshape(SEQS, SLOT, HEADS, HEAD_DIM), lengths))
        attended = low(low_back(attended.reshape(TOKENS, D)))
        hidden_state = input_rows + low_back(jnp.dot(attended, out_weight, precision=PRECISE))
        normed = low(rms_norm(hidden_state, ffn_gain))
        logits = low_back(jnp.dot(normed, router_weight, precision=PRECISE))
        router_probs = jax.nn.softmax(logits, axis=1)
        gates = jnp.take_along_axis(router_probs, routes, axis=1)
        share_weight = jax.nn.sigmoid(low_back(jnp.dot(normed, share_vector, precision=PRECISE)))
        share_pre = low_back(jnp.dot(normed, share_gate_weight, precision=PRECISE))
        share_lin = low_back(jnp.dot(normed, share_up_weight, precision=PRECISE))
        share_hidden = low(low_back(jax.nn.silu(share_pre) * share_lin))
        share_out = low_back(jnp.dot(share_hidden, share_down_weight, precision=PRECISE))
        padded_normed = jnp.concatenate([normed, jnp.zeros((1, D), normed.dtype)], axis=0)

        def expert_pass(expert_stack):
            row_index, gate_weight, up_weight, down_weight = expert_stack
            expert_rows = padded_normed[row_index]
            gate_pre = low_back(jnp.dot(expert_rows, gate_weight, precision=PRECISE))
            up_pre = low_back(jnp.dot(expert_rows, up_weight, precision=PRECISE))
            expert_hidden = low(low_back(jax.nn.silu(gate_pre) * up_pre))
            return low_back(jnp.dot(expert_hidden, down_weight, precision=PRECISE))
        expert_outs = lax.map(jax.checkpoint(expert_pass), (token_of, gate_stack, up_stack, down_stack))
        padded_gates = jnp.concatenate([gates.reshape(-1), jnp.zeros((1,), gates.dtype)])
        weighted = expert_outs * padded_gates[slot_table][:, :, None]
        mixture = jnp.zeros((TOKENS + 1, D), expert_outs.dtype).at[token_of.reshape(-1)].add(weighted.reshape(-1, D))[:TOKENS]
        return valid_rows[:, None] * (hidden_state + mixture + share_weight[:, None] * share_out)
    floats = (tokens.astype(jnp.float32), w_query.astype(jnp.float32), w_key.astype(jnp.float32), w_value.astype(jnp.float32), w_out.astype(jnp.float32), b_query.astype(jnp.float32), b_key.astype(jnp.float32), b_value.astype(jnp.float32), gain_attention.astype(jnp.float32), gain_experts.astype(jnp.float32), w_router.astype(jnp.float32), w_shared_gate.astype(jnp.float32), shared_gate.astype(jnp.float32), shared_up.astype(jnp.float32), shared_down.astype(jnp.float32), expert_gate.astype(jnp.float32), expert_up.astype(jnp.float32), expert_down.astype(jnp.float32))
    output, pull = jax.vjp(layer, *floats)
    grads = pull(cotangent.astype(jnp.float32))
    count_cells = jnp.sum(lengths).astype(jnp.float32) * D
    rms_output = jnp.sqrt(jnp.sum(output * output) / count_cells)
    rms_grad = jnp.sqrt(jnp.sum(grads[0] * grads[0]) / count_cells)
    return (output.astype(jnp.bfloat16), grads[0].astype(jnp.bfloat16), grads[1], grads[2], grads[3], grads[4], grads[5], grads[6], grads[7], grads[8], grads[9], grads[10], grads[11], grads[12], grads[13], grads[14], grads[15], grads[16], grads[17], rms_output, rms_grad)
```

```python
import functools

import jax
import jax.numpy as jnp
from jax import lax
from jax.experimental import pallas as pl
from jax.experimental.pallas import tpu as pltpu
from jax.sharding import Mesh
from jax.sharding import PartitionSpec as P

HEAD_DIM = 128
SLOT = 4096


EPSILON = 1e-06
ROPE_BASE = 1000000.0
MASKED = -1e30


def shifted(shard, axis, by):
    length = lax.axis_size(axis)
    pairs = [(i, i + by) for i in range(length) if 0 <= i + by < length]
    return lax.ppermute(shard, axis, pairs)


def rope_tables(positions, head_dim):
    half_dim = head_dim // 2
    frequency = ROPE_BASE ** (-(jnp.arange(half_dim, dtype=jnp.float32) * 2.0) / head_dim)
    angles = positions.astype(jnp.float32)[:, None] * frequency[None, :]
    cosine = jnp.concatenate([jnp.cos(angles), jnp.cos(angles)], axis=1)
    sine_table = jnp.concatenate([jnp.sin(angles), jnp.sin(angles)], axis=1)
    return (cosine, sine_table)


def rotate(values, cosine, sine_table):
    half_dim = values.shape[-1] // 2
    turned = jnp.concatenate([-values[..., half_dim:], values[..., :half_dim]], axis=-1)
    return values * cosine[:, None, :] + turned * sine_table[:, None, :]


def rotate_back(grads, cosine, sine_table):
    half_dim = grads.shape[-1] // 2
    moved = grads * sine_table[:, None, :]
    return grads * cosine[:, None, :] + jnp.concatenate(
        [moved[..., half_dim:], -moved[..., :half_dim]], axis=-1
    )


def product(left, right):
    return jnp.dot(left, right, preferred_element_type=jnp.float32)


def product_bt(left, right):
    return lax.dot_general(
        left, right, (((1,), (1,)), ((), ())), preferred_element_type=jnp.float32
    )


def product_at(left, right):
    return lax.dot_general(
        left, right, (((0,), (0,)), ((), ())), preferred_element_type=jnp.float32
    )


def norm_scale(values):
    return lax.rsqrt(jnp.mean(values * values, axis=1, keepdims=True) + EPSILON)


def norm_back(grad_normed, values, inverse, gain):
    scaled = values * inverse
    pushed = grad_normed * gain
    back_rows = inverse * (pushed - scaled * jnp.mean(pushed * scaled, axis=1, keepdims=True))
    return (back_rows, jnp.sum(grad_normed * scaled, axis=0))


def silu_grad(values):
    sigma = jax.nn.sigmoid(values)
    return sigma * (1.0 + values * (1.0 - sigma))


def general(
    tokens,
    cotangent,
    lengths,
    routes,
    w_query,
    w_key,
    w_value,
    w_out,
    b_query,
    b_key,
    b_value,
    gain_attention,
    gain_experts,
    w_router,
    w_shared_gate,
    shared_gate,
    shared_up,
    shared_down,
    expert_gate,
    expert_up,
    expert_down,
):
    exp_count = lax.axis_size("exp")
    exp_index = lax.axis_index("exp")
    tp_count = lax.axis_size("tp")
    tp_index = lax.axis_index("tp")
    row_count, model_width = tokens.shape
    local_experts = expert_gate.shape[0]
    expert_count = local_experts * exp_count
    top_count = routes.shape[1]
    capacity = 2 * row_count * top_count // expert_count
    quarter = capacity // tp_count
    head_dim = HEAD_DIM
    heads_here = w_query.shape[1] // head_dim
    group_size = SLOT // row_count
    scale = 1.0 / head_dim**0.5

    def own_slots(whole_rows):
        return lax.dynamic_slice_in_dim(whole_rows, tp_index * quarter, quarter, 2)

    def place_slots(part_rows):
        empty_rows = jnp.zeros((exp_count, local_experts, capacity, model_width), part_rows.dtype)
        return lax.dynamic_update_slice_in_dim(empty_rows, part_rows, tp_index * quarter, 2)

    gathered = (
        lax.all_gather(w_query, "exp", axis=0, tiled=True),
        lax.all_gather(w_key, "exp", axis=0, tiled=True),
        lax.all_gather(w_value, "exp", axis=0, tiled=True),
        lax.all_gather(w_out, "exp", axis=1, tiled=True),
        lax.all_gather(b_query, "exp", axis=0, tiled=True),
        lax.all_gather(b_key, "exp", axis=0, tiled=True),
        lax.all_gather(b_value, "exp", axis=0, tiled=True),
        lax.all_gather(gain_attention, "exp", axis=0, tiled=True),
        lax.all_gather(gain_experts, "exp", axis=0, tiled=True),
        lax.all_gather(w_router, "exp", axis=0, tiled=True),
        lax.all_gather(w_shared_gate, "exp", axis=0, tiled=True),
        lax.all_gather(shared_gate, "exp", axis=0, tiled=True),
        lax.all_gather(shared_up, "exp", axis=0, tiled=True),
        lax.all_gather(shared_down, "exp", axis=1, tiled=True),
    )
    (
        query_full,
        key_full,
        value_full,
        out_full,
        query_bias,
        key_bias,
        value_bias,
        attn_gain,
        ffn_gain,
        router_full,
        share_vector,
        share_gate_full,
        share_up_full,
        share_down_full,
    ) = gathered
    attn_gain = attn_gain.astype(jnp.float32)
    ffn_gain = ffn_gain.astype(jnp.float32)
    first_row = exp_index * row_count
    slot_index = first_row // SLOT
    offset = first_row % SLOT
    positions = offset + jnp.arange(row_count, dtype=jnp.int32)
    length = jnp.sum(
        jnp.where(jnp.arange(lengths.shape[0], dtype=jnp.int32) == slot_index, lengths, 0)
    )
    valid_rows = (positions < length).astype(jnp.float32)
    cosine, sine_table = rope_tables(positions, head_dim)
    input_rows = tokens.astype(jnp.float32)
    inverse_first = norm_scale(input_rows)
    normed_first = (input_rows * inverse_first * attn_gain).astype(jnp.bfloat16)
    query_lin = product(normed_first, query_full) + query_bias.astype(jnp.float32)
    key_lin = product(normed_first, key_full) + key_bias.astype(jnp.float32)
    value_lin = product(normed_first, value_full) + value_bias.astype(jnp.float32)
    query_rot = rotate(
        query_lin.reshape(row_count, heads_here, head_dim), cosine, sine_table
    ).astype(jnp.bfloat16)
    key_rot = rotate(key_lin.reshape(row_count, heads_here, head_dim), cosine, sine_table).astype(
        jnp.bfloat16
    )
    value_low = value_lin.reshape(row_count, heads_here, head_dim).astype(jnp.bfloat16)
    key_list = [key_rot]
    value_list = [value_low]
    for distance in range(1, group_size):
        earlier_keys, earlier_values = shifted((key_rot, value_low), "exp", distance)
        key_list.append(earlier_keys)
        value_list.append(earlier_values)
    all_keys = jnp.concatenate(key_list, axis=0)
    all_values = jnp.concatenate(value_list, axis=0)
    key_index = jnp.arange(group_size * row_count, dtype=jnp.int32)
    key_pos = offset - key_index // row_count * row_count + key_index % row_count
    allowed = (
        (key_pos[None, :] >= 0)
        & (key_pos[None, :] <= positions[:, None])
        & (key_pos[None, :] < length)
    )
    scores = (
        jnp.einsum("qhd,khd->hqk", query_rot, all_keys, preferred_element_type=jnp.float32) * scale
    )
    scores = jnp.where(allowed[None, :, :], scores, MASKED)
    peak_score = jnp.max(scores, axis=2, keepdims=True)
    weights = jnp.exp(scores - peak_score)
    total_weight = jnp.sum(weights, axis=2, keepdims=True)
    log_total = peak_score + jnp.log(total_weight)
    attn_probs = (weights / total_weight).astype(jnp.bfloat16)
    attended = jnp.einsum(
        "hqk,khd->qhd", attn_probs, all_values, preferred_element_type=jnp.float32
    )
    attended = attended.reshape(row_count, heads_here * head_dim).astype(jnp.bfloat16)
    attn_sum = lax.psum(product(attended, out_full).astype(jnp.bfloat16), "tp").astype(jnp.float32)
    hidden_state = input_rows + attn_sum
    inverse_second = norm_scale(hidden_state)
    normed = (hidden_state * inverse_second * ffn_gain).astype(jnp.bfloat16)
    logits = product(normed, router_full)
    router_probs = jax.nn.softmax(logits, axis=1)
    chosen = (
        routes[:, :, None] == jnp.arange(expert_count, dtype=jnp.int32)[None, None, :]
    ).astype(jnp.float32)
    gates = jnp.sum(chosen * router_probs[:, None, :], axis=2)
    share_weight = jax.nn.sigmoid(product(normed, share_vector))
    share_pre = product(normed, share_gate_full)
    share_lin = product(normed, share_up_full)
    share_hidden = (jax.nn.silu(share_pre) * share_lin).astype(jnp.bfloat16)
    share_out = product(share_hidden, share_down_full)
    flat_routes = routes.reshape(-1)
    pair_count = row_count * top_count
    pick_table = (
        flat_routes[:, None] == jnp.arange(expert_count, dtype=jnp.int32)[None, :]
    ).astype(jnp.int32)
    rank_in_expert = jnp.sum((jnp.cumsum(pick_table, axis=0) - 1) * pick_table, axis=1)
    target = flat_routes * capacity + rank_in_expert
    slot_pair = (
        jnp.full((expert_count * capacity,), pair_count, jnp.int32)
        .at[target]
        .set(jnp.arange(pair_count, dtype=jnp.int32))
    )
    slot_token = jnp.where(slot_pair < pair_count, slot_pair // top_count, row_count)
    padded_rows = jnp.concatenate([normed, jnp.zeros((1, model_width), jnp.bfloat16)], axis=0)
    outgoing = padded_rows[slot_token].reshape(exp_count, local_experts, capacity, model_width)
    sending = own_slots(outgoing)
    working = lax.all_gather(
        lax.all_to_all(sending, "exp", split_axis=0, concat_axis=0, tiled=True),
        "tp",
        axis=2,
        tiled=True,
    )
    gate_pre = jnp.einsum(
        "sxcd,xdf->sxcf", working, expert_gate, preferred_element_type=jnp.float32
    )
    up_pre = jnp.einsum("sxcd,xdf->sxcf", working, expert_up, preferred_element_type=jnp.float32)
    inner = (jax.nn.silu(gate_pre) * up_pre).astype(jnp.bfloat16)
    result_rows = jnp.einsum(
        "sxcf,xfd->sxcd", inner, expert_down, preferred_element_type=jnp.float32
    )
    result_rows = lax.psum_scatter(
        result_rows.astype(jnp.bfloat16), "tp", scatter_dimension=2, tiled=True
    ).astype(jnp.float32)
    back_rows = lax.all_to_all(
        result_rows.astype(jnp.bfloat16), "exp", split_axis=0, concat_axis=0, tiled=True
    ).astype(result_rows.dtype)
    returned = back_rows
    returned = place_slots(returned)
    expert_rows = returned.reshape(expert_count * capacity, model_width)[target].reshape(
        row_count, top_count, model_width
    )
    mixture = jnp.einsum("tk,tkd->td", gates, expert_rows) + share_weight[:, None] * share_out
    mixture = lax.psum(mixture.astype(jnp.bfloat16), "tp").astype(jnp.float32)
    output = valid_rows[:, None] * (hidden_state + mixture)
    grad_out = cotangent.astype(jnp.float32) * valid_rows[:, None]
    share_grad = (grad_out * share_weight[:, None]).astype(jnp.bfloat16)
    grad_share_hidden = (
        product_bt(share_grad, share_down_full).astype(jnp.bfloat16).astype(jnp.float32)
    )
    grad_share_pre = (grad_share_hidden * share_lin * silu_grad(share_pre)).astype(jnp.bfloat16)
    grad_share_lin = (grad_share_hidden * jax.nn.silu(share_pre)).astype(jnp.bfloat16)
    d_shared_down = product_at(share_hidden, share_grad)
    d_shared_gate = product_at(normed, grad_share_pre)
    d_shared_up = product_at(normed, grad_share_lin)
    back_normed = product_bt(grad_share_pre, share_gate_full) + product_bt(
        grad_share_lin, share_up_full
    )
    gate_part = jnp.einsum("td,tkd->tk", grad_out, expert_rows)
    share_part = jnp.sum(grad_out * share_out, axis=1)
    pair_grads = (
        (grad_out[:, None, :] * gates[:, :, None])
        .astype(jnp.bfloat16)
        .reshape(pair_count, model_width)
    )
    padded_grads = jnp.concatenate([pair_grads, jnp.zeros((1, model_width), jnp.bfloat16)], axis=0)
    outgoing_grads = padded_grads[slot_pair].reshape(
        exp_count, local_experts, capacity, model_width
    )
    sending_grads = own_slots(outgoing_grads)
    arrived_grads, arrived_rows = (
        lax.all_to_all(sending_grads, "exp", split_axis=0, concat_axis=0, tiled=True),
        lax.all_to_all(sending, "exp", split_axis=0, concat_axis=0, tiled=True),
    )
    arrived_grads, arrived_rows = (
        lax.all_gather(arrived_grads, "tp", axis=2, tiled=True),
        lax.all_gather(arrived_rows, "tp", axis=2, tiled=True),
    )
    gate_pre = jnp.einsum(
        "sxcd,xdf->sxcf", arrived_rows, expert_gate, preferred_element_type=jnp.float32
    )
    up_pre = jnp.einsum(
        "sxcd,xdf->sxcf", arrived_rows, expert_up, preferred_element_type=jnp.float32
    )
    inner = (jax.nn.silu(gate_pre) * up_pre).astype(jnp.bfloat16)
    grad_inner = jnp.einsum(
        "sxcd,xfd->sxcf", arrived_grads, expert_down, preferred_element_type=jnp.float32
    )
    grad_inner = grad_inner.astype(jnp.bfloat16).astype(jnp.float32)
    grad_gate_pre = (grad_inner * up_pre * silu_grad(gate_pre)).astype(jnp.bfloat16)
    grad_up_pre = (grad_inner * jax.nn.silu(gate_pre)).astype(jnp.bfloat16)
    rows_back = jnp.einsum(
        "sxcf,xdf->sxcd", grad_gate_pre, expert_gate, preferred_element_type=jnp.float32
    )
    rows_back = rows_back + jnp.einsum(
        "sxcf,xdf->sxcd", grad_up_pre, expert_up, preferred_element_type=jnp.float32
    )
    rows_back = lax.psum_scatter(
        rows_back.astype(jnp.bfloat16), "tp", scatter_dimension=2, tiled=True
    ).astype(jnp.float32)
    returned_grads = lax.all_to_all(
        rows_back.astype(jnp.bfloat16), "exp", split_axis=0, concat_axis=0, tiled=True
    ).astype(rows_back.dtype)
    returned_grads = place_slots(returned_grads)
    d_expert_gate = jnp.einsum(
        "sxcd,sxcf->xdf", arrived_rows, grad_gate_pre, preferred_element_type=jnp.float32
    )
    d_expert_up = jnp.einsum(
        "sxcd,sxcf->xdf", arrived_rows, grad_up_pre, preferred_element_type=jnp.float32
    )
    d_expert_down = jnp.einsum(
        "sxcf,sxcd->xfd", inner, arrived_grads, preferred_element_type=jnp.float32
    )
    grad_rows = returned_grads.reshape(expert_count * capacity, model_width)[target].reshape(
        row_count, top_count, model_width
    )
    back_normed = back_normed + jnp.sum(grad_rows, axis=1)
    scalar_part = jnp.concatenate([gate_part, share_part[:, None]], axis=1)
    summed_normed, scalar_sum = (
        lax.psum(back_normed.astype(jnp.bfloat16), "tp").astype(jnp.float32),
        lax.psum(scalar_part.astype(jnp.bfloat16), "tp").astype(jnp.float32),
    )
    grad_gates = scalar_sum[:, :top_count]
    grad_share_weight = scalar_sum[:, top_count]
    grad_router_probs = jnp.einsum("tk,tke->te", grad_gates, chosen)
    grad_logits = (
        router_probs
        * (grad_router_probs - jnp.sum(grad_router_probs * router_probs, axis=1, keepdims=True))
    ).astype(jnp.bfloat16)
    grad_share_logit = (grad_share_weight * share_weight * (1.0 - share_weight)).astype(
        jnp.bfloat16
    )
    d_router = product_at(normed, grad_logits)
    d_share_vector = product(grad_share_logit, normed)
    grad_normed = (
        summed_normed
        + product_bt(grad_logits, router_full)
        + grad_share_logit.astype(jnp.float32)[:, None] * share_vector.astype(jnp.float32)[None, :]
    )
    norm_rows, d_gain_experts = norm_back(grad_normed, hidden_state, inverse_second, ffn_gain)
    grad_hidden = grad_out + norm_rows
    grad_hidden_low = grad_hidden.astype(jnp.bfloat16)
    d_out_weight = product_at(attended, grad_hidden_low)
    grad_attended = (
        product_bt(grad_hidden_low, out_full)
        .astype(jnp.bfloat16)
        .reshape(row_count, heads_here, head_dim)
    )
    scores = (
        jnp.einsum("qhd,khd->hqk", query_rot, all_keys, preferred_element_type=jnp.float32) * scale
    )
    scores = jnp.where(allowed[None, :, :], scores, MASKED)
    probs_again = jnp.exp(scores - log_total)
    probs_low = probs_again.astype(jnp.bfloat16)
    grad_values = jnp.einsum(
        "hqk,qhd->khd", probs_low, grad_attended, preferred_element_type=jnp.float32
    )
    grad_probs = jnp.einsum(
        "qhd,khd->hqk", grad_attended, all_values, preferred_element_type=jnp.float32
    )
    grad_scores = (
        probs_again * (grad_probs - jnp.sum(probs_again * grad_probs, axis=2, keepdims=True))
    ).astype(jnp.bfloat16)
    grad_query = (
        jnp.einsum("hqk,khd->qhd", grad_scores, all_keys, preferred_element_type=jnp.float32)
        * scale
    )
    grad_keys = (
        jnp.einsum("hqk,qhd->khd", grad_scores, query_rot, preferred_element_type=jnp.float32)
        * scale
    )
    own_key_grads = grad_keys[:row_count]
    own_value_grads = grad_values[:row_count]
    for distance in range(1, group_size):
        lower_row = distance * row_count
        later_keys, later_values = (
            shifted(
                grad_keys[lower_row : lower_row + row_count].astype(jnp.bfloat16), "exp", -distance
            ).astype(jnp.float32),
            shifted(
                grad_values[lower_row : lower_row + row_count].astype(jnp.bfloat16),
                "exp",
                -distance,
            ).astype(jnp.float32),
        )
        own_key_grads = own_key_grads + later_keys
        own_value_grads = own_value_grads + later_values
    grad_query_lin = (
        rotate_back(grad_query, cosine, sine_table)
        .reshape(row_count, heads_here * head_dim)
        .astype(jnp.bfloat16)
    )
    grad_key_lin = (
        rotate_back(own_key_grads, cosine, sine_table)
        .reshape(row_count, heads_here * head_dim)
        .astype(jnp.bfloat16)
    )
    grad_value_lin = own_value_grads.reshape(row_count, heads_here * head_dim).astype(jnp.bfloat16)
    d_query = product_at(normed_first, grad_query_lin)
    d_key = product_at(normed_first, grad_key_lin)
    d_value = product_at(normed_first, grad_value_lin)
    d_query_bias = jnp.sum(grad_query_lin.astype(jnp.float32), axis=0)
    d_key_bias = jnp.sum(grad_key_lin.astype(jnp.float32), axis=0)
    d_value_bias = jnp.sum(grad_value_lin.astype(jnp.float32), axis=0)
    back_first = (
        product_bt(grad_query_lin, query_full)
        + product_bt(grad_key_lin, key_full)
        + product_bt(grad_value_lin, value_full)
    )
    back_first = lax.psum(back_first.astype(jnp.bfloat16), "tp").astype(jnp.float32)
    first_rows, d_gain_attention = norm_back(back_first, input_rows, inverse_first, attn_gain)
    grad_input = grad_hidden + first_rows
    reduced = (
        lax.psum_scatter(
            d_query.astype(jnp.bfloat16), "exp", scatter_dimension=0, tiled=True
        ).astype(jnp.float32),
        lax.psum_scatter(d_key.astype(jnp.bfloat16), "exp", scatter_dimension=0, tiled=True).astype(
            jnp.float32
        ),
        lax.psum_scatter(
            d_value.astype(jnp.bfloat16), "exp", scatter_dimension=0, tiled=True
        ).astype(jnp.float32),
        lax.psum_scatter(
            d_out_weight.astype(jnp.bfloat16), "exp", scatter_dimension=1, tiled=True
        ).astype(jnp.float32),
        lax.psum_scatter(
            d_query_bias.astype(jnp.bfloat16), "exp", scatter_dimension=0, tiled=True
        ).astype(jnp.float32),
        lax.psum_scatter(
            d_key_bias.astype(jnp.bfloat16), "exp", scatter_dimension=0, tiled=True
        ).astype(jnp.float32),
        lax.psum_scatter(
            d_value_bias.astype(jnp.bfloat16), "exp", scatter_dimension=0, tiled=True
        ).astype(jnp.float32),
        lax.psum_scatter(
            d_gain_attention.astype(jnp.bfloat16), "exp", scatter_dimension=0, tiled=True
        ).astype(jnp.float32),
        lax.psum_scatter(
            d_gain_experts.astype(jnp.bfloat16), "exp", scatter_dimension=0, tiled=True
        ).astype(jnp.float32),
        lax.psum_scatter(
            d_router.astype(jnp.bfloat16), "exp", scatter_dimension=0, tiled=True
        ).astype(jnp.float32),
        lax.psum_scatter(
            d_share_vector.astype(jnp.bfloat16), "exp", scatter_dimension=0, tiled=True
        ).astype(jnp.float32),
        lax.psum_scatter(
            d_shared_gate.astype(jnp.bfloat16), "exp", scatter_dimension=0, tiled=True
        ).astype(jnp.float32),
        lax.psum_scatter(
            d_shared_up.astype(jnp.bfloat16), "exp", scatter_dimension=0, tiled=True
        ).astype(jnp.float32),
        lax.psum_scatter(
            d_shared_down.astype(jnp.bfloat16), "exp", scatter_dimension=1, tiled=True
        ).astype(jnp.float32),
    )
    square_sums = lax.psum((jnp.sum(output * output), jnp.sum(grad_input * grad_input)), "exp")
    count_cells = jnp.sum(lengths).astype(jnp.float32) * model_width
    rms_output = jnp.sqrt(square_sums[0] / count_cells)
    rms_grad = jnp.sqrt(square_sums[1] / count_cells)
    return (
        output.astype(jnp.bfloat16),
        grad_input.astype(jnp.bfloat16),
        reduced[0],
        reduced[1],
        reduced[2],
        reduced[3],
        reduced[4],
        reduced[5],
        reduced[6],
        reduced[7],
        reduced[8],
        reduced[9],
        reduced[10],
        reduced[11],
        reduced[12],
        reduced[13],
        d_expert_gate,
        d_expert_up,
        d_expert_down,
        rms_output,
        rms_grad,
    )


def flat(pieces):
    return jnp.concatenate([p.reshape(-1) for p in pieces])


def key_window(info_ref, block, keys):
    return lax.rem(block + info_ref[0], 2), pl.ds(pl.multiple_of(block // 2 * keys, keys), keys)


def attend_back_kernel(
    info_ref, q_ref, kv_ref, do_ref, o_ref, lse_ref, dq_ref, dk_ref, dv_ref, *, tile, keys, rows
):
    step = pl.program_id(0)
    per_block = rows // tile
    base = (2 * (step // per_block) + info_ref[0]) * rows + (step % per_block) * tile

    @pl.when(step == 0)
    def _():
        dk_ref[...] = jnp.zeros_like(dk_ref)
        dv_ref[...] = jnp.zeros_like(dv_ref)

    query = q_ref[...]
    grad = do_ref[...]
    log_total = lse_ref[:, 0:1]
    delta = jnp.sum(grad.astype(jnp.float32) * o_ref[...], axis=1, keepdims=True)
    row_pos = base + lax.broadcasted_iota(jnp.int32, (tile, 1), 0)
    limit = jnp.minimum(row_pos, info_ref[1] - 1)
    column = lax.broadcasted_iota(jnp.int32, (tile, keys), 1)

    def body(j, acc):
        side, window = key_window(info_ref, j, keys)
        key = kv_ref[side, window, :HEAD_DIM]
        scores = product_bt(query, key) * (1.0 / HEAD_DIM**0.5)
        scores = jnp.where(column <= limit - j * keys, scores, MASKED)
        probs = jnp.exp(scores - log_total)
        dv_ref[side, window, :] += product_at(probs.astype(jnp.bfloat16), grad)
        grad_probs = product_bt(grad, kv_ref[side, window, HEAD_DIM:])
        grad_scores = (probs * (grad_probs - delta)).astype(jnp.bfloat16)
        dk_ref[side, window, :] += product_at(grad_scores, query)
        return acc + product(grad_scores, key)

    count = (base + tile + keys - 1) // keys
    dq_ref[...] = lax.fori_loop(0, count, body, jnp.zeros((tile, HEAD_DIM), jnp.float32))


def attend_back(info, query, key_values, grad, out, log_total, rows):
    count = query.shape[0]
    tile = 256
    half = key_values.shape[:2] + (HEAD_DIM,)
    whole = pl.BlockSpec(half, lambda i: (0, 0, 0))
    both = pl.BlockSpec(key_values.shape, lambda i: (0, 0, 0))
    part = pl.BlockSpec((tile, HEAD_DIM), lambda i: (i, 0))
    return pl.pallas_call(
        functools.partial(attend_back_kernel, tile=tile, keys=rows, rows=rows),
        grid=(count // tile,),
        in_specs=[pl.BlockSpec(memory_space=pltpu.SMEM), part, both, part, part, part],
        out_specs=[part, whole, whole],
        out_shape=[
            jax.ShapeDtypeStruct((count, HEAD_DIM), jnp.float32),
            jax.ShapeDtypeStruct(half, jnp.float32),
            jax.ShapeDtypeStruct(half, jnp.float32),
        ],
        compiler_params=pltpu.CompilerParams(vmem_limit_bytes=40 * 2**20),
        cost_estimate=pl.CostEstimate(
            flops=10 * count * count * HEAD_DIM,
            bytes_accessed=12 * 2**20,
            transcendentals=count * count,
        ),
    )(info, query, key_values, grad, out, log_total)


ROW_AXES = ("z", "x")
COLUMN_AXES = ("y", "c")
ALL_AXES = ("z", "x", "y", "c")
CHUNK_AXES = ("c", "y", "x", "z")
SAME_X = ("c", "y", "z")


def front_kernel(own_ref, parts_ref, rows_ref, weights_ref, send, send_z, recv, send_w, recv_w, here):
    z, x, y, c = (lax.axis_index(name) for name in ALL_AXES)
    z_count = lax.axis_size("z")
    chunks = own_ref.shape[0]

    def up(distance):
        return {"z": lax.rem(z + distance, z_count)}

    def remote(src, dst, send_sem, recv_sem, device):
        return pltpu.make_async_remote_copy(
            src_ref=src,
            dst_ref=dst,
            send_sem=send_sem,
            recv_sem=recv_sem,
            device_id=device,
            device_id_type=pl.DeviceIdType.MESH,
        )

    def spread_z(k, d):
        block = rows_ref.at[c, y, z, k]
        return remote(own_ref.at[k], block, send_z.at[d - 1, k], recv.at[1 + d, k], up(d))

    def spread_y(k):
        block = rows_ref.at[c, y, :, k]
        return remote(block, block, send.at[0, k], recv.at[0, k], {"y": 1 - y})

    def spread_c(k):
        block = rows_ref.at[c, :, :, k]
        return remote(block, block, send.at[1, k], recv.at[1, k], {"c": 1 - c})

    def weights_z(d):
        there = lax.rem(z + d, z_count)
        return remote(
            parts_ref.at[there], weights_ref.at[z, x], send_w.at[d], recv_w.at[d], up(d)
        )

    def weights_x():
        block = weights_ref.at[:, x]
        return remote(block, block, send_w.at[0], recv_w.at[0], {"x": 1 - x})

    barrier = pltpu.get_barrier_semaphore()
    for device in ({"x": 1 - x}, {"y": 1 - y}, {"c": 1 - c}, up(1), up(2), up(3)):
        pl.semaphore_signal(
            barrier, inc=1, device_id=device, device_id_type=pl.DeviceIdType.MESH
        )
    keep = pltpu.make_async_copy(own_ref, rows_ref.at[c, y, z], here.at[0])
    keep_w = pltpu.make_async_copy(parts_ref.at[z], weights_ref.at[z, x], here.at[1])
    keep.start()
    keep_w.start()
    pl.semaphore_wait(barrier, 6)
    for k in range(chunks):
        for d in range(1, 4):
            spread_z(k, d).start()
        if k == 0:
            for d in range(1, 4):
                weights_z(d).start()
    keep.wait()
    keep_w.wait()
    for k in range(chunks):
        for d in range(1, 4):
            spread_z(k, d).wait()
        spread_y(k).start()
        if k == 0:
            for d in range(1, 4):
                weights_z(d).wait()
            weights_x().start()
        if k > 0:
            spread_y(k - 1).wait()
            spread_c(k - 1).start()
    spread_y(chunks - 1).wait()
    spread_c(chunks - 1).start()
    for k in range(chunks):
        spread_c(k).wait()
    weights_x().wait()


def front(rows, parts, chunks=4):
    own, model = rows.shape
    zs = lax.axis_size("z")
    shape = (2, 2, zs, chunks, own // chunks, model)
    anywhere = pl.BlockSpec(memory_space=pl.ANY)
    dma = pltpu.SemaphoreType.DMA
    gathered, weights = pl.pallas_call(
        front_kernel,
        in_specs=[anywhere, anywhere],
        out_specs=[anywhere, anywhere],
        out_shape=[
            jax.ShapeDtypeStruct(shape, rows.dtype),
            jax.ShapeDtypeStruct((zs, 2) + parts.shape[1:], parts.dtype),
        ],
        scratch_shapes=[
            dma((2, chunks)),
            dma((3, chunks)),
            dma((5, chunks)),
            dma((4,)),
            dma((4,)),
            dma((2,)),
        ],
        compiler_params=pltpu.CompilerParams(
            collective_id=0, has_side_effects=True, vmem_limit_bytes=16 * 2**20
        ),
    )(rows.reshape(chunks, own // chunks, model), parts)
    return gathered.reshape(4 * zs * own, model), weights


def middle_kernel(
    length_ref,
    rows_ref,
    w_ref,
    row_ref,
    block_ref,
    leaving_ref,
    sh_ref,
    q_ref,
    kv_ref,
    att_ref,
    lse_ref,
    part_ref,
    joined_ref,
    all_ref,
    shared_ref,
    peaks,
    totals,
    send,
    recv,
    once,
    once_in,
    here,
    *,
    rows,
):
    z, x, y, c = (lax.axis_index(name) for name in ALL_AXES)
    z_count = lax.axis_size("z")
    e_count = 2 * z_count
    chunks = leaving_ref.shape[0]
    head = HEAD_DIM
    count, model = rows_ref.shape
    block = model // e_count
    own = rows // 4
    tile = 2 * own
    half = model // 2
    left, right = pl.ds(0, half), pl.ds(half, leaving_ref.shape[2] - half)
    flip = {"x": {"x": 1 - x}, "y": {"y": 1 - y}, "c": {"c": 1 - c}}

    def up(distance):
        return {"z": lax.rem(z + distance, z_count)}

    def copy_to(src, dst, send_sem, recv_sem, device):
        return pltpu.make_async_remote_copy(
            src_ref=src,
            dst_ref=dst,
            send_sem=send_sem,
            recv_sem=recv_sem,
            device_id=device,
            device_id_type=pl.DeviceIdType.MESH,
        )

    def remote(slot, k, src, dst, device):
        return copy_to(src, dst, send.at[slot, k], recv.at[slot, k], device)

    def spread_z(k):
        return [
            remote(4 + d, k, leaving_ref.at[k], all_ref.at[c, y, x, z, k], up(d))
            for d in range(1, 4)
        ]

    def spread_2(k):
        a = all_ref.at[c, y, x, :, k, :, left]
        b = all_ref.at[c, y, x, :, k, :, right]
        return remote(0, k, a, a, flip["x"]), remote(1, k, b, b, flip["y"])

    def spread_3(k):
        a = all_ref.at[c, y, :, :, k, :, left]
        b = all_ref.at[c, :, x, :, k, :, right]
        return remote(2, k, a, a, flip["y"]), remote(3, k, b, b, flip["x"])

    def spread_c(k):
        a = all_ref.at[c, :, :, :, k]
        return (remote(4, k, a, a, flip["c"]),)

    def share(d, other):
        z_to, x_to = lax.rem(z + d, z_count), 1 - x if other else x
        i = d + z_count if other else d
        return copy_to(
            sh_ref.at[2 * z_to + x_to],
            shared_ref.at[2 * z + x],
            once.at[i],
            once_in.at[i],
            {"z": z_to, "x": x_to},
        )

    def key_values():
        return copy_to(kv_ref.at[0], kv_ref.at[1], once.at[0], once_in.at[0], flip["x"])

    def start(copies):
        for copy in copies:
            copy.start()

    def finish(copies):
        for copy in copies:
            copy.wait()

    barrier = pltpu.get_barrier_semaphore()
    partners = [flip["x"], flip["y"], flip["c"], up(1), up(2), up(3)]
    partners += [{"z": lax.rem(z + d, z_count), "x": 1 - x} for d in range(1, 4)]
    for device in partners:
        pl.semaphore_signal(
            barrier, inc=1, device_id=device, device_id_type=pl.DeviceIdType.MESH
        )
    keep = pltpu.make_async_copy(leaving_ref, all_ref.at[c, y, x, z], here.at[0])
    keep_share = pltpu.make_async_copy(
        sh_ref.at[2 * z + x], shared_ref.at[2 * z + x], here.at[1]
    )
    keep.start()
    keep_share.start()
    for i in range(z_count):
        for j in range(2):
            e = 2 * i + j
            joined_ref[e * block : (e + 1) * block] = w_ref[i, j, :block]
    bias = w_ref[z, 0, pl.ds(block, 16)].astype(jnp.float32) + w_ref[
        z, 1, pl.ds(block, 16)
    ].astype(jnp.float32)
    bias = bias[0:1, : 3 * head]
    lane = lax.broadcasted_iota(jnp.int32, (1, head), 1)
    sign = jnp.where(lane < head // 2, -1.0, 1.0)
    pl.semaphore_wait(barrier, 9)
    for k in range(chunks):
        start(spread_z(k))
    shares = [share(d, other) for d in range(4) for other in (False, True) if d or other]

    def project(t, carry):
        lin = product(rows_ref[pl.ds(t * tile, tile), :], joined_ref[:, : 3 * head]) + bias
        for h in range(2):
            s = 2 * t + h
            z_of, y_of, c_of = lax.rem(s, 4), lax.rem(s // 4, 2), s // 8
            place = pl.ds(pl.multiple_of((z_of * 4 + y_of * 2 + c_of) * own, own), own)
            block_cos, block_sin = block_ref[0, pl.ds(s, 1)], block_ref[1, pl.ds(s, 1)]
            cosine = block_cos * row_ref[0] - block_sin * row_ref[1]
            sine = (block_sin * row_ref[0] + block_cos * row_ref[1]) * sign
            part = lin[h * own : (h + 1) * own]
            query, key = part[:, :head], part[:, head : 2 * head]
            query = query * cosine + pltpu.roll(query, head // 2, 1) * sine
            key = key * cosine + pltpu.roll(key, head // 2, 1) * sine
            q_ref[place, :] = query.astype(jnp.bfloat16)
            kv_ref[0, place, :head] = key.astype(jnp.bfloat16)
            kv_ref[0, place, head:] = part[:, 2 * head :].astype(jnp.bfloat16)
        return carry

    lax.fori_loop(0, count // tile, project, 0)
    key_values().start()
    start(shares)
    keep.wait()
    finish(spread_z(0))
    start(spread_2(0))
    column = lax.broadcasted_iota(jnp.int32, (tile, rows), 1)

    def scan(i, side, blocks, carry):
        query = q_ref[pl.ds(pl.multiple_of(i * tile, tile), tile), :]
        base = (2 * (i // 2) + x) * rows + lax.rem(i, 2) * tile
        row_pos = base + lax.broadcasted_iota(jnp.int32, (tile, 1), 0)
        limit = jnp.minimum(row_pos, length_ref[0] - 1)
        parity = x if side == 0 else 1 - x

        def body(m, carry):
            peak, total, acc = carry
            window = pl.ds(pl.multiple_of(m * rows, rows), rows)
            scores = product_bt(query, kv_ref[side, window, :head]) * (1.0 / head**0.5)
            scores = jnp.where(column <= limit - (2 * m + parity) * rows, scores, MASKED)
            new_peak = jnp.maximum(peak, jnp.max(scores, axis=1, keepdims=True))
            weights = jnp.exp(scores - new_peak)
            shrink = jnp.exp(peak - new_peak)
            total = shrink * total + jnp.sum(weights, axis=1, keepdims=True)
            acc = shrink * acc + product(
                weights.astype(jnp.bfloat16), kv_ref[side, window, head:]
            )
            return (new_peak, total, acc)

        return lax.fori_loop(0, blocks, body, carry)

    def first_pass(i, carry):
        peak, total, acc = scan(
            i,
            0,
            i // 2 + 1,
            (
                jnp.full((tile, 1), MASKED, jnp.float32),
                jnp.zeros((tile, 1), jnp.float32),
                jnp.zeros((tile, head), jnp.float32),
            ),
        )
        place = pl.ds(pl.multiple_of(i * tile, tile), tile)
        peaks[place, :] = jnp.broadcast_to(peak, (tile, head))
        totals[place, :] = jnp.broadcast_to(total, (tile, head))
        att_ref[place, :] = acc
        return carry

    lax.fori_loop(0, count // tile, first_pass, 0)
    finish(spread_z(1))
    start(spread_2(1))
    key_values().wait()

    def second_pass(i, carry):
        place = pl.ds(pl.multiple_of(i * tile, tile), tile)
        peak, total, acc = scan(
            i, 1, i // 2 + x, (peaks[place, 0:1], totals[place, 0:1], att_ref[place, :])
        )
        acc = acc / total
        att_ref[place, :] = acc
        lse_ref[place, :] = jnp.broadcast_to(peak + jnp.log(total), (tile, head))
        part = product_bt(acc.astype(jnp.bfloat16), joined_ref[:, 3 * head :]).astype(
            jnp.bfloat16
        )
        for h in range(2):
            z_of, y_of, c_of = i // 2, lax.rem(i, 2), h
            part_ref[c_of * 8 + y_of * 4 + z_of] = part[h * own : (h + 1) * own]
        return carry

    lax.fori_loop(0, count // tile, second_pass, 0)
    finish(spread_2(0))
    start(spread_3(0))
    for k in range(2, chunks):
        finish(spread_z(k))
        start(spread_2(k))
        finish(spread_2(k - 1))
        start(spread_3(k - 1))
        finish(spread_3(k - 2))
        start(spread_c(k - 2))
    finish(spread_2(chunks - 1))
    start(spread_3(chunks - 1))
    for k in (chunks - 2, chunks - 1):
        finish(spread_3(k))
        start(spread_c(k))
    for k in range(chunks):
        finish(spread_c(k))
    finish(shares)
    keep_share.wait()


def middle(length, gathered, weights, row_table, block_table, leaving, shared, rows, chunks=4):
    own, wide = leaving.shape
    count, model = gathered.shape
    zs = lax.axis_size("z")
    head = HEAD_DIM
    piece = own // chunks
    bf16, f32 = jnp.bfloat16, jnp.float32
    anywhere = pl.BlockSpec(memory_space=pl.ANY)
    inside = pl.BlockSpec(memory_space=pltpu.VMEM)
    vm, dma = pltpu.VMEM, pltpu.SemaphoreType.DMA
    shape = jax.ShapeDtypeStruct
    results = pl.pallas_call(
        functools.partial(middle_kernel, rows=rows),
        in_specs=[pl.BlockSpec(memory_space=pltpu.SMEM)] + [inside] * 4 + [anywhere] * 2,
        out_specs=[inside] * 6 + [anywhere] * 2,
        out_shape=[
            shape((count, head), bf16),
            shape((2, count, 2 * head), bf16),
            shape((count, head), f32),
            shape((count, head), f32),
            shape((count // own, own, model), bf16),
            shape((model, 4 * head), bf16),
            shape((2, 2, 2, zs, chunks, piece, wide), bf16),
            shape(shared.shape, bf16),
        ],
        scratch_shapes=[
            vm((count, head), f32),
            vm((count, head), f32),
            dma((8, chunks)),
            dma((8, chunks)),
            dma((8,)),
            dma((8,)),
            dma((2,)),
        ],
        compiler_params=pltpu.CompilerParams(
            collective_id=3, has_side_effects=True, vmem_limit_bytes=56 * 2**20
        ),
        cost_estimate=pl.CostEstimate(
            flops=10 * count * model * head, bytes_accessed=60 * 2**20, transcendentals=count * count
        ),
    )(
        length,
        gathered,
        weights,
        row_table,
        block_table,
        leaving.reshape(chunks, piece, wide),
        shared,
    )
    query, key_values, attended, log_total, partial, joined, spread, shared = results
    return (
        query,
        key_values,
        attended,
        log_total,
        partial.reshape(count, model),
        joined,
        spread.reshape(8 * zs * own, wide),
        shared,
    )


def expert_rows(first, normed, grads, routes, w_ref, d_ref, s_ref, units, experts):
    width = d_ref.shape[0]
    rows = normed.shape[0]
    pre = product_bt(normed, w_ref[...])
    gate_pre = pre[:, :width]
    up_pre = pre[:, width:]
    lane = lax.broadcasted_iota(jnp.int32, (rows, 128), 1)
    router_lane = lane - (128 - experts)
    logits = jnp.where(router_lane >= 0, gate_pre[:, width - 128 :], MASKED)
    expo = jnp.exp(logits - jnp.max(logits, axis=1, keepdims=True))
    probs = expo / jnp.sum(expo, axis=1, keepdims=True)

    def gate_of(expert):
        picked = jnp.sum((routes == expert).astype(jnp.float32), axis=1, keepdims=True)
        return picked * jnp.sum(
            jnp.where(router_lane == expert, probs, 0.0), axis=1, keepdims=True
        )

    share = jax.nn.sigmoid(
        jnp.sum(jnp.where(router_lane == 0, up_pre[:, width - 128 :], 0.0), axis=1, keepdims=True)
    )
    column = lax.broadcasted_iota(jnp.int32, (rows, width), 1)
    scale = jnp.where(column < width - experts, share, 0.0)
    for index in reversed(range(2)):
        scale = jnp.where(column < (index + 1) * units, gate_of(first + index), scale)
    sigma = jax.nn.sigmoid(gate_pre)
    swish = gate_pre * sigma
    hidden = swish * up_pre
    scaled = (hidden * scale).astype(jnp.bfloat16)
    mixture = product(scaled, d_ref[...]).astype(jnp.bfloat16)
    back = product_bt(grads, d_ref[...])
    gate_sums = product((back * hidden).astype(jnp.bfloat16), s_ref[...]).astype(jnp.bfloat16)
    back = back * scale
    grad_gate = (back * up_pre * (sigma * (1.0 + gate_pre * (1.0 - sigma)))).astype(jnp.bfloat16)
    grad_up = (back * swish).astype(jnp.bfloat16)
    pushed = product(grad_gate, w_ref[:width]) + product(grad_up, w_ref[width:])
    return scaled, grad_gate, grad_up, mixture, pushed.astype(jnp.bfloat16), gate_sums


def add_low(*terms):
    total = terms[0].astype(jnp.float32)
    for term in terms[1:]:
        total = total + term.astype(jnp.float32)
    return total.astype(jnp.bfloat16)


def stream_kernel(
    part_ref,
    x_ref,
    gain_ref,
    g_ref,
    eg_ref,
    eu_ref,
    ed_ref,
    sh_ref,
    router_ref,
    s_ref,
    all_ref,
    hs_ref,
    dgu_ref,
    out_ref,
    hidden_ref,
    own_ref,
    lrc_ref,
    lr2_ref,
    lr3_ref,
    lca_ref,
    lcb_ref,
    l2a_ref,
    l2b_ref,
    l3a_ref,
    l3b_ref,
    lza_ref,
    lzb_ref,
    w_ref,
    d_ref,
    n_buf,
    g_buf,
    pa,
    pb,
    ca,
    cb,
    da,
    db,
    ea,
    eb,
    fa,
    fb,
    qa,
    qb,
    sa,
    sb,
    ta,
    tb,
    hs_buf,
    dgu_buf,
    ra,
    rb,
    rc,
    rd,
    re,
    rf,
    send,
    send_z,
    send_r,
    recv,
    here,
    weigh,
    *,
    units,
    experts,
):
    z, x, y, c = (lax.axis_index(name) for name in ALL_AXES)
    z_count = lax.axis_size("z")
    chunks = x_ref.shape[0]
    model = x_ref.shape[2]
    width = d_ref.shape[0]
    cut = pa.shape[-1]
    half = model // 2
    left, right = pl.ds(0, half), pl.ds(half, half)
    first = 2 * (2 * z + x)
    flip = {"x": {"x": 1 - x}, "y": {"y": 1 - y}, "c": {"c": 1 - c}}

    def up(distance):
        return {"z": lax.rem(z + distance, z_count)}

    def remote(slot, k, src, dst, device):
        return pltpu.make_async_remote_copy(
            src_ref=src,
            dst_ref=dst,
            send_sem=send.at[slot, lax.rem(k, 2)],
            recv_sem=recv.at[slot, k],
            device_id=device,
            device_id_type=pl.DeviceIdType.MESH,
        )

    def spread_z(k, d):
        return pltpu.make_async_remote_copy(
            src_ref=own_ref.at[k],
            dst_ref=all_ref.at[c, y, x, z, k],
            send_sem=send_z.at[d - 1, k],
            recv_sem=recv.at[20 + d, k],
            device_id=up(d),
            device_id_type=pl.DeviceIdType.MESH,
        )

    def heads_c(k):
        return pltpu.make_async_remote_copy(
            src_ref=part_ref.at[1 - c, :, :, k],
            dst_ref=lrc_ref.at[k],
            send_sem=send_r.at[k],
            recv_sem=recv.at[24, k],
            device_id=flip["c"],
            device_id_type=pl.DeviceIdType.MESH,
        )

    def heads_y(k):
        return (remote(17, k, rc.at[lax.rem(k, 2), 1 - y], lr2_ref.at[k], flip["y"]),)

    def heads_z(k):
        copies = []
        for d in range(1, 4):
            there = lax.rem(z + d, z_count)
            copies.append(remote(17 + d, k, re.at[lax.rem(k, 2), there], lr3_ref.at[k, d - 1], up(d)))
        return copies

    def load_hc(k):
        return (
            pltpu.make_async_copy(part_ref.at[c, :, :, k], ra, here.at[15]),
            pltpu.make_async_copy(lrc_ref.at[k], rb, here.at[16]),
        )

    def load_hy(k):
        return (pltpu.make_async_copy(lr2_ref.at[k], rd, here.at[17]),)

    def load_hz(k):
        return (pltpu.make_async_copy(lr3_ref.at[k], rf, here.at[18]),)

    def keep(k):
        return pltpu.make_async_copy(own_ref.at[k], all_ref.at[c, y, x, z, k], here.at[19 + lax.rem(k, 2)])

    def spread_2(k):
        a = all_ref.at[c, y, x, :, k, :, left]
        b = all_ref.at[c, y, x, :, k, :, right]
        return remote(0, k, a, a, flip["x"]), remote(1, k, b, b, flip["y"])

    def spread_3(k):
        a = all_ref.at[c, y, :, :, k, :, left]
        b = all_ref.at[c, :, x, :, k, :, right]
        return remote(2, k, a, a, flip["y"]), remote(3, k, b, b, flip["x"])

    def spread_c(k):
        a = all_ref.at[c, :, :, :, k]
        return (remote(4, k, a, a, flip["c"]),)

    def sum_c(k):
        slot = lax.rem(k, 2)
        return (
            remote(5, k, pa.at[slot, 1 - c], lca_ref.at[k], flip["c"]),
            remote(6, k, pb.at[slot, 1 - c], lcb_ref.at[k], flip["c"]),
        )

    def sum_2(k):
        return (
            remote(7, k, qa.at[lax.rem(k, 2), 1 - y], l2a_ref.at[k], flip["y"]),
            remote(8, k, qb.at[lax.rem(k, 2), :, 1 - x], l2b_ref.at[k], flip["x"]),
        )

    def sum_3(k):
        return (
            remote(9, k, sa.at[lax.rem(k, 2), 1 - x], l3a_ref.at[k], flip["x"]),
            remote(10, k, sb.at[lax.rem(k, 2), 1 - y], l3b_ref.at[k], flip["y"]),
        )

    def sum_z(k):
        copies = []
        for d in range(1, 4):
            there = lax.rem(z + d, z_count)
            copies.append(remote(10 + d, k, ta.at[lax.rem(k, 2), there], lza_ref.at[k, d - 1], up(d)))
            copies.append(remote(13 + d, k, tb.at[lax.rem(k, 2), there], lzb_ref.at[k, d - 1], up(d)))
        return copies

    def load_rows(k):
        slot = lax.rem(k, 2)
        return (
            pltpu.make_async_copy(all_ref.at[:, :, :, :, k], n_buf.at[slot], here.at[slot]),
            pltpu.make_async_copy(g_ref.at[:, :, :, :, k], g_buf.at[slot], here.at[13 + slot]),
        )

    def load_c(k):
        return (
            pltpu.make_async_copy(lca_ref.at[k], ca, here.at[2]),
            pltpu.make_async_copy(lcb_ref.at[k], cb, here.at[3]),
        )

    def load_2(k):
        return (
            pltpu.make_async_copy(l2a_ref.at[k], da, here.at[4]),
            pltpu.make_async_copy(l2b_ref.at[k], db, here.at[5]),
        )

    def load_3(k):
        return (
            pltpu.make_async_copy(l3a_ref.at[k], ea, here.at[6]),
            pltpu.make_async_copy(l3b_ref.at[k], eb, here.at[7]),
        )

    def load_z(k):
        return (
            pltpu.make_async_copy(lza_ref.at[k], fa, here.at[8]),
            pltpu.make_async_copy(lzb_ref.at[k], fb, here.at[9]),
        )

    def store_rows(k):
        return (
            pltpu.make_async_copy(hs_buf, hs_ref.at[:, :, :, :, k], here.at[10]),
            pltpu.make_async_copy(dgu_buf, dgu_ref.at[:, :, :, :, k], here.at[11]),
        )

    def start(copies):
        for copy in copies:
            copy.start()

    def finish(copies):
        for copy in copies:
            copy.wait()

    def at(k, body):
        pl.when((k >= 0) & (k < chunks))(lambda: body(k))

    barrier = pltpu.get_barrier_semaphore()
    for device in (flip["x"], flip["y"], flip["c"], up(1), up(2), up(3)):
        pl.semaphore_signal(
            barrier, inc=1, device_id=device, device_id_type=pl.DeviceIdType.MESH
        )
    pl.semaphore_wait(barrier, 6)

    def first_sends(k, carry):
        heads_c(k).start()
        return carry

    lax.fori_loop(0, chunks, first_sends, 0)
    routed, share = eg_ref.shape[0], sh_ref.shape[1] // 3
    low = pl.ds(routed, share)
    high = pl.ds(width + routed, share)

    def weight_copies():
        pairs = [
            (eg_ref, w_ref.at[pl.ds(0, routed)]),
            (eu_ref, w_ref.at[pl.ds(width, routed)]),
            (ed_ref, d_ref.at[pl.ds(0, routed)]),
            (router_ref.at[0], w_ref.at[pl.ds(width - experts, experts)]),
            (router_ref.at[1], w_ref.at[pl.ds(2 * width - experts, experts)]),
        ]
        cells = model // sh_ref.shape[0]
        for e in range(sh_ref.shape[0]):
            columns = pl.ds(e * cells, cells)
            pairs.append((sh_ref.at[e, pl.ds(0, share)], w_ref.at[low, columns]))
            pairs.append((sh_ref.at[e, pl.ds(share, share)], w_ref.at[high, columns]))
            pairs.append((sh_ref.at[e, pl.ds(2 * share, share)], d_ref.at[low, columns]))
        return [
            pltpu.make_async_copy(src, dst, weigh.at[i]) for i, (src, dst) in enumerate(pairs)
        ]

    start(weight_copies())
    d_ref[pl.ds(width - experts, experts), :] = jnp.zeros((experts, model), jnp.bfloat16)

    def arrive_hc(k):
        heads_c(k).wait()
        start(load_hc(k))

    def arrive_hy(k):
        finish(heads_y(k))
        start(load_hy(k))

    def arrive_hz(k):
        finish(heads_z(k))
        start(load_hz(k))

    def close_hc(k):
        finish(load_hc(k))
        slot = lax.rem(k, 2)

        def each(i, carry):
            for j in range(2):
                rc[slot, j, i] = add_low(ra[j, i], rb[j, i])
            return carry

        lax.fori_loop(0, z_count, each, 0)
        start(heads_y(k))

    def close_hy(k):
        finish(load_hy(k))
        slot = lax.rem(k, 2)
        for i in range(4):
            re[slot, i] = add_low(rc[slot, y, i], rd[i])
        start(heads_z(k))

    def close_hz(k):
        finish(load_hz(k))
        total = re[lax.rem(k, 2), z].astype(jnp.float32)
        for d in range(3):
            total = total + rf[d].astype(jnp.float32)
        hidden = x_ref[k].astype(jnp.float32) + total
        inverse = lax.rsqrt(jnp.mean(hidden * hidden, axis=1, keepdims=True) + EPSILON)
        hidden_ref[k] = hidden
        own_ref[k] = (hidden * inverse * gain_ref[...]).astype(jnp.bfloat16)
        keep(k).start()
        for d in range(1, 4):
            spread_z(k, d).start()

    def gather_2(k):
        keep(k).wait()
        for d in range(1, 4):
            spread_z(k, d).wait()
        start(spread_2(k))

    def gather_3(k):
        finish(spread_2(k))
        start(spread_3(k))

    def gather_c(k):
        finish(spread_3(k))
        start(spread_c(k))

    def gathered(k):
        finish(spread_c(k))
        start(load_rows(k))

    def work(k, part):
        slot = lax.rem(k, 2)
        rows = 256
        normed = n_buf[slot, part].reshape(rows, model)
        grads = g_buf[slot, part].reshape(rows, model + 128)
        routes = grads[:, model : model + 128].astype(jnp.int32)
        grads = grads[:, :model]
        scaled, grad_gate, grad_up, mixture, pushed, gate_sums = expert_rows(
            first, normed, grads, routes, w_ref, d_ref, s_ref, units, experts
        )
        shape = (2, 2, z_count, 16)
        hs_buf[part] = scaled.reshape(shape + (width,))
        dgu_buf[part, :, :, :, :, :width] = grad_gate.reshape(shape + (width,))
        dgu_buf[part, :, :, :, :, width:] = grad_up.reshape(shape + (width,))
        pa[slot, part] = mixture[:, :cut].reshape(shape + (cut,))
        rest = model - cut
        pb[slot, part, :, :, :, :, :rest] = mixture[:, cut:].reshape(shape + (rest,))
        pb[slot, part, :, :, :, :, rest : rest + model] = pushed.reshape(shape + (model,))
        pb[slot, part, :, :, :, :, rest + model :] = gate_sums.reshape(shape + (128,))

    def work_first(k):
        finish(load_rows(k))
        at(k - 1, lambda j: finish(store_rows(j)))
        work(k, 0)

    def work_second(k):
        work(k, 1)
        start(store_rows(k))

    def arrive_c(k):
        finish(sum_c(k))
        start(load_c(k))

    def arrive_2(k):
        finish(sum_2(k))
        start(load_2(k))

    def arrive_3(k):
        finish(sum_3(k))
        start(load_3(k))

    def arrive_z(k):
        finish(sum_z(k))
        start(load_z(k))

    def close_z(k):
        finish(load_z(k))
        slot = lax.rem(k, 2)
        own_a = ta[slot, z].astype(jnp.float32)
        own_b = tb[slot, z].astype(jnp.float32)
        for d in range(3):
            own_a = own_a + fa[d].astype(jnp.float32)
            own_b = own_b + fb[d].astype(jnp.float32)
        out_ref[k, :, :cut] = own_a
        out_ref[k, :, cut:] = own_b

    def close_3(k):
        finish(load_3(k))
        slot = lax.rem(k, 2)

        def each(i, carry):
            ta[slot, i] = add_low(sa[slot, x, i], ea[i])
            tb[slot, i] = add_low(sb[slot, y, i], eb[i])
            return carry

        lax.fori_loop(0, z_count, each, 0)
        start(sum_z(k))

    def close_2(k):
        finish(load_2(k))
        slot = lax.rem(k, 2)

        def each(i, carry):
            for j in range(2):
                sa[slot, j, i] = add_low(qa[slot, y, j, i], da[j, i])
                sb[slot, j, i] = add_low(qb[slot, j, x, i], db[j, i])
            return carry

        lax.fori_loop(0, z_count, each, 0)
        start(sum_3(k))

    def close_c(k):
        finish(load_c(k))
        slot = lax.rem(k, 2)

        def each(i, carry):
            for j in range(2):
                for m in range(2):
                    qa[slot, j, m, i] = add_low(pa[slot, c, j, m, i], ca[j, m, i])
                    qb[slot, j, m, i] = add_low(pb[slot, c, j, m, i], cb[j, m, i])
            return carry

        lax.fori_loop(0, z_count, each, 0)
        start(sum_2(k))

    def tick(i, carry):
        at(i - 11, gathered)
        at(i - 10, gather_c)
        at(i - 8, gather_3)
        at(i - 6, gather_2)
        pl.when(i == 12)(lambda: finish(weight_copies()))
        at(i - 12, work_first)
        at(i - 19, arrive_z)
        at(i - 17, arrive_3)
        at(i - 15, arrive_2)
        at(i - 13, arrive_c)
        at(i - 4, arrive_hz)
        at(i - 2, arrive_hy)
        at(i, arrive_hc)
        at(i - 12, work_second)
        at(i - 4, close_hz)
        at(i - 2, close_hy)
        at(i, close_hc)
        at(i - 19, close_z)
        at(i - 17, close_3)
        at(i - 15, close_2)
        at(i - 13, close_c)
        at(i - 12, lambda k: start(sum_c(k)))
        return carry

    lax.fori_loop(0, chunks + 19, tick, 0)
    finish(store_rows(chunks - 1))


def stream(
    partial, tokens, gain, grads, gates, ups, downs, shared, router, segments, units, experts, chunks
):
    own, model = tokens.shape
    width = segments.shape[0]
    piece = own // chunks
    zs = lax.axis_size("z")
    lead = (2, 2, 2, zs)
    partial = partial.reshape((2, 2, zs, chunks, piece, model))
    grads = grads.reshape(lead + (chunks, piece, model + 128))
    tokens = tokens.reshape(chunks, piece, model)
    cut = model // 2
    extra = 2 * model + 128 - cut
    bf16 = jnp.bfloat16
    shapes = [
        (lead + (chunks, piece, model), bf16),
        (lead + (chunks, piece, width), bf16),
        (lead + (chunks, piece, 2 * width), bf16),
        ((chunks, piece, 2 * model + 128), jnp.float32),
        ((chunks, piece, model), jnp.float32),
        ((chunks, piece, model), bf16),
        ((chunks, 2, zs, piece, model), bf16),
        ((chunks, zs, piece, model), bf16),
        ((chunks, 3, piece, model), bf16),
        ((chunks, 2, 2, zs, piece, cut), bf16),
        ((chunks, 2, 2, zs, piece, extra), bf16),
        ((chunks, 2, zs, piece, cut), bf16),
        ((chunks, 2, zs, piece, extra), bf16),
        ((chunks, zs, piece, cut), bf16),
        ((chunks, zs, piece, extra), bf16),
        ((chunks, 3, piece, cut), bf16),
        ((chunks, 3, piece, extra), bf16),
    ]
    anywhere = pl.BlockSpec(memory_space=pl.ANY)
    inside = pl.BlockSpec(memory_space=pltpu.VMEM)
    vm = pltpu.VMEM
    dma = pltpu.SemaphoreType.DMA
    scratch = [
        vm((2 * width, model), bf16),
        vm((width, model), bf16),
        vm((2,) + lead + (piece, model), bf16),
        vm((2,) + lead + (piece, model + 128), bf16),
        vm((2,) + lead + (piece, cut), bf16),
        vm((2,) + lead + (piece, extra), bf16),
        vm((2, 2, zs, piece, cut), bf16),
        vm((2, 2, zs, piece, extra), bf16),
        vm((2, zs, piece, cut), bf16),
        vm((2, zs, piece, extra), bf16),
        vm((zs, piece, cut), bf16),
        vm((zs, piece, extra), bf16),
        vm((3, piece, cut), bf16),
        vm((3, piece, extra), bf16),
        vm((2, 2, 2, zs, piece, cut), bf16),
        vm((2, 2, 2, zs, piece, extra), bf16),
        vm((2, 2, zs, piece, cut), bf16),
        vm((2, 2, zs, piece, extra), bf16),
        vm((2, zs, piece, cut), bf16),
        vm((2, zs, piece, extra), bf16),
        vm(lead + (piece, width), bf16),
        vm(lead + (piece, 2 * width), bf16),
        vm((2, zs, piece, model), bf16),
        vm((2, zs, piece, model), bf16),
        vm((2, 2, zs, piece, model), bf16),
        vm((zs, piece, model), bf16),
        vm((2, zs, piece, model), bf16),
        vm((3, piece, model), bf16),
        dma((21, 2)),
        dma((3, chunks)),
        dma((chunks,)),
        dma((25, chunks)),
        dma((21,)),
        dma((5 + 3 * shared.shape[0],)),
    ]
    rows = own * 8 * zs
    results = pl.pallas_call(
        functools.partial(stream_kernel, units=units, experts=experts),
        in_specs=[anywhere, inside, inside] + [anywhere] * 6 + [inside],
        out_specs=[anywhere] * 3 + [inside] * 3 + [anywhere] * 11,
        out_shape=[jax.ShapeDtypeStruct(s, t) for s, t in shapes],
        scratch_shapes=scratch,
        compiler_params=pltpu.CompilerParams(
            collective_id=1, has_side_effects=True, vmem_limit_bytes=61 * 2**20
        ),
        cost_estimate=pl.CostEstimate(
            flops=12 * rows * model * width,
            bytes_accessed=rows * (14 * model + 6 * width),
            transcendentals=rows * width,
        ),
    )(partial, tokens, gain, grads, gates, ups, downs, shared, router, segments)
    gathered, scaled, slopes, sums, hidden, normed = results[:6]
    return (
        gathered.reshape(rows, model),
        scaled.reshape(rows, width),
        slopes.reshape(rows, 2 * width),
        sums.reshape(own, 2 * model + 128),
        hidden.reshape(own, model),
        normed.reshape(own, model),
    )


def finish_kernel(
    part_ref,
    grads_ref,
    x_ref,
    wp_ref,
    bp_ref,
    w_ref,
    e_ref,
    rows_ref,
    heads_ref,
    bias_ref,
    gain_ref,
    square_ref,
    extra_ref,
    lc,
    ly,
    lz,
    rc,
    re,
    gt,
    wl,
    bl,
    ws,
    gs,
    gl,
    ss,
    sl,
    ls,
    ll,
    lx,
    lu,
    lv,
    send,
    send_k,
    recv,
    once,
    once_in,
    here,
):
    z, x, y, c = (lax.axis_index(name) for name in ALL_AXES)
    z_count = lax.axis_size("z")
    chunks, _, model = x_ref.shape
    head = HEAD_DIM
    flip = {"x": {"x": 1 - x}, "y": {"y": 1 - y}, "c": {"c": 1 - c}}

    def up(distance):
        return {"z": lax.rem(z + distance, z_count)}

    def copy_to(src, dst, send_sem, recv_sem, device):
        return pltpu.make_async_remote_copy(
            src_ref=src,
            dst_ref=dst,
            send_sem=send_sem,
            recv_sem=recv_sem,
            device_id=device,
            device_id_type=pl.DeviceIdType.MESH,
        )

    def heads_c(k):
        return copy_to(
            part_ref.at[1 - c, :, :, k], lc.at[k], send_k.at[k], recv.at[0, k], flip["c"]
        )

    def heads_y(k):
        return copy_to(rc.at[lax.rem(k, 2), 1 - y], ly.at[k], send.at[0, lax.rem(k, 2)], recv.at[1, k], flip["y"])

    def heads_z(k, d):
        there = lax.rem(z + d, z_count)
        return copy_to(
            re.at[lax.rem(k, 2), there], lz.at[k, d - 1], send.at[d, lax.rem(k, 2)], recv.at[1 + d, k], up(d)
        )

    def keep(k):
        return pltpu.make_async_copy(gt.at[k], rows_ref.at[y, c, k], here.at[lax.rem(k, 2)])

    def rows_y(k):
        return copy_to(gt.at[k], rows_ref.at[y, c, k], send.at[4, lax.rem(k, 2)], recv.at[5, k], flip["y"])

    def rows_c(k):
        block = rows_ref.at[:, c, k]
        return copy_to(block, block, send.at[5, lax.rem(k, 2)], recv.at[6, k], flip["c"])

    def single(i, src, dst, device):
        return copy_to(src, dst, once.at[i], once_in.at[i], device)

    def weights_x():
        return (
            single(0, wp_ref.at[1 - x], wl, flip["x"]),
            single(1, bp_ref.at[1 - x], bl, flip["x"]),
        )

    def weights_z(d):
        return single(1 + d, ws.at[lax.rem(z + d, z_count)], heads_ref.at[z], up(d))

    def at(k, body):
        pl.when((k >= 0) & (k < chunks))(lambda: body(k))

    barrier = pltpu.get_barrier_semaphore()
    for device in (flip["x"], flip["y"], flip["c"], up(1), up(2), up(3)):
        pl.semaphore_signal(
            barrier, inc=1, device_id=device, device_id_type=pl.DeviceIdType.MESH
        )
    square_ref[...] = jnp.zeros_like(square_ref)
    pl.semaphore_wait(barrier, 6)

    def first_sends(k, carry):
        heads_c(k).start()
        return carry

    lax.fori_loop(0, chunks, first_sends, 0)
    for copy in weights_x():
        copy.start()

    def close_c(k):
        heads_c(k).wait()
        slot = lax.rem(k, 2)

        def each(i, carry):
            for j in range(2):
                rc[slot, j, i] = add_low(part_ref[c, j, i, k], lc[k, j, i])
            return carry

        lax.fori_loop(0, z_count, each, 0)
        heads_y(k).start()

    def close_y(k):
        heads_y(k).wait()
        slot = lax.rem(k, 2)
        for i in range(4):
            re[slot, i] = add_low(rc[slot, y, i], ly[k, i])
        for d in range(1, 4):
            heads_z(k, d).start()

    def close_z(k):
        for d in range(1, 4):
            heads_z(k, d).wait()
        pushed = re[lax.rem(k, 2), z].astype(jnp.float32)
        for d in range(3):
            pushed = pushed + lz[k, d].astype(jnp.float32)
        values = x_ref[k].astype(jnp.float32)
        inverse = lax.rsqrt(jnp.mean(values * values, axis=1, keepdims=True) + EPSILON)
        scaled = values * inverse
        total = grads_ref[k] + inverse * (
            pushed - scaled * jnp.mean(pushed * scaled, axis=1, keepdims=True)
        )
        gt[k] = total.astype(jnp.bfloat16)
        squares = total * total
        squares = squares[:8] + squares[8:]
        lanes = squares[:, :128]
        for j in range(1, model // 128):
            lanes = lanes + squares[:, j * 128 : (j + 1) * 128]
        square_ref[...] += lanes
        keep(k).start()
        rows_y(k).start()

    def close_rows(k):
        keep(k).wait()
        rows_y(k).wait()
        rows_c(k).start()

    def close_all(k):
        rows_c(k).wait()

    def weights_sum():
        for copy in weights_x():
            copy.wait()
        bias_ref[...] = bp_ref[x].astype(jnp.float32) + bl[...].astype(jnp.float32)

        def each(i, carry):
            ws[i] = add_low(wp_ref[x, i], wl[i])
            return carry

        lax.fori_loop(0, z_count, each, 0)
        heads_ref[z] = ws[z]
        for d in range(1, 4):
            weights_z(d).start()

    def extra_c():
        return single(13, e_ref, ll.at[0], flip["c"])

    def extra_y():
        return single(14, ls, ll.at[1], flip["y"])

    def extra_x():
        return single(15, lx.at[1 - x], lu, flip["x"])

    def extra_z(d):
        return single(15 + d, lx.at[x, lax.rem(z + d, z_count)], lv.at[d - 1], up(d))

    def extra_sum_c():
        extra_c().wait()
        ls[...] = e_ref[...] + ll[0]
        extra_y().start()

    def extra_sum_y():
        extra_y().wait()
        lx[...] = ls[...] + ll[1]
        extra_x().start()

    def extra_sum_x():
        extra_x().wait()
        lx[x] = lx[x] + lu[...]
        for d in range(1, 4):
            extra_z(d).start()

    extra_c().start()

    def tick(i, carry):
        at(i - 7, close_all)
        at(i - 6, close_rows)
        at(i - 4, close_z)
        at(i - 2, close_y)
        at(i, close_c)
        pl.when(i == 2)(weights_sum)
        pl.when(i == 2)(extra_sum_c)
        pl.when(i == 4)(extra_sum_y)
        pl.when(i == 6)(extra_sum_x)
        return carry

    lax.fori_loop(0, chunks + 7, tick, 0)
    for d in range(1, 4):
        extra_z(d).wait()
    extra_ref[...] = lx[x, z] + lv[0] + lv[1] + lv[2]
    ss[0] = square_ref[...]
    squares_c = single(5, ss.at[0], sl.at[0], flip["c"])
    squares_c.start()
    for d in range(1, 4):
        weights_z(d).wait()
    total = jnp.zeros(gain_ref.shape, jnp.float32)
    for i in range(4):
        for j in range(3):
            columns = slice(j * head, (j + 1) * head)
            total = total + w_ref[i, :, columns].astype(jnp.float32) * heads_ref[
                i, :, columns
            ].astype(jnp.float32)
    gs[0] = total
    gain_y = single(6, gs.at[0], gl.at[0], flip["y"])
    gain_y.start()
    squares_c.wait()
    ss[1] = ss[0] + sl[0]
    squares_y = single(7, ss.at[1], sl.at[1], flip["y"])
    squares_y.start()
    gain_y.wait()
    gs[1] = gs[0] + gl[0]
    gain_c = single(8, gs.at[1], gl.at[1], flip["c"])
    gain_c.start()
    squares_y.wait()
    ss[2] = ss[1] + sl[1]
    squares_x = single(9, ss.at[2], sl.at[2], flip["x"])
    squares_x.start()
    squares_x.wait()
    ss[3] = ss[2] + sl[2]
    squares_z = [single(9 + d, ss.at[3], sl.at[2 + d], up(d)) for d in range(1, 4)]
    for copy in squares_z:
        copy.start()
    gain_c.wait()
    gain_ref[...] = gs[1] + gl[1]
    for copy in squares_z:
        copy.wait()
    square_ref[...] = ss[3] + sl[3] + sl[4] + sl[5]


def finish(partial, grads, tokens, weight_parts, bias_parts, weights, extras, chunks):
    own, model = tokens.shape
    piece = own // chunks
    zs = lax.axis_size("z")
    bf16, f32 = jnp.bfloat16, jnp.float32
    block, wide = weight_parts.shape[2:]
    anywhere = pl.BlockSpec(memory_space=pl.ANY)
    inside = pl.BlockSpec(memory_space=pltpu.VMEM)
    vm = pltpu.VMEM
    dma = pltpu.SemaphoreType.DMA
    rows, heads, bias, gain, square, extra = pl.pallas_call(
        finish_kernel,
        in_specs=[inside] * 7,
        out_specs=[anywhere] + [inside] * 5,
        out_shape=[
            jax.ShapeDtypeStruct((2, 2, chunks, piece, model), bf16),
            jax.ShapeDtypeStruct((zs, block, wide), bf16),
            jax.ShapeDtypeStruct(bias_parts.shape[1:], f32),
            jax.ShapeDtypeStruct((block, 128), f32),
            jax.ShapeDtypeStruct((8, 128), f32),
            jax.ShapeDtypeStruct(extras.shape[2:], f32),
        ],
        scratch_shapes=[
            vm((chunks, 2, zs, piece, model), bf16),
            vm((chunks, zs, piece, model), bf16),
            vm((chunks, 3, piece, model), bf16),
            vm((2, 2, zs, piece, model), bf16),
            vm((2, zs, piece, model), bf16),
            vm((chunks, piece, model), bf16),
            vm((zs, block, wide), bf16),
            vm(bias_parts.shape[1:], bf16),
            vm((zs, block, wide), bf16),
            vm((2, block, 128), f32),
            vm((2, block, 128), f32),
            vm((4, 8, 128), f32),
            vm((6, 8, 128), f32),
            vm(extras.shape, f32),
            vm((2,) + extras.shape, f32),
            vm(extras.shape, f32),
            vm(extras.shape[1:], f32),
            vm((3,) + extras.shape[2:], f32),
            dma((6, 2)),
            dma((chunks,)),
            dma((7, chunks)),
            dma((19,)),
            dma((19,)),
            dma((2,)),
        ],
        compiler_params=pltpu.CompilerParams(
            collective_id=2, has_side_effects=True, vmem_limit_bytes=48 * 2**20
        ),
        cost_estimate=pl.CostEstimate(
            flops=100 * own * model, bytes_accessed=40 * 2**20, transcendentals=0
        ),
    )(
        partial.reshape(2, 2, zs, chunks, piece, model),
        grads.reshape(chunks, piece, model),
        tokens.reshape(chunks, piece, model),
        weight_parts,
        bias_parts,
        weights,
        extras,
    )
    return rows.reshape(4 * own, model), heads, bias, gain, square, extra


def weight_grads_kernel(
    n_ref, g_ref, slopes_ref, scaled_ref, gate_ref, up_ref, down_ref, sh_ref, *, units, share
):
    width = scaled_ref.shape[1]
    low = 2 * units
    first = product_at(n_ref[...], slopes_ref[...]).T
    second = product_at(g_ref[...], scaled_ref[...]).T
    for ref, rows in ((gate_ref, first[:width]), (up_ref, first[width:]), (down_ref, second)):
        for i in range(2):
            ref[i] = rows[i * units : (i + 1) * units]
    for i, rows in enumerate((first[:width], first[width:], second)):
        sh_ref[0, i * share : (i + 1) * share] = rows[low : low + share].astype(jnp.bfloat16)


def weight_grads(normed, grads, slopes, scaled, units, share, blocks):
    count, model = normed.shape
    width = scaled.shape[1]
    block = model // blocks
    one = pl.Buffered(1)
    f32, bf16 = jnp.float32, jnp.bfloat16
    rows = pl.BlockSpec((2, units, block), lambda i: (0, 0, i))
    return pl.pallas_call(
        functools.partial(weight_grads_kernel, units=units, share=share),
        grid=(blocks,),
        in_specs=[
            pl.BlockSpec((count, block), lambda i: (0, i)),
            pl.BlockSpec((count, block), lambda i: (0, i)),
            pl.BlockSpec(slopes.shape, lambda i: (0, 0), pipeline_mode=one),
            pl.BlockSpec(scaled.shape, lambda i: (0, 0), pipeline_mode=one),
        ],
        out_specs=[rows, rows, rows, pl.BlockSpec((1, 3 * share, block), lambda i: (i, 0, 0))],
        out_shape=[jax.ShapeDtypeStruct((2, units, model), f32)] * 3
        + [jax.ShapeDtypeStruct((blocks, 3 * share, block), bf16)],
        compiler_params=pltpu.CompilerParams(vmem_limit_bytes=56 * 2**20),
        cost_estimate=pl.CostEstimate(
            flops=6 * count * model * width,
            bytes_accessed=count * (4 * model + 6 * width) + 12 * model * width,
            transcendentals=0,
        ),
    )(normed, grads, slopes, scaled)


def packed(
    tokens,
    cotangent,
    lengths,
    routes,
    w_query,
    w_key,
    w_value,
    w_out,
    b_query,
    b_key,
    b_value,
    gain_attention,
    gain_experts,
    w_router,
    w_shared_gate,
    shared_gate,
    shared_up,
    shared_down,
    expert_gate,
    expert_up,
    expert_down,
    chunks=8,
):
    f32, bf16 = jnp.float32, jnp.bfloat16
    heads_z = lax.axis_size("z")
    exp_count = heads_z * lax.axis_size("x")
    tp_count = lax.axis_size("y") * lax.axis_size("c")
    z_index, x_index = lax.axis_index("z"), lax.axis_index("x")
    exp_index = z_index * lax.axis_size("x") + x_index
    tp_index = lax.axis_index("y") * lax.axis_size("c") + lax.axis_index("c")
    rows, model = tokens.shape
    total_rows = rows * exp_count
    own = rows // tp_count
    block = model // exp_count
    local_experts, _, units = expert_gate.shape
    experts = local_experts * exp_count
    shared_units = shared_gate.shape[1] // exp_count
    head = HEAD_DIM
    length = lengths[0]

    def my_rows(array):
        return lax.dynamic_slice_in_dim(array, tp_index * own, own, 0)

    own_tokens = my_rows(tokens).astype(f32)
    normed_first = (own_tokens * norm_scale(own_tokens)).astype(bf16)
    gain_rows = gain_attention.astype(f32)
    attn_gain_own = gain_rows[:, None]
    query_part, key_part, value_part = (
        (w.astype(f32) * attn_gain_own).astype(bf16).reshape(block, heads_z, head)
        for w in (w_query, w_key, w_value)
    )
    out_part = w_out.reshape(heads_z, head, block).transpose(2, 0, 1)
    attn_parts = jnp.concatenate([query_part, key_part, value_part, out_part], axis=2)
    half_dim = head // 2
    side = x_index * half_dim
    bias_row = jnp.zeros((3, head), bf16)
    bias_row = lax.dynamic_update_slice(
        bias_row, jnp.stack([b_query, b_key, b_value]), (jnp.zeros_like(side), side)
    )
    small = flat([gain_experts, w_router.T, w_shared_gate])
    small = jnp.pad(small, (0, 15 * 4 * head - small.shape[0])).reshape(15, 4 * head)
    small = jnp.concatenate([jnp.pad(bias_row.reshape(1, 3 * head), ((0, 0), (0, head))), small])
    attn_parts = jnp.concatenate(
        [
            attn_parts.transpose(1, 0, 2),
            jnp.broadcast_to(small[None], (heads_z, 16, 4 * head)),
        ],
        axis=1,
    )
    first_half, arrived_weights = front(normed_first, attn_parts)
    small = arrived_weights[:, :, block + 1 :].reshape(exp_count, 15 * 4 * head)

    own_first = exp_index * rows + tp_index * own
    own_positions = own_first + jnp.arange(own, dtype=jnp.int32)
    valid = (own_positions < length).astype(f32)[:, None]
    grad_out_low = (my_rows(cotangent).astype(f32) * valid).astype(bf16)
    own_routes = my_rows(routes)
    leaving = jnp.concatenate(
        [grad_out_low, jnp.pad(own_routes.astype(bf16), ((0, 0), (0, 124)), constant_values=-1.0)],
        axis=1,
    )
    shared_parts = jnp.concatenate(
        [
            w.reshape(exp_count, shared_units, block)
            for w in (shared_gate.T, shared_up.T, shared_down)
        ],
        axis=1,
    )
    place = 0
    ffn_gain = small[:, place : place + block].reshape(model).astype(f32)
    place += block
    router_rows = (
        small[:, place : place + block * experts]
        .reshape(exp_count, experts, block)
        .transpose(1, 0, 2)
        .reshape(experts, model)
    )
    place += block * experts
    share_vector = small[:, place : place + block].reshape(model)

    frequency = ROPE_BASE ** (-(jnp.arange(half_dim, dtype=f32) * 2.0) / head)
    row_angle = jnp.arange(own, dtype=f32)[:, None] * frequency[None, :]
    places = (
        jnp.arange(2)[:, None, None] * own
        + jnp.arange(2)[None, :, None] * 2 * own
        + (jnp.arange(heads_z)[None, None, :] * 2 + x_index) * rows
    )
    block_angle = places.reshape(-1).astype(f32)[:, None] * frequency[None, :]
    row_cos, row_sin = jnp.cos(row_angle)[None], jnp.sin(row_angle)[None]
    block_cos, block_sin = jnp.cos(block_angle)[:, None], jnp.sin(block_angle)[:, None]
    cosine = (block_cos * row_cos - block_sin * row_sin).reshape(heads_z * rows, half_dim)
    sine = (block_sin * row_cos + block_cos * row_sin).reshape(heads_z * rows, half_dim)

    def rope_back(values):
        one, two = values[:, :half_dim], values[:, half_dim:]
        return jnp.concatenate([one * cosine + two * sine, two * cosine - one * sine], axis=1)

    def by_position(array):
        return (
            array.reshape((2, 2, heads_z, own) + array.shape[1:])
            .transpose(2, 1, 0, 3, 4)
            .reshape(array.shape)
        )

    def by_owner(array):
        return (
            array.reshape((heads_z, 2, 2, own) + array.shape[1:])
            .transpose(2, 1, 0, 3, 4)
            .reshape(array.shape)
        )

    flip = [(0, 1), (1, 0)]
    def twice(cos, sin):
        return jnp.stack([jnp.tile(cos, (1, 2)), jnp.tile(sin, (1, 2))])

    query_rot, key_values, attended, log_total, attn_part, attn_weights, grad_all, shared_parts = (
        middle(
            lengths,
            first_half,
            arrived_weights,
            twice(row_cos[0], row_sin[0]),
            twice(block_cos[:, 0], block_sin[:, 0]),
            leaving,
            shared_parts,
            rows,
        )
    )
    info = jnp.stack([x_index, length]).astype(jnp.int32)
    attended_low = by_owner(attended.astype(bf16))
    out_weight = attn_weights[:, 3 * head :]

    width = local_experts * units + shared_units + experts
    router_pair = jnp.stack(
        [router_rows, jnp.pad(share_vector[None, :], ((0, experts - 1), (0, 0)))]
    )
    unit = jnp.arange(width, dtype=jnp.int32)
    segment = jnp.where(
        unit < local_experts * units, exp_index * local_experts + unit // units, experts
    )
    segments = (
        (segment[:, None] == jnp.arange(128, dtype=jnp.int32)[None, :])
        & (unit < width - experts)[:, None]
    ).astype(bf16)
    normed_all, scaled_all, slope_all, mixed_sum, hidden_state, normed = stream(
        attn_part,
        my_rows(tokens),
        ffn_gain[None, :],
        grad_all,
        expert_gate.transpose(0, 2, 1).reshape(local_experts * units, model),
        expert_up.transpose(0, 2, 1).reshape(local_experts * units, model),
        expert_down.reshape(local_experts * units, model),
        shared_parts,
        router_pair,
        segments,
        units,
        experts,
        chunks,
    )
    inverse_second = norm_scale(hidden_state)
    d_expert_gate, d_expert_up, d_expert_down, d_shared = weight_grads(
        normed_all, grad_all, slope_all, scaled_all, units, shared_units, exp_count
    )

    output = valid * (hidden_state + mixed_sum[:, :model])
    mixed = lax.all_gather(output.astype(bf16), COLUMN_AXES, axis=0, tiled=True)

    router_probs = jax.nn.softmax(product_bt(normed, router_rows), axis=1)
    share_weight = jax.nn.sigmoid(product(normed, share_vector))
    chosen = jnp.sum(
        (own_routes[:, :, None] == jnp.arange(experts, dtype=jnp.int32)[None, None, :]).astype(f32),
        axis=1,
    )
    grad_router_probs = chosen * mixed_sum[:, 2 * model : 2 * model + experts]
    grad_share_weight = mixed_sum[:, 2 * model + experts]
    grad_logits = (
        router_probs
        * (grad_router_probs - jnp.sum(grad_router_probs * router_probs, axis=1, keepdims=True))
    ).astype(bf16)
    grad_share_logit = (grad_share_weight * share_weight * (1.0 - share_weight)).astype(bf16)
    grad_normed = (
        mixed_sum[:, model : 2 * model]
        + product(grad_logits, router_rows)
        + grad_share_logit.astype(f32)[:, None] * share_vector.astype(f32)[None, :]
    )
    norm_rows, d_gain_experts = norm_back(grad_normed, hidden_state, inverse_second, ffn_gain)
    grad_hidden = grad_out_low.astype(f32) + norm_rows
    hidden_half = lax.all_gather(grad_hidden.astype(bf16), SAME_X, axis=0, tiled=True)
    router_grads = product_at(
        jnp.concatenate([grad_logits, grad_share_logit[:, None]], axis=1), normed
    )
    extras = jnp.concatenate(
        [
            router_grads,
            d_gain_experts[None, :],
            jnp.broadcast_to(jnp.sum(output * output), (1, model)),
            jnp.zeros((5, model), f32),
        ]
    )
    extras = extras.reshape(-1, heads_z, 2, block).transpose(2, 1, 0, 3)
    hidden_half, d_shared = lax.optimization_barrier((hidden_half, d_shared))
    arrived = lax.all_to_all(d_shared, ROW_AXES, 0, 0, tiled=True).astype(f32)
    d_shared_gate, d_shared_up, d_shared_down = (
        arrived[:, k * shared_units : (k + 1) * shared_units].reshape(
            exp_count * shared_units, block
        )
        for k in range(3)
    )
    d_shared_gate, d_shared_up = d_shared_gate.T, d_shared_up.T
    grad_attended = product(hidden_half, out_weight).astype(bf16)
    d_out_weight = product_at(hidden_half, attended_low)
    scale = 1.0 / head**0.5
    grad_query, grad_key, grad_value = attend_back(
        info, query_rot, key_values, by_position(grad_attended), attended, log_total, rows
    )
    grad_kv = jnp.concatenate([grad_key, grad_value], axis=2).astype(bf16)
    away = lax.ppermute(grad_kv[1], "x", flip)
    grad_kv = by_owner(
        jnp.concatenate([grad_key[0], grad_value[0]], axis=1) + away.astype(f32)
    )
    grad_qkv = jnp.concatenate(
        [
            rope_back(by_owner(grad_query)) * scale,
            rope_back(grad_kv[:, :head]) * scale,
            grad_kv[:, head:],
        ],
        axis=1,
    ).astype(bf16)
    d_attn = jnp.concatenate([product_at(first_half, grad_qkv), d_out_weight], axis=1).astype(bf16)
    d_biases = jnp.sum(grad_qkv.astype(f32), axis=0).astype(bf16).reshape(3, 2, head // 2)
    d_biases = jnp.pad(
        d_biases.transpose(1, 0, 2).reshape(2, 1, 3 * head // 2),
        ((0, 0), (0, 15), (0, 4 * head - 3 * head // 2)),
    )
    raw = jnp.concatenate(
        [w.reshape(block, heads_z, head) for w in (w_query, w_key, w_value)], axis=2
    ).transpose(1, 0, 2)
    grad_tokens, d_attn, d_bias_row, d_gain_attention, squares, extras = finish(
        product_bt(grad_qkv, attn_weights[:, : 3 * head]).astype(bf16),
        grad_hidden,
        my_rows(tokens),
        d_attn.reshape(heads_z, 2, block, 4 * head).transpose(1, 0, 2, 3),
        d_biases,
        raw,
        extras,
        chunks,
    )
    d_attn = d_attn.astype(f32)
    d_bias_row = d_bias_row[0]
    d_gain_attention = jnp.sum(d_gain_attention, axis=1)
    d_query, d_key, d_value = (
        d_attn[:, :, k * head : (k + 1) * head].transpose(1, 0, 2).reshape(block, heads_z * head)
        * attn_gain_own
        for k in range(3)
    )
    d_out = d_attn[:, :, 3 * head :].transpose(0, 2, 1).reshape(heads_z * head, block)
    half_head = head // 2

    d_router, d_share_vector = extras[:experts].T, extras[experts]
    d_gain_experts = extras[experts + 1]
    cells = length.astype(f32) * model
    rms_output = jnp.sqrt(extras[experts + 2, 0] / cells)
    rms_grad = jnp.sqrt(jnp.sum(squares) / cells)
    return (
        mixed,
        grad_tokens,
        d_query,
        d_key,
        d_value,
        d_out,
        d_bias_row[:half_head],
        d_bias_row[half_head : 2 * half_head],
        d_bias_row[2 * half_head : 3 * half_head],
        d_gain_attention,
        d_gain_experts,
        d_router,
        d_share_vector,
        d_shared_gate,
        d_shared_up,
        d_shared_down,
        d_expert_gate.transpose(0, 2, 1),
        d_expert_up.transpose(0, 2, 1),
        d_expert_down,
        rms_output,
        rms_grad,
    )


def specs(row, column):
    both = column + row
    ins = (
        P(row, None),
        P(row, None),
        P(),
        P(row, None),
        P(row, column),
        P(row, column),
        P(row, column),
        P(column, row),
        P(both),
        P(both),
        P(both),
        P(row),
        P(row),
        P(row, None),
        P(row),
        P(row, column),
        P(row, column),
        P(column, row),
        P(row, None, column),
        P(row, None, column),
        P(row, column, None),
    )
    outs = (
        P(row, None),
        P(row, None),
        P(row, column),
        P(row, column),
        P(row, column),
        P(column, row),
        P(both),
        P(both),
        P(both),
        P(row),
        P(row),
        P(row, None),
        P(row),
        P(row, column),
        P(row, column),
        P(column, row),
        P(row, None, column),
        P(row, None, column),
        P(row, column, None),
        P(),
        P(),
    )
    return ins, outs


def solution(mesh):
    if (mesh.shape["exp"], mesh.shape["tp"]) == (8, 4):
        body, row, column = packed, ROW_AXES, COLUMN_AXES
        mesh = Mesh(mesh.devices.reshape(4, 2, 2, 2), ALL_AXES)
    else:
        body, row, column = general, ("exp",), ("tp",)
    ins, outs = specs(row, column)
    return jax.shard_map(body, mesh=mesh, in_specs=ins, out_specs=outs, check_vma=False)
```

```python
import functools

import jax
import jax.numpy as jnp
import numpy as np
from jax import lax
from jax.experimental import pallas as pl
from jax.experimental.pallas import tpu as pltpu
from jax.sharding import Mesh
from jax.sharding import PartitionSpec as P

HEAD_DIM = 128
SLOT = 4096


EPSILON = 1e-06
ROPE_BASE = 1000000.0
MASKED = -1e30


def shifted(shard, axis, by):
    length = lax.axis_size(axis)
    pairs = [(i, i + by) for i in range(length) if 0 <= i + by < length]
    return lax.ppermute(shard, axis, pairs)


def rope_tables(positions, head_dim):
    half_dim = head_dim // 2
    frequency = ROPE_BASE ** (-(jnp.arange(half_dim, dtype=jnp.float32) * 2.0) / head_dim)
    angles = positions.astype(jnp.float32)[:, None] * frequency[None, :]
    cosine = jnp.concatenate([jnp.cos(angles), jnp.cos(angles)], axis=1)
    sine_table = jnp.concatenate([jnp.sin(angles), jnp.sin(angles)], axis=1)
    return (cosine, sine_table)


def rotate(values, cosine, sine_table):
    half_dim = values.shape[-1] // 2
    turned = jnp.concatenate([-values[..., half_dim:], values[..., :half_dim]], axis=-1)
    return values * cosine[:, None, :] + turned * sine_table[:, None, :]


def rotate_back(grads, cosine, sine_table):
    half_dim = grads.shape[-1] // 2
    moved = grads * sine_table[:, None, :]
    return grads * cosine[:, None, :] + jnp.concatenate(
        [moved[..., half_dim:], -moved[..., :half_dim]], axis=-1
    )


def product(left, right):
    return jnp.dot(left, right, preferred_element_type=jnp.float32)


def product_bt(left, right):
    return lax.dot_general(
        left, right, (((1,), (1,)), ((), ())), preferred_element_type=jnp.float32
    )


def product_at(left, right):
    return lax.dot_general(
        left, right, (((0,), (0,)), ((), ())), preferred_element_type=jnp.float32
    )


def norm_scale(values):
    return lax.rsqrt(jnp.mean(values * values, axis=1, keepdims=True) + EPSILON)


def norm_back(grad_normed, values, inverse, gain):
    scaled = values * inverse
    pushed = grad_normed * gain
    back_rows = inverse * (pushed - scaled * jnp.mean(pushed * scaled, axis=1, keepdims=True))
    return (back_rows, jnp.sum(grad_normed * scaled, axis=0))


def silu_grad(values):
    sigma = jax.nn.sigmoid(values)
    return sigma * (1.0 + values * (1.0 - sigma))


def general(
    tokens,
    cotangent,
    lengths,
    routes,
    w_query,
    w_key,
    w_value,
    w_out,
    b_query,
    b_key,
    b_value,
    gain_attention,
    gain_experts,
    w_router,
    w_shared_gate,
    shared_gate,
    shared_up,
    shared_down,
    expert_gate,
    expert_up,
    expert_down,
):
    exp_count = lax.axis_size("exp")
    exp_index = lax.axis_index("exp")
    tp_count = lax.axis_size("tp")
    tp_index = lax.axis_index("tp")
    row_count, model_width = tokens.shape
    local_experts = expert_gate.shape[0]
    expert_count = local_experts * exp_count
    top_count = routes.shape[1]
    capacity = 2 * row_count * top_count // expert_count
    quarter = capacity // tp_count
    head_dim = HEAD_DIM
    heads_here = w_query.shape[1] // head_dim
    group_size = SLOT // row_count
    scale = 1.0 / head_dim**0.5

    def own_slots(whole_rows):
        return lax.dynamic_slice_in_dim(whole_rows, tp_index * quarter, quarter, 2)

    def place_slots(part_rows):
        empty_rows = jnp.zeros((exp_count, local_experts, capacity, model_width), part_rows.dtype)
        return lax.dynamic_update_slice_in_dim(empty_rows, part_rows, tp_index * quarter, 2)

    gathered = (
        lax.all_gather(w_query, "exp", axis=0, tiled=True),
        lax.all_gather(w_key, "exp", axis=0, tiled=True),
        lax.all_gather(w_value, "exp", axis=0, tiled=True),
        lax.all_gather(w_out, "exp", axis=1, tiled=True),
        lax.all_gather(b_query, "exp", axis=0, tiled=True),
        lax.all_gather(b_key, "exp", axis=0, tiled=True),
        lax.all_gather(b_value, "exp", axis=0, tiled=True),
        lax.all_gather(gain_attention, "exp", axis=0, tiled=True),
        lax.all_gather(gain_experts, "exp", axis=0, tiled=True),
        lax.all_gather(w_router, "exp", axis=0, tiled=True),
        lax.all_gather(w_shared_gate, "exp", axis=0, tiled=True),
        lax.all_gather(shared_gate, "exp", axis=0, tiled=True),
        lax.all_gather(shared_up, "exp", axis=0, tiled=True),
        lax.all_gather(shared_down, "exp", axis=1, tiled=True),
    )
    (
        query_full,
        key_full,
        value_full,
        out_full,
        query_bias,
        key_bias,
        value_bias,
        attn_gain,
        ffn_gain,
        router_full,
        share_vector,
        share_gate_full,
        share_up_full,
        share_down_full,
    ) = gathered
    attn_gain = attn_gain.astype(jnp.float32)
    ffn_gain = ffn_gain.astype(jnp.float32)
    first_row = exp_index * row_count
    slot_index = first_row // SLOT
    offset = first_row % SLOT
    positions = offset + jnp.arange(row_count, dtype=jnp.int32)
    length = jnp.sum(
        jnp.where(jnp.arange(lengths.shape[0], dtype=jnp.int32) == slot_index, lengths, 0)
    )
    valid_rows = (positions < length).astype(jnp.float32)
    cosine, sine_table = rope_tables(positions, head_dim)
    input_rows = tokens.astype(jnp.float32)
    inverse_first = norm_scale(input_rows)
    normed_first = (input_rows * inverse_first * attn_gain).astype(jnp.bfloat16)
    query_lin = product(normed_first, query_full) + query_bias.astype(jnp.float32)
    key_lin = product(normed_first, key_full) + key_bias.astype(jnp.float32)
    value_lin = product(normed_first, value_full) + value_bias.astype(jnp.float32)
    query_rot = rotate(
        query_lin.reshape(row_count, heads_here, head_dim), cosine, sine_table
    ).astype(jnp.bfloat16)
    key_rot = rotate(key_lin.reshape(row_count, heads_here, head_dim), cosine, sine_table).astype(
        jnp.bfloat16
    )
    value_low = value_lin.reshape(row_count, heads_here, head_dim).astype(jnp.bfloat16)
    key_list = [key_rot]
    value_list = [value_low]
    for distance in range(1, group_size):
        earlier_keys, earlier_values = shifted((key_rot, value_low), "exp", distance)
        key_list.append(earlier_keys)
        value_list.append(earlier_values)
    all_keys = jnp.concatenate(key_list, axis=0)
    all_values = jnp.concatenate(value_list, axis=0)
    key_index = jnp.arange(group_size * row_count, dtype=jnp.int32)
    key_pos = offset - key_index // row_count * row_count + key_index % row_count
    allowed = (
        (key_pos[None, :] >= 0)
        & (key_pos[None, :] <= positions[:, None])
        & (key_pos[None, :] < length)
    )
    scores = (
        jnp.einsum("qhd,khd->hqk", query_rot, all_keys, preferred_element_type=jnp.float32) * scale
    )
    scores = jnp.where(allowed[None, :, :], scores, MASKED)
    peak_score = jnp.max(scores, axis=2, keepdims=True)
    weights = jnp.exp(scores - peak_score)
    total_weight = jnp.sum(weights, axis=2, keepdims=True)
    log_total = peak_score + jnp.log(total_weight)
    attn_probs = (weights / total_weight).astype(jnp.bfloat16)
    attended = jnp.einsum(
        "hqk,khd->qhd", attn_probs, all_values, preferred_element_type=jnp.float32
    )
    attended = attended.reshape(row_count, heads_here * head_dim).astype(jnp.bfloat16)
    attn_sum = lax.psum(product(attended, out_full).astype(jnp.bfloat16), "tp").astype(jnp.float32)
    hidden_state = input_rows + attn_sum
    inverse_second = norm_scale(hidden_state)
    normed = (hidden_state * inverse_second * ffn_gain).astype(jnp.bfloat16)
    logits = product(normed, router_full)
    router_probs = jax.nn.softmax(logits, axis=1)
    chosen = (
        routes[:, :, None] == jnp.arange(expert_count, dtype=jnp.int32)[None, None, :]
    ).astype(jnp.float32)
    gates = jnp.sum(chosen * router_probs[:, None, :], axis=2)
    share_weight = jax.nn.sigmoid(product(normed, share_vector))
    share_pre = product(normed, share_gate_full)
    share_lin = product(normed, share_up_full)
    share_hidden = (jax.nn.silu(share_pre) * share_lin).astype(jnp.bfloat16)
    share_out = product(share_hidden, share_down_full)
    flat_routes = routes.reshape(-1)
    pair_count = row_count * top_count
    pick_table = (
        flat_routes[:, None] == jnp.arange(expert_count, dtype=jnp.int32)[None, :]
    ).astype(jnp.int32)
    rank_in_expert = jnp.sum((jnp.cumsum(pick_table, axis=0) - 1) * pick_table, axis=1)
    target = flat_routes * capacity + rank_in_expert
    slot_pair = (
        jnp.full((expert_count * capacity,), pair_count, jnp.int32)
        .at[target]
        .set(jnp.arange(pair_count, dtype=jnp.int32))
    )
    slot_token = jnp.where(slot_pair < pair_count, slot_pair // top_count, row_count)
    padded_rows = jnp.concatenate([normed, jnp.zeros((1, model_width), jnp.bfloat16)], axis=0)
    outgoing = padded_rows[slot_token].reshape(exp_count, local_experts, capacity, model_width)
    sending = own_slots(outgoing)
    working = lax.all_gather(
        lax.all_to_all(sending, "exp", split_axis=0, concat_axis=0, tiled=True),
        "tp",
        axis=2,
        tiled=True,
    )
    gate_pre = jnp.einsum(
        "sxcd,xdf->sxcf", working, expert_gate, preferred_element_type=jnp.float32
    )
    up_pre = jnp.einsum("sxcd,xdf->sxcf", working, expert_up, preferred_element_type=jnp.float32)
    inner = (jax.nn.silu(gate_pre) * up_pre).astype(jnp.bfloat16)
    result_rows = jnp.einsum(
        "sxcf,xfd->sxcd", inner, expert_down, preferred_element_type=jnp.float32
    )
    result_rows = lax.psum_scatter(
        result_rows.astype(jnp.bfloat16), "tp", scatter_dimension=2, tiled=True
    ).astype(jnp.float32)
    back_rows = lax.all_to_all(
        result_rows.astype(jnp.bfloat16), "exp", split_axis=0, concat_axis=0, tiled=True
    ).astype(result_rows.dtype)
    returned = back_rows
    returned = place_slots(returned)
    expert_rows = returned.reshape(expert_count * capacity, model_width)[target].reshape(
        row_count, top_count, model_width
    )
    mixture = jnp.einsum("tk,tkd->td", gates, expert_rows) + share_weight[:, None] * share_out
    mixture = lax.psum(mixture.astype(jnp.bfloat16), "tp").astype(jnp.float32)
    output = valid_rows[:, None] * (hidden_state + mixture)
    grad_out = cotangent.astype(jnp.float32) * valid_rows[:, None]
    share_grad = (grad_out * share_weight[:, None]).astype(jnp.bfloat16)
    grad_share_hidden = (
        product_bt(share_grad, share_down_full).astype(jnp.bfloat16).astype(jnp.float32)
    )
    grad_share_pre = (grad_share_hidden * share_lin * silu_grad(share_pre)).astype(jnp.bfloat16)
    grad_share_lin = (grad_share_hidden * jax.nn.silu(share_pre)).astype(jnp.bfloat16)
    d_shared_down = product_at(share_hidden, share_grad)
    d_shared_gate = product_at(normed, grad_share_pre)
    d_shared_up = product_at(normed, grad_share_lin)
    back_normed = product_bt(grad_share_pre, share_gate_full) + product_bt(
        grad_share_lin, share_up_full
    )
    gate_part = jnp.einsum("td,tkd->tk", grad_out, expert_rows)
    share_part = jnp.sum(grad_out * share_out, axis=1)
    pair_grads = (
        (grad_out[:, None, :] * gates[:, :, None])
        .astype(jnp.bfloat16)
        .reshape(pair_count, model_width)
    )
    padded_grads = jnp.concatenate([pair_grads, jnp.zeros((1, model_width), jnp.bfloat16)], axis=0)
    outgoing_grads = padded_grads[slot_pair].reshape(
        exp_count, local_experts, capacity, model_width
    )
    sending_grads = own_slots(outgoing_grads)
    arrived_grads, arrived_rows = (
        lax.all_to_all(sending_grads, "exp", split_axis=0, concat_axis=0, tiled=True),
        lax.all_to_all(sending, "exp", split_axis=0, concat_axis=0, tiled=True),
    )
    arrived_grads, arrived_rows = (
        lax.all_gather(arrived_grads, "tp", axis=2, tiled=True),
        lax.all_gather(arrived_rows, "tp", axis=2, tiled=True),
    )
    gate_pre = jnp.einsum(
        "sxcd,xdf->sxcf", arrived_rows, expert_gate, preferred_element_type=jnp.float32
    )
    up_pre = jnp.einsum(
        "sxcd,xdf->sxcf", arrived_rows, expert_up, preferred_element_type=jnp.float32
    )
    inner = (jax.nn.silu(gate_pre) * up_pre).astype(jnp.bfloat16)
    grad_inner = jnp.einsum(
        "sxcd,xfd->sxcf", arrived_grads, expert_down, preferred_element_type=jnp.float32
    )
    grad_inner = grad_inner.astype(jnp.bfloat16).astype(jnp.float32)
    grad_gate_pre = (grad_inner * up_pre * silu_grad(gate_pre)).astype(jnp.bfloat16)
    grad_up_pre = (grad_inner * jax.nn.silu(gate_pre)).astype(jnp.bfloat16)
    rows_back = jnp.einsum(
        "sxcf,xdf->sxcd", grad_gate_pre, expert_gate, preferred_element_type=jnp.float32
    )
    rows_back = rows_back + jnp.einsum(
        "sxcf,xdf->sxcd", grad_up_pre, expert_up, preferred_element_type=jnp.float32
    )
    rows_back = lax.psum_scatter(
        rows_back.astype(jnp.bfloat16), "tp", scatter_dimension=2, tiled=True
    ).astype(jnp.float32)
    returned_grads = lax.all_to_all(
        rows_back.astype(jnp.bfloat16), "exp", split_axis=0, concat_axis=0, tiled=True
    ).astype(rows_back.dtype)
    returned_grads = place_slots(returned_grads)
    d_expert_gate = jnp.einsum(
        "sxcd,sxcf->xdf", arrived_rows, grad_gate_pre, preferred_element_type=jnp.float32
    )
    d_expert_up = jnp.einsum(
        "sxcd,sxcf->xdf", arrived_rows, grad_up_pre, preferred_element_type=jnp.float32
    )
    d_expert_down = jnp.einsum(
        "sxcf,sxcd->xfd", inner, arrived_grads, preferred_element_type=jnp.float32
    )
    grad_rows = returned_grads.reshape(expert_count * capacity, model_width)[target].reshape(
        row_count, top_count, model_width
    )
    back_normed = back_normed + jnp.sum(grad_rows, axis=1)
    scalar_part = jnp.concatenate([gate_part, share_part[:, None]], axis=1)
    summed_normed, scalar_sum = (
        lax.psum(back_normed.astype(jnp.bfloat16), "tp").astype(jnp.float32),
        lax.psum(scalar_part.astype(jnp.bfloat16), "tp").astype(jnp.float32),
    )
    grad_gates = scalar_sum[:, :top_count]
    grad_share_weight = scalar_sum[:, top_count]
    grad_router_probs = jnp.einsum("tk,tke->te", grad_gates, chosen)
    grad_logits = (
        router_probs
        * (grad_router_probs - jnp.sum(grad_router_probs * router_probs, axis=1, keepdims=True))
    ).astype(jnp.bfloat16)
    grad_share_logit = (grad_share_weight * share_weight * (1.0 - share_weight)).astype(
        jnp.bfloat16
    )
    d_router = product_at(normed, grad_logits)
    d_share_vector = product(grad_share_logit, normed)
    grad_normed = (
        summed_normed
        + product_bt(grad_logits, router_full)
        + grad_share_logit.astype(jnp.float32)[:, None] * share_vector.astype(jnp.float32)[None, :]
    )
    norm_rows, d_gain_experts = norm_back(grad_normed, hidden_state, inverse_second, ffn_gain)
    grad_hidden = grad_out + norm_rows
    grad_hidden_low = grad_hidden.astype(jnp.bfloat16)
    d_out_weight = product_at(attended, grad_hidden_low)
    grad_attended = (
        product_bt(grad_hidden_low, out_full)
        .astype(jnp.bfloat16)
        .reshape(row_count, heads_here, head_dim)
    )
    scores = (
        jnp.einsum("qhd,khd->hqk", query_rot, all_keys, preferred_element_type=jnp.float32) * scale
    )
    scores = jnp.where(allowed[None, :, :], scores, MASKED)
    probs_again = jnp.exp(scores - log_total)
    probs_low = probs_again.astype(jnp.bfloat16)
    grad_values = jnp.einsum(
        "hqk,qhd->khd", probs_low, grad_attended, preferred_element_type=jnp.float32
    )
    grad_probs = jnp.einsum(
        "qhd,khd->hqk", grad_attended, all_values, preferred_element_type=jnp.float32
    )
    grad_scores = (
        probs_again * (grad_probs - jnp.sum(probs_again * grad_probs, axis=2, keepdims=True))
    ).astype(jnp.bfloat16)
    grad_query = (
        jnp.einsum("hqk,khd->qhd", grad_scores, all_keys, preferred_element_type=jnp.float32)
        * scale
    )
    grad_keys = (
        jnp.einsum("hqk,qhd->khd", grad_scores, query_rot, preferred_element_type=jnp.float32)
        * scale
    )
    own_key_grads = grad_keys[:row_count]
    own_value_grads = grad_values[:row_count]
    for distance in range(1, group_size):
        lower_row = distance * row_count
        later_keys, later_values = (
            shifted(
                grad_keys[lower_row : lower_row + row_count].astype(jnp.bfloat16), "exp", -distance
            ).astype(jnp.float32),
            shifted(
                grad_values[lower_row : lower_row + row_count].astype(jnp.bfloat16),
                "exp",
                -distance,
            ).astype(jnp.float32),
        )
        own_key_grads = own_key_grads + later_keys
        own_value_grads = own_value_grads + later_values
    grad_query_lin = (
        rotate_back(grad_query, cosine, sine_table)
        .reshape(row_count, heads_here * head_dim)
        .astype(jnp.bfloat16)
    )
    grad_key_lin = (
        rotate_back(own_key_grads, cosine, sine_table)
        .reshape(row_count, heads_here * head_dim)
        .astype(jnp.bfloat16)
    )
    grad_value_lin = own_value_grads.reshape(row_count, heads_here * head_dim).astype(jnp.bfloat16)
    d_query = product_at(normed_first, grad_query_lin)
    d_key = product_at(normed_first, grad_key_lin)
    d_value = product_at(normed_first, grad_value_lin)
    d_query_bias = jnp.sum(grad_query_lin.astype(jnp.float32), axis=0)
    d_key_bias = jnp.sum(grad_key_lin.astype(jnp.float32), axis=0)
    d_value_bias = jnp.sum(grad_value_lin.astype(jnp.float32), axis=0)
    back_first = (
        product_bt(grad_query_lin, query_full)
        + product_bt(grad_key_lin, key_full)
        + product_bt(grad_value_lin, value_full)
    )
    back_first = lax.psum(back_first.astype(jnp.bfloat16), "tp").astype(jnp.float32)
    first_rows, d_gain_attention = norm_back(back_first, input_rows, inverse_first, attn_gain)
    grad_input = grad_hidden + first_rows
    reduced = (
        lax.psum_scatter(
            d_query.astype(jnp.bfloat16), "exp", scatter_dimension=0, tiled=True
        ).astype(jnp.float32),
        lax.psum_scatter(d_key.astype(jnp.bfloat16), "exp", scatter_dimension=0, tiled=True).astype(
            jnp.float32
        ),
        lax.psum_scatter(
            d_value.astype(jnp.bfloat16), "exp", scatter_dimension=0, tiled=True
        ).astype(jnp.float32),
        lax.psum_scatter(
            d_out_weight.astype(jnp.bfloat16), "exp", scatter_dimension=1, tiled=True
        ).astype(jnp.float32),
        lax.psum_scatter(
            d_query_bias.astype(jnp.bfloat16), "exp", scatter_dimension=0, tiled=True
        ).astype(jnp.float32),
        lax.psum_scatter(
            d_key_bias.astype(jnp.bfloat16), "exp", scatter_dimension=0, tiled=True
        ).astype(jnp.float32),
        lax.psum_scatter(
            d_value_bias.astype(jnp.bfloat16), "exp", scatter_dimension=0, tiled=True
        ).astype(jnp.float32),
        lax.psum_scatter(
            d_gain_attention.astype(jnp.bfloat16), "exp", scatter_dimension=0, tiled=True
        ).astype(jnp.float32),
        lax.psum_scatter(
            d_gain_experts.astype(jnp.bfloat16), "exp", scatter_dimension=0, tiled=True
        ).astype(jnp.float32),
        lax.psum_scatter(
            d_router.astype(jnp.bfloat16), "exp", scatter_dimension=0, tiled=True
        ).astype(jnp.float32),
        lax.psum_scatter(
            d_share_vector.astype(jnp.bfloat16), "exp", scatter_dimension=0, tiled=True
        ).astype(jnp.float32),
        lax.psum_scatter(
            d_shared_gate.astype(jnp.bfloat16), "exp", scatter_dimension=0, tiled=True
        ).astype(jnp.float32),
        lax.psum_scatter(
            d_shared_up.astype(jnp.bfloat16), "exp", scatter_dimension=0, tiled=True
        ).astype(jnp.float32),
        lax.psum_scatter(
            d_shared_down.astype(jnp.bfloat16), "exp", scatter_dimension=1, tiled=True
        ).astype(jnp.float32),
    )
    square_sums = lax.psum((jnp.sum(output * output), jnp.sum(grad_input * grad_input)), "exp")
    count_cells = jnp.sum(lengths).astype(jnp.float32) * model_width
    rms_output = jnp.sqrt(square_sums[0] / count_cells)
    rms_grad = jnp.sqrt(square_sums[1] / count_cells)
    return (
        output.astype(jnp.bfloat16),
        grad_input.astype(jnp.bfloat16),
        reduced[0],
        reduced[1],
        reduced[2],
        reduced[3],
        reduced[4],
        reduced[5],
        reduced[6],
        reduced[7],
        reduced[8],
        reduced[9],
        reduced[10],
        reduced[11],
        reduced[12],
        reduced[13],
        d_expert_gate,
        d_expert_up,
        d_expert_down,
        rms_output,
        rms_grad,
    )


def flat(pieces):
    return jnp.concatenate([p.reshape(-1) for p in pieces])


def key_window(info_ref, block, keys):
    return lax.rem(block + info_ref[0], 2), pl.ds(pl.multiple_of(block // 2 * keys, keys), keys)


def attend_back_kernel(
    info_ref, q_ref, kv_ref, do_ref, o_ref, lse_ref, dq_ref, dk_ref, dv_ref, *, tile, keys, rows
):
    step = pl.program_id(0)
    per_block = rows // tile
    base = (2 * (step // per_block) + info_ref[0]) * rows + (step % per_block) * tile

    @pl.when(step == 0)
    def _():
        dk_ref[...] = jnp.zeros_like(dk_ref)
        dv_ref[...] = jnp.zeros_like(dv_ref)

    query = q_ref[...]
    grad = do_ref[...]
    log_total = lse_ref[:, 0:1]
    delta = jnp.sum(grad.astype(jnp.float32) * o_ref[...], axis=1, keepdims=True)
    row_pos = base + lax.broadcasted_iota(jnp.int32, (tile, 1), 0)
    limit = jnp.minimum(row_pos, info_ref[1] - 1)
    column = lax.broadcasted_iota(jnp.int32, (tile, keys), 1)

    def body(j, acc):
        side, window = key_window(info_ref, j, keys)
        key = kv_ref[side, window, :HEAD_DIM]
        scores = product_bt(query, key) * (1.0 / HEAD_DIM**0.5)
        scores = jnp.where(column <= limit - j * keys, scores, MASKED)
        probs = jnp.exp(scores - log_total)
        dv_ref[side, window, :] += product_at(probs.astype(jnp.bfloat16), grad)
        grad_probs = product_bt(grad, kv_ref[side, window, HEAD_DIM:])
        grad_scores = (probs * (grad_probs - delta)).astype(jnp.bfloat16)
        dk_ref[side, window, :] += product_at(grad_scores, query)
        return acc + product(grad_scores, key)

    count = (base + tile + keys - 1) // keys
    dq_ref[...] = lax.fori_loop(0, count, body, jnp.zeros((tile, HEAD_DIM), jnp.float32))


def attend_back(info, query, key_values, grad, out, log_total, rows):
    count = query.shape[0]
    tile = 256
    half = key_values.shape[:2] + (HEAD_DIM,)
    whole = pl.BlockSpec(half, lambda i: (0, 0, 0))
    both = pl.BlockSpec(key_values.shape, lambda i: (0, 0, 0))
    part = pl.BlockSpec((tile, HEAD_DIM), lambda i: (i, 0))
    return pl.pallas_call(
        functools.partial(attend_back_kernel, tile=tile, keys=rows, rows=rows),
        grid=(count // tile,),
        in_specs=[pl.BlockSpec(memory_space=pltpu.SMEM), part, both, part, part, part],
        out_specs=[part, whole, whole],
        out_shape=[
            jax.ShapeDtypeStruct((count, HEAD_DIM), jnp.float32),
            jax.ShapeDtypeStruct(half, jnp.float32),
            jax.ShapeDtypeStruct(half, jnp.float32),
        ],
        compiler_params=pltpu.CompilerParams(vmem_limit_bytes=40 * 2**20),
        cost_estimate=pl.CostEstimate(
            flops=10 * count * count * HEAD_DIM,
            bytes_accessed=12 * 2**20,
            transcendentals=count * count,
        ),
    )(info, query, key_values, grad, out, log_total)


ROW_AXES = ("z", "x")
COLUMN_AXES = ("y", "c")
ALL_AXES = ("z", "x", "y", "c")
CHUNK_AXES = ("c", "y", "x", "z")
SAME_X = ("c", "y", "z")


def front_kernel(own_ref, parts_ref, rows_ref, weights_ref, send, send_z, recv, send_w, recv_w, here):
    z, x, y, c = (lax.axis_index(name) for name in ALL_AXES)
    z_count = lax.axis_size("z")
    chunks = own_ref.shape[0]

    def up(distance):
        return {"z": lax.rem(z + distance, z_count)}

    def remote(src, dst, send_sem, recv_sem, device):
        return pltpu.make_async_remote_copy(
            src_ref=src,
            dst_ref=dst,
            send_sem=send_sem,
            recv_sem=recv_sem,
            device_id=device,
            device_id_type=pl.DeviceIdType.MESH,
        )

    def spread_z(k, d):
        block = rows_ref.at[c, y, z, k]
        return remote(own_ref.at[k], block, send_z.at[d - 1, k], recv.at[1 + d, k], up(d))

    def spread_y(k):
        block = rows_ref.at[c, y, :, k]
        return remote(block, block, send.at[0, k], recv.at[0, k], {"y": 1 - y})

    def spread_c(k):
        block = rows_ref.at[c, :, :, k]
        return remote(block, block, send.at[1, k], recv.at[1, k], {"c": 1 - c})

    def weights_z(d):
        there = lax.rem(z + d, z_count)
        return remote(
            parts_ref.at[there], weights_ref.at[z, x], send_w.at[d], recv_w.at[d], up(d)
        )

    def weights_x():
        block = weights_ref.at[:, x]
        return remote(block, block, send_w.at[0], recv_w.at[0], {"x": 1 - x})

    barrier = pltpu.get_barrier_semaphore()
    for device in ({"x": 1 - x}, {"y": 1 - y}, {"c": 1 - c}, up(1), up(2), up(3)):
        pl.semaphore_signal(
            barrier, inc=1, device_id=device, device_id_type=pl.DeviceIdType.MESH
        )
    keep = pltpu.make_async_copy(own_ref, rows_ref.at[c, y, z], here.at[0])
    keep_w = pltpu.make_async_copy(parts_ref.at[z], weights_ref.at[z, x], here.at[1])
    keep.start()
    keep_w.start()
    pl.semaphore_wait(barrier, 6)
    for k in range(chunks):
        for d in range(1, 4):
            spread_z(k, d).start()
        if k == 0:
            for d in range(1, 4):
                weights_z(d).start()
    keep.wait()
    keep_w.wait()
    for k in range(chunks):
        for d in range(1, 4):
            spread_z(k, d).wait()
        spread_y(k).start()
        if k == 0:
            for d in range(1, 4):
                weights_z(d).wait()
            weights_x().start()
        if k > 0:
            spread_y(k - 1).wait()
            spread_c(k - 1).start()
    spread_y(chunks - 1).wait()
    spread_c(chunks - 1).start()
    for k in range(chunks):
        spread_c(k).wait()
    weights_x().wait()


def front(rows, parts, chunks=4):
    own, model = rows.shape
    zs = lax.axis_size("z")
    shape = (2, 2, zs, chunks, own // chunks, model)
    anywhere = pl.BlockSpec(memory_space=pl.ANY)
    dma = pltpu.SemaphoreType.DMA
    gathered, weights = pl.pallas_call(
        front_kernel,
        in_specs=[anywhere, anywhere],
        out_specs=[anywhere, anywhere],
        out_shape=[
            jax.ShapeDtypeStruct(shape, rows.dtype),
            jax.ShapeDtypeStruct((zs, 2) + parts.shape[1:], parts.dtype),
        ],
        scratch_shapes=[
            dma((2, chunks)),
            dma((3, chunks)),
            dma((5, chunks)),
            dma((4,)),
            dma((4,)),
            dma((2,)),
        ],
        compiler_params=pltpu.CompilerParams(
            collective_id=0, has_side_effects=True, vmem_limit_bytes=16 * 2**20
        ),
    )(rows.reshape(chunks, own // chunks, model), parts)
    return gathered.reshape(4 * zs * own, model), weights


def middle_kernel(
    length_ref,
    rows_ref,
    w_ref,
    row_ref,
    block_ref,
    leaving_ref,
    sh_ref,
    q_ref,
    kv_ref,
    att_ref,
    lse_ref,
    part_ref,
    joined_ref,
    all_ref,
    shared_ref,
    peaks,
    totals,
    send,
    recv,
    once,
    once_in,
    here,
    *,
    rows,
):
    z, x, y, c = (lax.axis_index(name) for name in ALL_AXES)
    z_count = lax.axis_size("z")
    e_count = 2 * z_count
    chunks = leaving_ref.shape[0]
    head = HEAD_DIM
    count, model = rows_ref.shape
    block = model // e_count
    own = rows // 4
    tile = 2 * own
    flip = {"x": {"x": 1 - x}, "y": {"y": 1 - y}, "c": {"c": 1 - c}}

    def up(distance):
        return {"z": lax.rem(z + distance, z_count)}

    def copy_to(src, dst, send_sem, recv_sem, device):
        return pltpu.make_async_remote_copy(
            src_ref=src,
            dst_ref=dst,
            send_sem=send_sem,
            recv_sem=recv_sem,
            device_id=device,
            device_id_type=pl.DeviceIdType.MESH,
        )

    def remote(slot, k, src, dst, device):
        return copy_to(src, dst, send.at[slot, k], recv.at[slot, k], device)

    def spread_z(k):
        return [
            remote(4 + d, k, leaving_ref.at[k], all_ref.at[c, y, x, z, k], up(d))
            for d in range(1, 4)
        ]

    def spread_2(k):
        a = all_ref.at[c, y, x, :, k]
        return (remote(0, k, a, a, flip["x"]),)

    def spread_3(k):
        a = all_ref.at[c, y, :, :, k]
        return (remote(1, k, a, a, flip["y"]),)

    def spread_c(k):
        copies = []
        for j in range(2):
            a = all_ref.at[c, j, :, :, k]
            copies.append(remote(2 + j, k, a, a, flip["c"]))
        return copies

    def share(d, other):
        z_to, x_to = lax.rem(z + d, z_count), 1 - x if other else x
        i = d + z_count if other else d
        return copy_to(
            sh_ref.at[2 * z_to + x_to],
            shared_ref.at[2 * z + x],
            once.at[i],
            once_in.at[i],
            {"z": z_to, "x": x_to},
        )

    def key_values():
        return copy_to(kv_ref.at[0], kv_ref.at[1], once.at[0], once_in.at[0], flip["x"])

    def start(copies):
        for copy in copies:
            copy.start()

    def finish(copies):
        for copy in copies:
            copy.wait()

    barrier = pltpu.get_barrier_semaphore()
    partners = [flip["x"], flip["y"], flip["c"], up(1), up(2), up(3)]
    partners += [{"z": lax.rem(z + d, z_count), "x": 1 - x} for d in range(1, 4)]
    for device in partners:
        pl.semaphore_signal(
            barrier, inc=1, device_id=device, device_id_type=pl.DeviceIdType.MESH
        )
    keep = pltpu.make_async_copy(leaving_ref, all_ref.at[c, y, x, z], here.at[0])
    keep_share = pltpu.make_async_copy(
        sh_ref.at[2 * z + x], shared_ref.at[2 * z + x], here.at[1]
    )
    keep.start()
    keep_share.start()
    for i in range(z_count):
        for j in range(2):
            e = 2 * i + j
            joined_ref[e * block : (e + 1) * block] = w_ref[i, j, :block]
    bias = w_ref[z, 0, pl.ds(block, 16)].astype(jnp.float32) + w_ref[
        z, 1, pl.ds(block, 16)
    ].astype(jnp.float32)
    bias = bias[0:1, : 3 * head]
    lane = lax.broadcasted_iota(jnp.int32, (1, head), 1)
    sign = jnp.where(lane < head // 2, -1.0, 1.0)
    pl.semaphore_wait(barrier, 9)
    for k in range(chunks):
        start(spread_z(k))
    shares = [share(d, other) for d in range(4) for other in (False, True) if d or other]

    def project(t, carry):
        lin = product(rows_ref[pl.ds(t * tile, tile), :], joined_ref[:, : 3 * head]) + bias
        for h in range(2):
            s = 2 * t + h
            z_of, y_of, c_of = lax.rem(s, 4), lax.rem(s // 4, 2), s // 8
            place = pl.ds(pl.multiple_of((z_of * 4 + y_of * 2 + c_of) * own, own), own)
            block_cos, block_sin = block_ref[x, 0, pl.ds(s, 1)], block_ref[x, 1, pl.ds(s, 1)]
            cosine = block_cos * row_ref[0] - block_sin * row_ref[1]
            sine = (block_sin * row_ref[0] + block_cos * row_ref[1]) * sign
            part = lin[h * own : (h + 1) * own]
            query, key = part[:, :head], part[:, head : 2 * head]
            query = query * cosine + pltpu.roll(query, head // 2, 1) * sine
            key = key * cosine + pltpu.roll(key, head // 2, 1) * sine
            q_ref[place, :] = query.astype(jnp.bfloat16)
            kv_ref[0, place, :head] = key.astype(jnp.bfloat16)
            kv_ref[0, place, head:] = part[:, 2 * head :].astype(jnp.bfloat16)
        return carry

    lax.fori_loop(0, count // tile, project, 0)
    key_values().start()
    start(shares)
    keep.wait()
    finish(spread_z(0))
    start(spread_2(0))
    column = lax.broadcasted_iota(jnp.int32, (tile, rows), 1)

    def scan(i, side, blocks, carry):
        query = q_ref[pl.ds(pl.multiple_of(i * tile, tile), tile), :]
        base = (2 * (i // 2) + x) * rows + lax.rem(i, 2) * tile
        row_pos = base + lax.broadcasted_iota(jnp.int32, (tile, 1), 0)
        limit = jnp.minimum(row_pos, length_ref[0] - 1)
        parity = x if side == 0 else 1 - x

        def body(m, carry):
            peak, total, acc = carry
            window = pl.ds(pl.multiple_of(m * rows, rows), rows)
            scores = product_bt(query, kv_ref[side, window, :head]) * (1.0 / head**0.5)
            scores = jnp.where(column <= limit - (2 * m + parity) * rows, scores, MASKED)
            new_peak = jnp.maximum(peak, jnp.max(scores, axis=1, keepdims=True))
            weights = jnp.exp(scores - new_peak)
            shrink = jnp.exp(peak - new_peak)
            total = shrink * total + jnp.sum(weights, axis=1, keepdims=True)
            acc = shrink * acc + product(
                weights.astype(jnp.bfloat16), kv_ref[side, window, head:]
            )
            return (new_peak, total, acc)

        return lax.fori_loop(0, blocks, body, carry)

    def first_pass(i, carry):
        peak, total, acc = scan(
            i,
            0,
            i // 2 + 1,
            (
                jnp.full((tile, 1), MASKED, jnp.float32),
                jnp.zeros((tile, 1), jnp.float32),
                jnp.zeros((tile, head), jnp.float32),
            ),
        )
        place = pl.ds(pl.multiple_of(i * tile, tile), tile)
        peaks[place, :] = jnp.broadcast_to(peak, (tile, head))
        totals[place, :] = jnp.broadcast_to(total, (tile, head))
        att_ref[place, :] = acc
        return carry

    lax.fori_loop(0, count // tile, first_pass, 0)
    finish(spread_z(1))
    start(spread_2(1))
    finish(spread_2(0))
    start(spread_3(0))
    key_values().wait()

    def second_pass(i, carry):
        place = pl.ds(pl.multiple_of(i * tile, tile), tile)
        peak, total, acc = scan(
            i, 1, i // 2 + x, (peaks[place, 0:1], totals[place, 0:1], att_ref[place, :])
        )
        acc = acc / total
        att_ref[place, :] = acc
        lse_ref[place, :] = jnp.broadcast_to(peak + jnp.log(total), (tile, head))
        part = product_bt(acc.astype(jnp.bfloat16), joined_ref[:, 3 * head :]).astype(
            jnp.bfloat16
        )
        for h in range(2):
            z_of, y_of, c_of = i // 2, lax.rem(i, 2), h
            part_ref[c_of * 8 + y_of * 4 + z_of] = part[h * own : (h + 1) * own]

        @pl.when(i == 2)
        def _():
            finish(spread_z(2))
            start(spread_2(2))
            finish(spread_2(1))
            start(spread_3(1))

        @pl.when(i == 5)
        def _():
            finish(spread_z(3))
            start(spread_2(3))
            finish(spread_2(2))
            start(spread_3(2))
            finish(spread_3(0))
            start(spread_c(0))

        return carry

    lax.fori_loop(0, count // tile, second_pass, 0)
    finish(spread_2(3))
    start(spread_3(3))
    for k in range(1, chunks):
        finish(spread_3(k))
        start(spread_c(k))
    for k in range(chunks):
        finish(spread_c(k))
    finish(shares)
    keep_share.wait()


def middle(length, gathered, weights, row_table, block_table, leaving, shared, rows, chunks=4):
    own, wide = leaving.shape
    count, model = gathered.shape
    zs = lax.axis_size("z")
    head = HEAD_DIM
    piece = own // chunks
    bf16, f32 = jnp.bfloat16, jnp.float32
    anywhere = pl.BlockSpec(memory_space=pl.ANY)
    inside = pl.BlockSpec(memory_space=pltpu.VMEM)
    vm, dma = pltpu.VMEM, pltpu.SemaphoreType.DMA
    shape = jax.ShapeDtypeStruct
    results = pl.pallas_call(
        functools.partial(middle_kernel, rows=rows),
        in_specs=[pl.BlockSpec(memory_space=pltpu.SMEM)] + [inside] * 4 + [anywhere] * 2,
        out_specs=[inside] * 6 + [anywhere] * 2,
        out_shape=[
            shape((count, head), bf16),
            shape((2, count, 2 * head), bf16),
            shape((count, head), f32),
            shape((count, head), f32),
            shape((count // own, own, model), bf16),
            shape((model, 4 * head), bf16),
            shape((2, 2, 2, zs, chunks, piece, wide), bf16),
            shape(shared.shape, bf16),
        ],
        scratch_shapes=[
            vm((count, head), f32),
            vm((count, head), f32),
            dma((8, chunks)),
            dma((8, chunks)),
            dma((8,)),
            dma((8,)),
            dma((2,)),
        ],
        compiler_params=pltpu.CompilerParams(
            collective_id=3, has_side_effects=True, vmem_limit_bytes=56 * 2**20
        ),
        cost_estimate=pl.CostEstimate(
            flops=10 * count * model * head, bytes_accessed=60 * 2**20, transcendentals=count * count
        ),
    )(
        length,
        gathered,
        weights,
        row_table,
        block_table,
        leaving.reshape(chunks, piece, wide),
        shared,
    )
    query, key_values, attended, log_total, partial, joined, spread, shared = results
    return (
        query,
        key_values,
        attended,
        log_total,
        partial.reshape(count, model),
        joined,
        spread.reshape(8 * zs * own, wide),
        shared,
    )


def expert_rows(first, normed, grads, routes, w_ref, d_ref, s_ref, units, experts):
    width = d_ref.shape[0]
    rows = normed.shape[0]
    pre = product_bt(normed, w_ref[...])
    gate_pre = pre[:, :width]
    up_pre = pre[:, width:]
    lane = lax.broadcasted_iota(jnp.int32, (rows, 128), 1)
    router_lane = lane - (128 - experts)
    logits = jnp.where(router_lane >= 0, gate_pre[:, width - 128 :], MASKED)
    expo = jnp.exp(logits - jnp.max(logits, axis=1, keepdims=True))
    probs = expo / jnp.sum(expo, axis=1, keepdims=True)

    def gate_of(expert):
        picked = jnp.sum((routes == expert).astype(jnp.float32), axis=1, keepdims=True)
        return picked * jnp.sum(
            jnp.where(router_lane == expert, probs, 0.0), axis=1, keepdims=True
        )

    share = jax.nn.sigmoid(
        jnp.sum(jnp.where(router_lane == 0, up_pre[:, width - 128 :], 0.0), axis=1, keepdims=True)
    )
    column = lax.broadcasted_iota(jnp.int32, (rows, width), 1)
    scale = jnp.where(column < width - experts, share, 0.0)
    for index in reversed(range(2)):
        scale = jnp.where(column < (index + 1) * units, gate_of(first + index), scale)
    sigma = jax.nn.sigmoid(gate_pre)
    swish = gate_pre * sigma
    hidden = swish * up_pre
    scaled = (hidden * scale).astype(jnp.bfloat16)
    mixture = product(scaled, d_ref[...]).astype(jnp.bfloat16)
    back = product_bt(grads, d_ref[...])
    gate_sums = product((back * hidden).astype(jnp.bfloat16), s_ref[...]).astype(jnp.bfloat16)
    back = back * scale
    grad_gate = (back * up_pre * (sigma * (1.0 + gate_pre * (1.0 - sigma)))).astype(jnp.bfloat16)
    grad_up = (back * swish).astype(jnp.bfloat16)
    pushed = product(grad_gate, w_ref[:width]) + product(grad_up, w_ref[width:])
    return scaled, grad_gate, grad_up, mixture, pushed.astype(jnp.bfloat16), gate_sums


def add_low(*terms):
    total = terms[0].astype(jnp.float32)
    for term in terms[1:]:
        total = total + term.astype(jnp.float32)
    return total.astype(jnp.bfloat16)


def stream_kernel(
    part_ref,
    x_ref,
    gain_ref,
    g_ref,
    eg_ref,
    eu_ref,
    ed_ref,
    sh_ref,
    router_ref,
    s_ref,
    all_ref,
    hs_ref,
    dgu_ref,
    out_ref,
    hidden_ref,
    own_ref,
    lrc_ref,
    lr2_ref,
    lr3_ref,
    lca_ref,
    lcb_ref,
    l2a_ref,
    l2b_ref,
    l3a_ref,
    l3b_ref,
    lza_ref,
    lzb_ref,
    w_ref,
    d_ref,
    n_buf,
    g_buf,
    pa,
    pb,
    ca,
    cb,
    da,
    db,
    ea,
    eb,
    fa,
    fb,
    qa,
    qb,
    sa,
    sb,
    ta,
    tb,
    hs_buf,
    dgu_buf,
    ra,
    rb,
    rc,
    rd,
    re,
    rf,
    send,
    send_z,
    send_r,
    send_c,
    recv_c,
    recv,
    here,
    weigh,
    *,
    units,
    experts,
):
    z, x, y, c = (lax.axis_index(name) for name in ALL_AXES)
    z_count = lax.axis_size("z")
    chunks = x_ref.shape[0]
    model = x_ref.shape[2]
    width = d_ref.shape[0]
    cut = pa.shape[-1]
    half = model // 2
    left, right = pl.ds(0, half), pl.ds(half, half)
    first = 2 * (2 * z + x)
    flip = {"x": {"x": 1 - x}, "y": {"y": 1 - y}, "c": {"c": 1 - c}}

    def up(distance):
        return {"z": lax.rem(z + distance, z_count)}

    def remote(slot, k, src, dst, device):
        return pltpu.make_async_remote_copy(
            src_ref=src,
            dst_ref=dst,
            send_sem=send.at[slot, lax.rem(k, 2)],
            recv_sem=recv.at[slot, k],
            device_id=device,
            device_id_type=pl.DeviceIdType.MESH,
        )

    def spread_z(k, d):
        return pltpu.make_async_remote_copy(
            src_ref=own_ref.at[k],
            dst_ref=all_ref.at[c, y, x, z, k],
            send_sem=send_z.at[d - 1, k],
            recv_sem=recv.at[20 + d, k],
            device_id=up(d),
            device_id_type=pl.DeviceIdType.MESH,
        )

    def heads_c(k):
        return pltpu.make_async_remote_copy(
            src_ref=part_ref.at[1 - c, :, :, k],
            dst_ref=lrc_ref.at[k],
            send_sem=send_r.at[k],
            recv_sem=recv.at[24, k],
            device_id=flip["c"],
            device_id_type=pl.DeviceIdType.MESH,
        )

    def heads_y(k):
        return (remote(17, k, rc.at[lax.rem(k, 2), 1 - y], lr2_ref.at[k], flip["y"]),)

    def heads_z(k):
        copies = []
        for d in range(1, 4):
            there = lax.rem(z + d, z_count)
            copies.append(remote(17 + d, k, re.at[lax.rem(k, 2), there], lr3_ref.at[k, d - 1], up(d)))
        return copies

    def load_hc(k):
        return (
            pltpu.make_async_copy(part_ref.at[c, :, :, k], ra, here.at[15]),
            pltpu.make_async_copy(lrc_ref.at[k], rb, here.at[16]),
        )

    def load_hy(k):
        return (pltpu.make_async_copy(lr2_ref.at[k], rd, here.at[17]),)

    def load_hz(k):
        return (pltpu.make_async_copy(lr3_ref.at[k], rf, here.at[18]),)

    def keep(k):
        return pltpu.make_async_copy(own_ref.at[k], all_ref.at[c, y, x, z, k], here.at[19 + lax.rem(k, 2)])

    def spread_2(k):
        a = all_ref.at[c, y, x, :, k, :, left]
        b = all_ref.at[c, y, x, :, k, :, right]
        return remote(0, k, a, a, flip["x"]), remote(1, k, b, b, flip["y"])

    def spread_3(k):
        a = all_ref.at[c, y, :, :, k, :, left]
        b = all_ref.at[c, :, x, :, k, :, right]
        return remote(2, k, a, a, flip["y"]), remote(3, k, b, b, flip["x"])

    def across(slot, k, src, dst):
        return pltpu.make_async_remote_copy(
            src_ref=src,
            dst_ref=dst,
            send_sem=send_c.at[slot, lax.rem(k, 2)],
            recv_sem=recv_c.at[slot, k],
            device_id=flip["c"],
            device_id_type=pl.DeviceIdType.MESH,
        )

    def spread_c(k):
        copies = []
        for j in range(2):
            for m in range(2):
                a = all_ref.at[c, j, m, :, k]
                copies.append(across(2 * j + m, k, a, a))
        return copies

    def sum_c(k):
        slot = lax.rem(k, 2)
        copies = []
        for j in range(2):
            for m in range(2):
                i = 4 + 2 * j + m
                copies.append(across(i, k, pa.at[slot, 1 - c, j, m], lca_ref.at[k, j, m]))
                copies.append(across(4 + i, k, pb.at[slot, 1 - c, j, m], lcb_ref.at[k, j, m]))
        return copies

    def sum_2(k):
        return (
            remote(7, k, qa.at[lax.rem(k, 2), 1 - y], l2a_ref.at[k], flip["y"]),
            remote(8, k, qb.at[lax.rem(k, 2), :, 1 - x], l2b_ref.at[k], flip["x"]),
        )

    def sum_3(k):
        return (
            remote(9, k, sa.at[lax.rem(k, 2), 1 - x], l3a_ref.at[k], flip["x"]),
            remote(10, k, sb.at[lax.rem(k, 2), 1 - y], l3b_ref.at[k], flip["y"]),
        )

    def sum_z(k):
        copies = []
        for d in range(1, 4):
            there = lax.rem(z + d, z_count)
            copies.append(remote(10 + d, k, ta.at[lax.rem(k, 2), there], lza_ref.at[k, d - 1], up(d)))
            copies.append(remote(13 + d, k, tb.at[lax.rem(k, 2), there], lzb_ref.at[k, d - 1], up(d)))
        return copies

    def load_rows(k):
        slot = lax.rem(k, 2)
        return (
            pltpu.make_async_copy(all_ref.at[:, :, :, :, k], n_buf.at[slot], here.at[slot]),
            pltpu.make_async_copy(g_ref.at[:, :, :, :, k], g_buf.at[slot], here.at[13 + slot]),
        )

    def load_c(k):
        return (
            pltpu.make_async_copy(lca_ref.at[k], ca, here.at[2]),
            pltpu.make_async_copy(lcb_ref.at[k], cb, here.at[3]),
        )

    def load_2(k):
        return (
            pltpu.make_async_copy(l2a_ref.at[k], da, here.at[4]),
            pltpu.make_async_copy(l2b_ref.at[k], db, here.at[5]),
        )

    def load_3(k):
        return (
            pltpu.make_async_copy(l3a_ref.at[k], ea, here.at[6]),
            pltpu.make_async_copy(l3b_ref.at[k], eb, here.at[7]),
        )

    def load_z(k):
        return (
            pltpu.make_async_copy(lza_ref.at[k], fa, here.at[8]),
            pltpu.make_async_copy(lzb_ref.at[k], fb, here.at[9]),
        )

    def store_rows(k):
        return (
            pltpu.make_async_copy(hs_buf, hs_ref.at[:, :, :, :, k], here.at[10]),
            pltpu.make_async_copy(dgu_buf, dgu_ref.at[:, :, :, :, k], here.at[11]),
        )

    def start(copies):
        for copy in copies:
            copy.start()

    def finish(copies):
        for copy in copies:
            copy.wait()

    def at(k, body):
        pl.when((k >= 0) & (k < chunks))(lambda: body(k))

    barrier = pltpu.get_barrier_semaphore()
    for device in (flip["x"], flip["y"], flip["c"], up(1), up(2), up(3)):
        pl.semaphore_signal(
            barrier, inc=1, device_id=device, device_id_type=pl.DeviceIdType.MESH
        )
    pl.semaphore_wait(barrier, 6)

    def first_sends(k, carry):
        heads_c(k).start()
        return carry

    lax.fori_loop(0, chunks, first_sends, 0)
    routed, share = eg_ref.shape[0], sh_ref.shape[1] // 3
    low = pl.ds(routed, share)
    high = pl.ds(width + routed, share)

    def weight_copies():
        pairs = [
            (eg_ref, w_ref.at[pl.ds(0, routed)]),
            (eu_ref, w_ref.at[pl.ds(width, routed)]),
            (ed_ref, d_ref.at[pl.ds(0, routed)]),
            (router_ref.at[0], w_ref.at[pl.ds(width - experts, experts)]),
            (router_ref.at[1], w_ref.at[pl.ds(2 * width - experts, experts)]),
        ]
        cells = model // sh_ref.shape[0]
        for e in range(sh_ref.shape[0]):
            columns = pl.ds(e * cells, cells)
            pairs.append((sh_ref.at[e, pl.ds(0, share)], w_ref.at[low, columns]))
            pairs.append((sh_ref.at[e, pl.ds(share, share)], w_ref.at[high, columns]))
            pairs.append((sh_ref.at[e, pl.ds(2 * share, share)], d_ref.at[low, columns]))
        return [
            pltpu.make_async_copy(src, dst, weigh.at[i]) for i, (src, dst) in enumerate(pairs)
        ]

    start(weight_copies())
    d_ref[pl.ds(width - experts, experts), :] = jnp.zeros((experts, model), jnp.bfloat16)

    def arrive_hc(k):
        heads_c(k).wait()
        start(load_hc(k))

    def arrive_hy(k):
        finish(heads_y(k))
        start(load_hy(k))

    def arrive_hz(k):
        finish(heads_z(k))
        start(load_hz(k))

    def close_hc(k):
        finish(load_hc(k))
        slot = lax.rem(k, 2)

        def each(i, carry):
            for j in range(2):
                rc[slot, j, i] = add_low(ra[j, i], rb[j, i])
            return carry

        lax.fori_loop(0, z_count, each, 0)
        start(heads_y(k))

    def close_hy(k):
        finish(load_hy(k))
        slot = lax.rem(k, 2)
        for i in range(4):
            re[slot, i] = add_low(rc[slot, y, i], rd[i])
        start(heads_z(k))

    def close_hz(k):
        finish(load_hz(k))
        total = re[lax.rem(k, 2), z].astype(jnp.float32)
        for d in range(3):
            total = total + rf[d].astype(jnp.float32)
        hidden = x_ref[k].astype(jnp.float32) + total
        inverse = lax.rsqrt(jnp.mean(hidden * hidden, axis=1, keepdims=True) + EPSILON)
        hidden_ref[k] = hidden
        own_ref[k] = (hidden * inverse * gain_ref[...]).astype(jnp.bfloat16)
        keep(k).start()
        for d in range(1, 4):
            spread_z(k, d).start()

    def gather_2(k):
        keep(k).wait()
        for d in range(1, 4):
            spread_z(k, d).wait()
        start(spread_2(k))

    def gather_3(k):
        finish(spread_2(k))
        start(spread_3(k))

    def gather_c(k):
        finish(spread_3(k))
        start(spread_c(k))

    def gathered(k):
        finish(spread_c(k))
        start(load_rows(k))

    def work(k, part):
        slot = lax.rem(k, 2)
        rows = 256
        normed = n_buf[slot, part].reshape(rows, model)
        grads = g_buf[slot, part].reshape(rows, model + 128)
        routes = grads[:, model : model + 128].astype(jnp.int32)
        grads = grads[:, :model]
        scaled, grad_gate, grad_up, mixture, pushed, gate_sums = expert_rows(
            first, normed, grads, routes, w_ref, d_ref, s_ref, units, experts
        )
        shape = (2, 2, z_count, 16)
        hs_buf[part] = scaled.reshape(shape + (width,))
        dgu_buf[part, :, :, :, :, :width] = grad_gate.reshape(shape + (width,))
        dgu_buf[part, :, :, :, :, width:] = grad_up.reshape(shape + (width,))
        pa[slot, part] = mixture[:, :cut].reshape(shape + (cut,))
        rest = model - cut
        pb[slot, part, :, :, :, :, :rest] = mixture[:, cut:].reshape(shape + (rest,))
        pb[slot, part, :, :, :, :, rest : rest + model] = pushed.reshape(shape + (model,))
        pb[slot, part, :, :, :, :, rest + model :] = gate_sums.reshape(shape + (128,))

    def work_first(k):
        finish(load_rows(k))
        at(k - 1, lambda j: finish(store_rows(j)))
        work(k, 0)

    def work_second(k):
        work(k, 1)
        start(store_rows(k))

    def arrive_c(k):
        finish(sum_c(k))
        start(load_c(k))

    def arrive_2(k):
        finish(sum_2(k))
        start(load_2(k))

    def arrive_3(k):
        finish(sum_3(k))
        start(load_3(k))

    def arrive_z(k):
        finish(sum_z(k))
        start(load_z(k))

    def close_z(k):
        finish(load_z(k))
        slot = lax.rem(k, 2)
        own_a = ta[slot, z].astype(jnp.float32)
        own_b = tb[slot, z].astype(jnp.float32)
        for d in range(3):
            own_a = own_a + fa[d].astype(jnp.float32)
            own_b = own_b + fb[d].astype(jnp.float32)
        out_ref[k, :, :cut] = own_a
        out_ref[k, :, cut:] = own_b

    def close_3(k):
        finish(load_3(k))
        slot = lax.rem(k, 2)

        def each(i, carry):
            ta[slot, i] = add_low(sa[slot, x, i], ea[i])
            tb[slot, i] = add_low(sb[slot, y, i], eb[i])
            return carry

        lax.fori_loop(0, z_count, each, 0)
        start(sum_z(k))

    def close_2(k):
        finish(load_2(k))
        slot = lax.rem(k, 2)

        def each(i, carry):
            for j in range(2):
                sa[slot, j, i] = add_low(qa[slot, y, j, i], da[j, i])
                sb[slot, j, i] = add_low(qb[slot, j, x, i], db[j, i])
            return carry

        lax.fori_loop(0, z_count, each, 0)
        start(sum_3(k))

    def close_c(k):
        finish(load_c(k))
        slot = lax.rem(k, 2)

        def each(i, carry):
            for j in range(2):
                for m in range(2):
                    qa[slot, j, m, i] = add_low(pa[slot, c, j, m, i], ca[j, m, i])
                    qb[slot, j, m, i] = add_low(pb[slot, c, j, m, i], cb[j, m, i])
            return carry

        lax.fori_loop(0, z_count, each, 0)
        start(sum_2(k))

    def tick(i, carry):
        at(i - 11, gathered)
        at(i - 10, gather_c)
        at(i - 8, gather_3)
        at(i - 6, gather_2)
        pl.when(i == 12)(lambda: finish(weight_copies()))
        at(i - 12, work_first)
        at(i - 19, arrive_z)
        at(i - 17, arrive_3)
        at(i - 15, arrive_2)
        at(i - 13, arrive_c)
        at(i - 4, arrive_hz)
        at(i - 2, arrive_hy)
        at(i, arrive_hc)
        at(i - 12, work_second)
        at(i - 4, close_hz)
        at(i - 2, close_hy)
        at(i, close_hc)
        at(i - 19, close_z)
        at(i - 17, close_3)
        at(i - 15, close_2)
        at(i - 13, close_c)
        at(i - 12, lambda k: start(sum_c(k)))
        return carry

    lax.fori_loop(0, chunks + 19, tick, 0)
    finish(store_rows(chunks - 1))


def stream(
    partial, tokens, gain, grads, gates, ups, downs, shared, router, segments, units, experts, chunks
):
    own, model = tokens.shape
    width = segments.shape[0]
    piece = own // chunks
    zs = lax.axis_size("z")
    lead = (2, 2, 2, zs)
    partial = partial.reshape((2, 2, zs, chunks, piece, model))
    grads = grads.reshape(lead + (chunks, piece, model + 128))
    tokens = tokens.reshape(chunks, piece, model)
    cut = model // 2
    extra = 2 * model + 128 - cut
    bf16 = jnp.bfloat16
    shapes = [
        (lead + (chunks, piece, model), bf16),
        (lead + (chunks, piece, width), bf16),
        (lead + (chunks, piece, 2 * width), bf16),
        ((chunks, piece, 2 * model + 128), jnp.float32),
        ((chunks, piece, model), jnp.float32),
        ((chunks, piece, model), bf16),
        ((chunks, 2, zs, piece, model), bf16),
        ((chunks, zs, piece, model), bf16),
        ((chunks, 3, piece, model), bf16),
        ((chunks, 2, 2, zs, piece, cut), bf16),
        ((chunks, 2, 2, zs, piece, extra), bf16),
        ((chunks, 2, zs, piece, cut), bf16),
        ((chunks, 2, zs, piece, extra), bf16),
        ((chunks, zs, piece, cut), bf16),
        ((chunks, zs, piece, extra), bf16),
        ((chunks, 3, piece, cut), bf16),
        ((chunks, 3, piece, extra), bf16),
    ]
    anywhere = pl.BlockSpec(memory_space=pl.ANY)
    inside = pl.BlockSpec(memory_space=pltpu.VMEM)
    vm = pltpu.VMEM
    dma = pltpu.SemaphoreType.DMA
    scratch = [
        vm((2 * width, model), bf16),
        vm((width, model), bf16),
        vm((2,) + lead + (piece, model), bf16),
        vm((2,) + lead + (piece, model + 128), bf16),
        vm((2,) + lead + (piece, cut), bf16),
        vm((2,) + lead + (piece, extra), bf16),
        vm((2, 2, zs, piece, cut), bf16),
        vm((2, 2, zs, piece, extra), bf16),
        vm((2, zs, piece, cut), bf16),
        vm((2, zs, piece, extra), bf16),
        vm((zs, piece, cut), bf16),
        vm((zs, piece, extra), bf16),
        vm((3, piece, cut), bf16),
        vm((3, piece, extra), bf16),
        vm((2, 2, 2, zs, piece, cut), bf16),
        vm((2, 2, 2, zs, piece, extra), bf16),
        vm((2, 2, zs, piece, cut), bf16),
        vm((2, 2, zs, piece, extra), bf16),
        vm((2, zs, piece, cut), bf16),
        vm((2, zs, piece, extra), bf16),
        vm(lead + (piece, width), bf16),
        vm(lead + (piece, 2 * width), bf16),
        vm((2, zs, piece, model), bf16),
        vm((2, zs, piece, model), bf16),
        vm((2, 2, zs, piece, model), bf16),
        vm((zs, piece, model), bf16),
        vm((2, zs, piece, model), bf16),
        vm((3, piece, model), bf16),
        dma((21, 2)),
        dma((3, chunks)),
        dma((chunks,)),
        dma((12, 2)),
        dma((12, chunks)),
        dma((25, chunks)),
        dma((21,)),
        dma((5 + 3 * shared.shape[0],)),
    ]
    rows = own * 8 * zs
    results = pl.pallas_call(
        functools.partial(stream_kernel, units=units, experts=experts),
        in_specs=[anywhere, inside, inside] + [anywhere] * 6 + [inside],
        out_specs=[anywhere] * 3 + [inside] * 3 + [anywhere] * 11,
        out_shape=[jax.ShapeDtypeStruct(s, t) for s, t in shapes],
        scratch_shapes=scratch,
        compiler_params=pltpu.CompilerParams(
            collective_id=1, has_side_effects=True, vmem_limit_bytes=61 * 2**20
        ),
        cost_estimate=pl.CostEstimate(
            flops=12 * rows * model * width,
            bytes_accessed=rows * (14 * model + 6 * width),
            transcendentals=rows * width,
        ),
    )(partial, tokens, gain, grads, gates, ups, downs, shared, router, segments)
    gathered, scaled, slopes, sums, hidden, normed = results[:6]
    return (
        gathered.reshape(rows, model),
        scaled.reshape(rows, width),
        slopes.reshape(rows, 2 * width),
        sums.reshape(own, 2 * model + 128),
        hidden.reshape(own, model),
        normed.reshape(own, model),
    )


def finish_kernel(
    part_ref,
    grads_ref,
    x_ref,
    wp_ref,
    bp_ref,
    w_ref,
    e_ref,
    scale_ref,
    rows_ref,
    dq_ref,
    dk_ref,
    dv_ref,
    do_ref,
    bias_ref,
    gain_ref,
    square_ref,
    extra_ref,
    lc,
    ly,
    lz,
    rc,
    re,
    gt,
    wl,
    bl,
    ws,
    heads_ref,
    gs,
    gl,
    ss,
    sl,
    ls,
    ll,
    lx,
    lu,
    lv,
    send,
    send_k,
    recv,
    once,
    once_in,
    here,
):
    z, x, y, c = (lax.axis_index(name) for name in ALL_AXES)
    z_count = lax.axis_size("z")
    chunks, _, model = x_ref.shape
    head = HEAD_DIM
    flip = {"x": {"x": 1 - x}, "y": {"y": 1 - y}, "c": {"c": 1 - c}}

    def up(distance):
        return {"z": lax.rem(z + distance, z_count)}

    def copy_to(src, dst, send_sem, recv_sem, device):
        return pltpu.make_async_remote_copy(
            src_ref=src,
            dst_ref=dst,
            send_sem=send_sem,
            recv_sem=recv_sem,
            device_id=device,
            device_id_type=pl.DeviceIdType.MESH,
        )

    def heads_c(k):
        return copy_to(
            part_ref.at[1 - c, :, :, k], lc.at[k], send_k.at[k], recv.at[0, k], flip["c"]
        )

    def heads_y(k):
        return copy_to(rc.at[lax.rem(k, 2), 1 - y], ly.at[k], send.at[0, lax.rem(k, 2)], recv.at[1, k], flip["y"])

    def heads_z(k, d):
        there = lax.rem(z + d, z_count)
        return copy_to(
            re.at[lax.rem(k, 2), there], lz.at[k, d - 1], send.at[d, lax.rem(k, 2)], recv.at[1 + d, k], up(d)
        )

    def keep(k):
        return pltpu.make_async_copy(gt.at[k], rows_ref.at[y, c, k], here.at[lax.rem(k, 2)])

    def rows_y(k):
        return copy_to(gt.at[k], rows_ref.at[y, c, k], send.at[4, lax.rem(k, 2)], recv.at[5, k], flip["y"])

    def rows_c(k):
        block = rows_ref.at[:, c, k]
        return copy_to(block, block, send.at[5, lax.rem(k, 2)], recv.at[6, k], flip["c"])

    def single(i, src, dst, device):
        return copy_to(src, dst, once.at[i], once_in.at[i], device)

    def weights_x():
        return (
            single(0, wp_ref.at[1 - x], wl, flip["x"]),
            single(1, bp_ref.at[1 - x], bl, flip["x"]),
        )

    def weights_z(d):
        return single(1 + d, ws.at[lax.rem(z + d, z_count)], heads_ref.at[z], up(d))

    def at(k, body):
        pl.when((k >= 0) & (k < chunks))(lambda: body(k))

    barrier = pltpu.get_barrier_semaphore()
    for device in (flip["x"], flip["y"], flip["c"], up(1), up(2), up(3)):
        pl.semaphore_signal(
            barrier, inc=1, device_id=device, device_id_type=pl.DeviceIdType.MESH
        )
    square_ref[...] = jnp.zeros_like(square_ref)
    pl.semaphore_wait(barrier, 6)

    def first_sends(k, carry):
        heads_c(k).start()
        return carry

    lax.fori_loop(0, chunks, first_sends, 0)
    for copy in weights_x():
        copy.start()

    def close_c(k):
        heads_c(k).wait()
        slot = lax.rem(k, 2)

        def each(i, carry):
            for j in range(2):
                rc[slot, j, i] = add_low(part_ref[c, j, i, k], lc[k, j, i])
            return carry

        lax.fori_loop(0, z_count, each, 0)
        heads_y(k).start()

    def close_y(k):
        heads_y(k).wait()
        slot = lax.rem(k, 2)
        for i in range(4):
            re[slot, i] = add_low(rc[slot, y, i], ly[k, i])
        for d in range(1, 4):
            heads_z(k, d).start()

    def close_z(k):
        for d in range(1, 4):
            heads_z(k, d).wait()
        pushed = re[lax.rem(k, 2), z].astype(jnp.float32)
        for d in range(3):
            pushed = pushed + lz[k, d].astype(jnp.float32)
        values = x_ref[k].astype(jnp.float32)
        inverse = lax.rsqrt(jnp.mean(values * values, axis=1, keepdims=True) + EPSILON)
        scaled = values * inverse
        total = grads_ref[k] + inverse * (
            pushed - scaled * jnp.mean(pushed * scaled, axis=1, keepdims=True)
        )
        gt[k] = total.astype(jnp.bfloat16)
        squares = total * total
        squares = squares[:8] + squares[8:]
        lanes = squares[:, :128]
        for j in range(1, model // 128):
            lanes = lanes + squares[:, j * 128 : (j + 1) * 128]
        square_ref[...] += lanes
        keep(k).start()
        rows_y(k).start()

    def close_rows(k):
        keep(k).wait()
        rows_y(k).wait()
        rows_c(k).start()

    def close_all(k):
        rows_c(k).wait()

    def weights_sum():
        for copy in weights_x():
            copy.wait()
        bias_ref[...] = bp_ref[x].astype(jnp.float32) + bl[...].astype(jnp.float32)

        def each(i, carry):
            ws[i] = add_low(wp_ref[x, i], wl[i])
            return carry

        lax.fori_loop(0, z_count, each, 0)
        heads_ref[z] = ws[z]
        for d in range(1, 4):
            weights_z(d).start()

    def extra_c():
        return single(13, e_ref, ll.at[0], flip["c"])

    def extra_y():
        return single(14, ls, ll.at[1], flip["y"])

    def extra_x():
        return single(15, lx.at[1 - x], lu, flip["x"])

    def extra_z(d):
        return single(15 + d, lx.at[x, lax.rem(z + d, z_count)], lv.at[d - 1], up(d))

    def extra_sum_c():
        extra_c().wait()
        ls[...] = e_ref[...] + ll[0]
        extra_y().start()

    def extra_sum_y():
        extra_y().wait()
        lx[...] = ls[...] + ll[1]
        extra_x().start()

    def extra_sum_x():
        extra_x().wait()
        lx[x] = lx[x] + lu[...]
        for d in range(1, 4):
            extra_z(d).start()

    def gain_y():
        return single(6, gs.at[0], gl.at[0], flip["y"])

    def gain_c():
        return single(8, gs.at[1], gl.at[1], flip["c"])

    def weights_done():
        for d in range(1, 4):
            weights_z(d).wait()
        total = jnp.zeros(gain_ref.shape, jnp.float32)
        scale = scale_ref[...]
        for i in range(4):
            place = slice(i * head, (i + 1) * head)
            for j, ref in enumerate((dq_ref, dk_ref, dv_ref)):
                columns = slice(j * head, (j + 1) * head)
                values = heads_ref[i, :, columns].astype(jnp.float32)
                total = total + w_ref[i, :, columns].astype(jnp.float32) * values
                ref[:, place] = values * scale
            do_ref[place, :] = heads_ref[i, :, 3 * head :].astype(jnp.float32).T
        gs[0] = total
        gain_y().start()

    def gain_sum():
        gain_y().wait()
        gs[1] = gs[0] + gl[0]
        gain_c().start()

    extra_c().start()

    def tick(i, carry):
        at(i - 7, close_all)
        at(i - 6, close_rows)
        at(i - 4, close_z)
        at(i - 2, close_y)
        at(i, close_c)
        pl.when(i == 2)(weights_sum)
        pl.when(i == 2)(extra_sum_c)
        pl.when(i == 4)(extra_sum_y)
        pl.when(i == 6)(extra_sum_x)
        pl.when(i == 7)(weights_done)
        pl.when(i == 9)(gain_sum)
        return carry

    lax.fori_loop(0, chunks + 7, tick, 0)
    for d in range(1, 4):
        extra_z(d).wait()
    extra_ref[...] = lx[x, z] + lv[0] + lv[1] + lv[2]
    ss[0] = square_ref[...]
    squares_c = single(5, ss.at[0], sl.at[0], flip["c"])
    squares_c.start()
    squares_c.wait()
    ss[1] = ss[0] + sl[0]
    squares_y = single(7, ss.at[1], sl.at[1], flip["y"])
    squares_y.start()
    squares_y.wait()
    ss[2] = ss[1] + sl[1]
    squares_x = single(9, ss.at[2], sl.at[2], flip["x"])
    squares_x.start()
    squares_x.wait()
    ss[3] = ss[2] + sl[2]
    squares_z = [single(9 + d, ss.at[3], sl.at[2 + d], up(d)) for d in range(1, 4)]
    for copy in squares_z:
        copy.start()
    gain_c().wait()
    gain_ref[...] = gs[1] + gl[1]
    for copy in squares_z:
        copy.wait()
    square_ref[...] = ss[3] + sl[3] + sl[4] + sl[5]


def finish(partial, grads, tokens, weight_parts, bias_parts, weights, extras, scale, chunks):
    own, model = tokens.shape
    piece = own // chunks
    zs = lax.axis_size("z")
    bf16, f32 = jnp.bfloat16, jnp.float32
    block, wide = weight_parts.shape[2:]
    anywhere = pl.BlockSpec(memory_space=pl.ANY)
    inside = pl.BlockSpec(memory_space=pltpu.VMEM)
    vm = pltpu.VMEM
    dma = pltpu.SemaphoreType.DMA
    rows, d_query, d_key, d_value, d_out, bias, gain, square, extra = pl.pallas_call(
        finish_kernel,
        in_specs=[inside] * 8,
        out_specs=[anywhere] + [inside] * 8,
        out_shape=[
            jax.ShapeDtypeStruct((2, 2, chunks, piece, model), bf16),
            jax.ShapeDtypeStruct((block, wide), f32),
            jax.ShapeDtypeStruct((block, wide), f32),
            jax.ShapeDtypeStruct((block, wide), f32),
            jax.ShapeDtypeStruct((wide, block), f32),
            jax.ShapeDtypeStruct(bias_parts.shape[1:], f32),
            jax.ShapeDtypeStruct((block, 128), f32),
            jax.ShapeDtypeStruct((8, 128), f32),
            jax.ShapeDtypeStruct(extras.shape[2:], f32),
        ],
        scratch_shapes=[
            vm((chunks, 2, zs, piece, model), bf16),
            vm((chunks, zs, piece, model), bf16),
            vm((chunks, 3, piece, model), bf16),
            vm((2, 2, zs, piece, model), bf16),
            vm((2, zs, piece, model), bf16),
            vm((chunks, piece, model), bf16),
            vm((zs, block, wide), bf16),
            vm(bias_parts.shape[1:], bf16),
            vm((zs, block, wide), bf16),
            vm((zs, block, wide), bf16),
            vm((2, block, 128), f32),
            vm((2, block, 128), f32),
            vm((4, 8, 128), f32),
            vm((6, 8, 128), f32),
            vm(extras.shape, f32),
            vm((2,) + extras.shape, f32),
            vm(extras.shape, f32),
            vm(extras.shape[1:], f32),
            vm((3,) + extras.shape[2:], f32),
            dma((6, 2)),
            dma((chunks,)),
            dma((7, chunks)),
            dma((19,)),
            dma((19,)),
            dma((2,)),
        ],
        compiler_params=pltpu.CompilerParams(
            collective_id=2, has_side_effects=True, vmem_limit_bytes=48 * 2**20
        ),
        cost_estimate=pl.CostEstimate(
            flops=100 * own * model, bytes_accessed=40 * 2**20, transcendentals=0
        ),
    )(
        partial.reshape(2, 2, zs, chunks, piece, model),
        grads.reshape(chunks, piece, model),
        tokens.reshape(chunks, piece, model),
        weight_parts,
        bias_parts,
        weights,
        extras,
        scale,
    )
    return rows.reshape(4 * own, model), d_query, d_key, d_value, d_out, bias, gain, square, extra


def weight_grads_kernel(
    n_ref, g_ref, slopes_ref, scaled_ref, gate_ref, up_ref, down_ref, sh_ref, *, units, share
):
    width = scaled_ref.shape[1]
    low = 2 * units
    first = product_at(n_ref[...], slopes_ref[...]).T
    second = product_at(g_ref[...], scaled_ref[...]).T
    for ref, rows in ((gate_ref, first[:width]), (up_ref, first[width:]), (down_ref, second)):
        for i in range(2):
            ref[i] = rows[i * units : (i + 1) * units]
    for i, rows in enumerate((first[:width], first[width:], second)):
        sh_ref[0, i * share : (i + 1) * share] = rows[low : low + share].astype(jnp.bfloat16)


def weight_grads(normed, grads, slopes, scaled, units, share, blocks):
    count, model = normed.shape
    width = scaled.shape[1]
    block = model // blocks
    one = pl.Buffered(1)
    f32, bf16 = jnp.float32, jnp.bfloat16
    rows = pl.BlockSpec((2, units, block), lambda i: (0, 0, i))
    return pl.pallas_call(
        functools.partial(weight_grads_kernel, units=units, share=share),
        grid=(blocks,),
        in_specs=[
            pl.BlockSpec((count, block), lambda i: (0, i)),
            pl.BlockSpec((count, block), lambda i: (0, i)),
            pl.BlockSpec(slopes.shape, lambda i: (0, 0), pipeline_mode=one),
            pl.BlockSpec(scaled.shape, lambda i: (0, 0), pipeline_mode=one),
        ],
        out_specs=[rows, rows, rows, pl.BlockSpec((1, 3 * share, block), lambda i: (i, 0, 0))],
        out_shape=[jax.ShapeDtypeStruct((2, units, model), f32)] * 3
        + [jax.ShapeDtypeStruct((blocks, 3 * share, block), bf16)],
        compiler_params=pltpu.CompilerParams(vmem_limit_bytes=56 * 2**20),
        cost_estimate=pl.CostEstimate(
            flops=6 * count * model * width,
            bytes_accessed=count * (4 * model + 6 * width) + 12 * model * width,
            transcendentals=0,
        ),
    )(normed, grads, slopes, scaled)


def packed(
    tokens,
    cotangent,
    lengths,
    routes,
    w_query,
    w_key,
    w_value,
    w_out,
    b_query,
    b_key,
    b_value,
    gain_attention,
    gain_experts,
    w_router,
    w_shared_gate,
    shared_gate,
    shared_up,
    shared_down,
    expert_gate,
    expert_up,
    expert_down,
    chunks=8,
):
    f32, bf16 = jnp.float32, jnp.bfloat16
    heads_z = lax.axis_size("z")
    exp_count = heads_z * lax.axis_size("x")
    tp_count = lax.axis_size("y") * lax.axis_size("c")
    z_index, x_index = lax.axis_index("z"), lax.axis_index("x")
    exp_index = z_index * lax.axis_size("x") + x_index
    tp_index = lax.axis_index("y") * lax.axis_size("c") + lax.axis_index("c")
    rows, model = tokens.shape
    total_rows = rows * exp_count
    own = rows // tp_count
    block = model // exp_count
    local_experts, _, units = expert_gate.shape
    experts = local_experts * exp_count
    shared_units = shared_gate.shape[1] // exp_count
    head = HEAD_DIM
    length = lengths[0]

    def my_rows(array):
        return lax.dynamic_slice_in_dim(array, tp_index * own, own, 0)

    own_tokens = my_rows(tokens).astype(f32)
    normed_first = (own_tokens * norm_scale(own_tokens)).astype(bf16)
    gain_rows = gain_attention.astype(f32)
    attn_gain_own = gain_rows[:, None]
    query_part, key_part, value_part = (
        (w.astype(f32) * attn_gain_own).astype(bf16).reshape(block, heads_z, head)
        for w in (w_query, w_key, w_value)
    )
    out_part = w_out.reshape(heads_z, head, block).transpose(2, 0, 1)
    attn_parts = jnp.concatenate([query_part, key_part, value_part, out_part], axis=2)
    half_dim = head // 2
    side = x_index * half_dim
    bias_row = jnp.zeros((3, head), bf16)
    bias_row = lax.dynamic_update_slice(
        bias_row, jnp.stack([b_query, b_key, b_value]), (jnp.zeros_like(side), side)
    )
    small = flat([gain_experts, w_router.T, w_shared_gate])
    small = jnp.pad(small, (0, 15 * 4 * head - small.shape[0])).reshape(15, 4 * head)
    small = jnp.concatenate([jnp.pad(bias_row.reshape(1, 3 * head), ((0, 0), (0, head))), small])
    attn_parts = jnp.concatenate(
        [
            attn_parts.transpose(1, 0, 2),
            jnp.broadcast_to(small[None], (heads_z, 16, 4 * head)),
        ],
        axis=1,
    )
    first_half, arrived_weights = front(normed_first, attn_parts)
    small = arrived_weights[:, :, block + 1 :].reshape(exp_count, 15 * 4 * head)

    own_first = exp_index * rows + tp_index * own
    own_positions = own_first + jnp.arange(own, dtype=jnp.int32)
    valid = (own_positions < length).astype(f32)[:, None]
    grad_out_low = (my_rows(cotangent).astype(f32) * valid).astype(bf16)
    own_routes = my_rows(routes)
    leaving = jnp.concatenate(
        [grad_out_low, jnp.pad(own_routes.astype(bf16), ((0, 0), (0, 124)), constant_values=-1.0)],
        axis=1,
    )
    shared_parts = jnp.concatenate(
        [
            w.reshape(exp_count, shared_units, block)
            for w in (shared_gate.T, shared_up.T, shared_down)
        ],
        axis=1,
    )
    place = 0
    ffn_gain = small[:, place : place + block].reshape(model).astype(f32)
    place += block
    router_rows = (
        small[:, place : place + block * experts]
        .reshape(exp_count, experts, block)
        .transpose(1, 0, 2)
        .reshape(experts, model)
    )
    place += block * experts
    share_vector = small[:, place : place + block].reshape(model)

    frequency = np.tile(ROPE_BASE ** (-np.arange(half_dim) * 2.0 / head), 2)
    row_angle = np.arange(own)[:, None] * frequency
    starts = (
        np.arange(2)[:, None, None, None] * rows
        + np.arange(2)[None, :, None, None] * own
        + np.arange(2)[None, None, :, None] * 2 * own
        + np.arange(heads_z)[None, None, None, :] * 2 * rows
    )
    block_angle = starts.reshape(2, -1, 1) * frequency
    row_table = np.stack([np.cos(row_angle), np.sin(row_angle)]).astype(np.float32)
    block_table = np.stack([np.cos(block_angle), np.sin(block_angle)], axis=1).astype(np.float32)
    row_cos, row_sin = jnp.asarray(row_table[:, None, :, :half_dim])
    block_both = lax.dynamic_index_in_dim(jnp.asarray(block_table), x_index, 0, keepdims=False)
    block_cos, block_sin = block_both[:, :, None, :half_dim]
    cosine = (block_cos * row_cos - block_sin * row_sin).reshape(heads_z * rows, half_dim)
    sine = (block_sin * row_cos + block_cos * row_sin).reshape(heads_z * rows, half_dim)

    def rope_back(values):
        one, two = values[:, :half_dim], values[:, half_dim:]
        return jnp.concatenate([one * cosine + two * sine, two * cosine - one * sine], axis=1)

    def by_position(array):
        return (
            array.reshape((2, 2, heads_z, own) + array.shape[1:])
            .transpose(2, 1, 0, 3, 4)
            .reshape(array.shape)
        )

    def by_owner(array):
        return (
            array.reshape((heads_z, 2, 2, own) + array.shape[1:])
            .transpose(2, 1, 0, 3, 4)
            .reshape(array.shape)
        )

    flip = [(0, 1), (1, 0)]
    query_rot, key_values, attended, log_total, attn_part, attn_weights, grad_all, shared_parts = (
        middle(
            lengths,
            first_half,
            arrived_weights,
            jnp.asarray(row_table),
            jnp.asarray(block_table),
            leaving,
            shared_parts,
            rows,
        )
    )
    info = jnp.stack([x_index, length]).astype(jnp.int32)
    attended_low = by_owner(attended.astype(bf16))
    out_weight = attn_weights[:, 3 * head :]

    width = local_experts * units + shared_units + experts
    router_pair = jnp.stack(
        [router_rows, jnp.pad(share_vector[None, :], ((0, experts - 1), (0, 0)))]
    )
    unit = jnp.arange(width, dtype=jnp.int32)
    segment = jnp.where(
        unit < local_experts * units, exp_index * local_experts + unit // units, experts
    )
    segments = (
        (segment[:, None] == jnp.arange(128, dtype=jnp.int32)[None, :])
        & (unit < width - experts)[:, None]
    ).astype(bf16)
    normed_all, scaled_all, slope_all, mixed_sum, hidden_state, normed = stream(
        attn_part,
        my_rows(tokens),
        ffn_gain[None, :],
        grad_all,
        expert_gate.transpose(0, 2, 1).reshape(local_experts * units, model),
        expert_up.transpose(0, 2, 1).reshape(local_experts * units, model),
        expert_down.reshape(local_experts * units, model),
        shared_parts,
        router_pair,
        segments,
        units,
        experts,
        chunks,
    )
    inverse_second = norm_scale(hidden_state)
    d_expert_gate, d_expert_up, d_expert_down, d_shared = weight_grads(
        normed_all, grad_all, slope_all, scaled_all, units, shared_units, exp_count
    )

    output = valid * (hidden_state + mixed_sum[:, :model])
    mixed = lax.all_gather(output.astype(bf16), COLUMN_AXES, axis=0, tiled=True)

    router_probs = jax.nn.softmax(product_bt(normed, router_rows), axis=1)
    share_weight = jax.nn.sigmoid(product(normed, share_vector))
    chosen = jnp.sum(
        (own_routes[:, :, None] == jnp.arange(experts, dtype=jnp.int32)[None, None, :]).astype(f32),
        axis=1,
    )
    grad_router_probs = chosen * mixed_sum[:, 2 * model : 2 * model + experts]
    grad_share_weight = mixed_sum[:, 2 * model + experts]
    grad_logits = (
        router_probs
        * (grad_router_probs - jnp.sum(grad_router_probs * router_probs, axis=1, keepdims=True))
    ).astype(bf16)
    grad_share_logit = (grad_share_weight * share_weight * (1.0 - share_weight)).astype(bf16)
    grad_normed = (
        mixed_sum[:, model : 2 * model]
        + product(grad_logits, router_rows)
        + grad_share_logit.astype(f32)[:, None] * share_vector.astype(f32)[None, :]
    )
    norm_rows, d_gain_experts = norm_back(grad_normed, hidden_state, inverse_second, ffn_gain)
    grad_hidden = grad_out_low.astype(f32) + norm_rows
    hidden_half = lax.all_gather(grad_hidden.astype(bf16), SAME_X, axis=0, tiled=True)
    router_grads = product_at(
        jnp.concatenate([grad_logits, grad_share_logit[:, None]], axis=1), normed
    )
    extras = jnp.concatenate(
        [
            router_grads,
            d_gain_experts[None, :],
            jnp.broadcast_to(jnp.sum(output * output), (1, model)),
            jnp.zeros((5, model), f32),
        ]
    )
    extras = extras.reshape(-1, heads_z, 2, block).transpose(2, 1, 0, 3)
    hidden_half, d_shared = lax.optimization_barrier((hidden_half, d_shared))
    arrived = lax.all_to_all(d_shared, ROW_AXES, 0, 0, tiled=True).astype(f32)
    d_shared_gate, d_shared_up, d_shared_down = (
        arrived[:, k * shared_units : (k + 1) * shared_units].reshape(
            exp_count * shared_units, block
        )
        for k in range(3)
    )
    d_shared_gate, d_shared_up = d_shared_gate.T, d_shared_up.T
    grad_attended = product(hidden_half, out_weight).astype(bf16)
    d_out_weight = product_at(attended_low, hidden_half)
    scale = 1.0 / head**0.5
    grad_query, grad_key, grad_value = attend_back(
        info, query_rot, key_values, by_position(grad_attended), attended, log_total, rows
    )
    grad_kv = jnp.concatenate([grad_key, grad_value], axis=2).astype(bf16)
    away = lax.ppermute(grad_kv[1], "x", flip)
    grad_kv = by_owner(
        jnp.concatenate([grad_key[0], grad_value[0]], axis=1) + away.astype(f32)
    )
    grad_qkv = jnp.concatenate(
        [
            rope_back(by_owner(grad_query)) * scale,
            rope_back(grad_kv[:, :head]) * scale,
            grad_kv[:, head:],
        ],
        axis=1,
    ).astype(bf16)
    d_attn = jnp.concatenate([product_at(grad_qkv, first_half), d_out_weight]).astype(bf16)
    d_biases = jnp.sum(grad_qkv.astype(f32), axis=0).astype(bf16).reshape(3, 2, head // 2)
    d_biases = jnp.pad(
        d_biases.transpose(1, 0, 2).reshape(2, 1, 3 * head // 2),
        ((0, 0), (0, 15), (0, 4 * head - 3 * head // 2)),
    )
    raw = jnp.concatenate(
        [w.reshape(block, heads_z, head) for w in (w_query, w_key, w_value)], axis=2
    ).transpose(1, 0, 2)
    grad_tokens, d_query, d_key, d_value, d_out, d_bias_row, d_gain_attention, squares, extras = finish(
        product_bt(grad_qkv, attn_weights[:, : 3 * head]).astype(bf16),
        grad_hidden,
        my_rows(tokens),
        d_attn.reshape(4 * head, heads_z, 2, block).transpose(2, 1, 3, 0),
        d_biases,
        raw,
        extras,
        attn_gain_own,
        chunks,
    )
    d_bias_row = d_bias_row[0]
    d_gain_attention = jnp.sum(d_gain_attention, axis=1)
    half_head = head // 2

    d_router, d_share_vector = extras[:experts].T, extras[experts]
    d_gain_experts = extras[experts + 1]
    cells = length.astype(f32) * model
    rms_output = jnp.sqrt(extras[experts + 2, 0] / cells)
    rms_grad = jnp.sqrt(jnp.sum(squares) / cells)
    return (
        mixed,
        grad_tokens,
        d_query,
        d_key,
        d_value,
        d_out,
        d_bias_row[:half_head],
        d_bias_row[half_head : 2 * half_head],
        d_bias_row[2 * half_head : 3 * half_head],
        d_gain_attention,
        d_gain_experts,
        d_router,
        d_share_vector,
        d_shared_gate,
        d_shared_up,
        d_shared_down,
        d_expert_gate.transpose(0, 2, 1),
        d_expert_up.transpose(0, 2, 1),
        d_expert_down,
        rms_output,
        rms_grad,
    )


def specs(row, column):
    both = column + row
    ins = (
        P(row, None),
        P(row, None),
        P(),
        P(row, None),
        P(row, column),
        P(row, column),
        P(row, column),
        P(column, row),
        P(both),
        P(both),
        P(both),
        P(row),
        P(row),
        P(row, None),
        P(row),
        P(row, column),
        P(row, column),
        P(column, row),
        P(row, None, column),
        P(row, None, column),
        P(row, column, None),
    )
    outs = (
        P(row, None),
        P(row, None),
        P(row, column),
        P(row, column),
        P(row, column),
        P(column, row),
        P(both),
        P(both),
        P(both),
        P(row),
        P(row),
        P(row, None),
        P(row),
        P(row, column),
        P(row, column),
        P(column, row),
        P(row, None, column),
        P(row, None, column),
        P(row, column, None),
        P(),
        P(),
    )
    return ins, outs


def solution(mesh):
    if (mesh.shape["exp"], mesh.shape["tp"]) == (8, 4):
        body, row, column = packed, ROW_AXES, COLUMN_AXES
        mesh = Mesh(mesh.devices.reshape(4, 2, 2, 2), ALL_AXES)
    else:
        body, row, column = general, ("exp",), ("tp",)
    ins, outs = specs(row, column)
    return jax.shard_map(body, mesh=mesh, in_specs=ins, out_specs=outs, check_vma=False)
```

```python
import functools

import jax
import jax.numpy as jnp
import numpy as np
from jax import lax
from jax.experimental import pallas as pl
from jax.experimental.pallas import tpu as pltpu
from jax.sharding import Mesh
from jax.sharding import PartitionSpec as P

HEAD_DIM = 128
SLOT = 4096


EPSILON = 1e-06
ROPE_BASE = 1000000.0
MASKED = -1e30


def shifted(shard, axis, by):
    length = lax.axis_size(axis)
    pairs = [(i, i + by) for i in range(length) if 0 <= i + by < length]
    return lax.ppermute(shard, axis, pairs)


def rope_tables(positions, head_dim):
    half_dim = head_dim // 2
    frequency = ROPE_BASE ** (-(jnp.arange(half_dim, dtype=jnp.float32) * 2.0) / head_dim)
    angles = positions.astype(jnp.float32)[:, None] * frequency[None, :]
    cosine = jnp.concatenate([jnp.cos(angles), jnp.cos(angles)], axis=1)
    sine_table = jnp.concatenate([jnp.sin(angles), jnp.sin(angles)], axis=1)
    return (cosine, sine_table)


def rotate(values, cosine, sine_table):
    half_dim = values.shape[-1] // 2
    turned = jnp.concatenate([-values[..., half_dim:], values[..., :half_dim]], axis=-1)
    return values * cosine[:, None, :] + turned * sine_table[:, None, :]


def rotate_back(grads, cosine, sine_table):
    half_dim = grads.shape[-1] // 2
    moved = grads * sine_table[:, None, :]
    return grads * cosine[:, None, :] + jnp.concatenate(
        [moved[..., half_dim:], -moved[..., :half_dim]], axis=-1
    )


def product(left, right):
    return jnp.dot(left, right, preferred_element_type=jnp.float32)


def product_bt(left, right):
    return lax.dot_general(
        left, right, (((1,), (1,)), ((), ())), preferred_element_type=jnp.float32
    )


def product_at(left, right):
    return lax.dot_general(
        left, right, (((0,), (0,)), ((), ())), preferred_element_type=jnp.float32
    )


def norm_scale(values):
    return lax.rsqrt(jnp.mean(values * values, axis=1, keepdims=True) + EPSILON)


def norm_back(grad_normed, values, inverse, gain):
    scaled = values * inverse
    pushed = grad_normed * gain
    back_rows = inverse * (pushed - scaled * jnp.mean(pushed * scaled, axis=1, keepdims=True))
    return (back_rows, jnp.sum(grad_normed * scaled, axis=0))


def silu_grad(values):
    sigma = jax.nn.sigmoid(values)
    return sigma * (1.0 + values * (1.0 - sigma))


def general(
    tokens,
    cotangent,
    lengths,
    routes,
    w_query,
    w_key,
    w_value,
    w_out,
    b_query,
    b_key,
    b_value,
    gain_attention,
    gain_experts,
    w_router,
    w_shared_gate,
    shared_gate,
    shared_up,
    shared_down,
    expert_gate,
    expert_up,
    expert_down,
):
    exp_count = lax.axis_size("exp")
    exp_index = lax.axis_index("exp")
    tp_count = lax.axis_size("tp")
    tp_index = lax.axis_index("tp")
    row_count, model_width = tokens.shape
    local_experts = expert_gate.shape[0]
    expert_count = local_experts * exp_count
    top_count = routes.shape[1]
    capacity = 2 * row_count * top_count // expert_count
    quarter = capacity // tp_count
    head_dim = HEAD_DIM
    heads_here = w_query.shape[1] // head_dim
    group_size = SLOT // row_count
    scale = 1.0 / head_dim**0.5

    def own_slots(whole_rows):
        return lax.dynamic_slice_in_dim(whole_rows, tp_index * quarter, quarter, 2)

    def place_slots(part_rows):
        empty_rows = jnp.zeros((exp_count, local_experts, capacity, model_width), part_rows.dtype)
        return lax.dynamic_update_slice_in_dim(empty_rows, part_rows, tp_index * quarter, 2)

    gathered = (
        lax.all_gather(w_query, "exp", axis=0, tiled=True),
        lax.all_gather(w_key, "exp", axis=0, tiled=True),
        lax.all_gather(w_value, "exp", axis=0, tiled=True),
        lax.all_gather(w_out, "exp", axis=1, tiled=True),
        lax.all_gather(b_query, "exp", axis=0, tiled=True),
        lax.all_gather(b_key, "exp", axis=0, tiled=True),
        lax.all_gather(b_value, "exp", axis=0, tiled=True),
        lax.all_gather(gain_attention, "exp", axis=0, tiled=True),
        lax.all_gather(gain_experts, "exp", axis=0, tiled=True),
        lax.all_gather(w_router, "exp", axis=0, tiled=True),
        lax.all_gather(w_shared_gate, "exp", axis=0, tiled=True),
        lax.all_gather(shared_gate, "exp", axis=0, tiled=True),
        lax.all_gather(shared_up, "exp", axis=0, tiled=True),
        lax.all_gather(shared_down, "exp", axis=1, tiled=True),
    )
    (
        query_full,
        key_full,
        value_full,
        out_full,
        query_bias,
        key_bias,
        value_bias,
        attn_gain,
        ffn_gain,
        router_full,
        share_vector,
        share_gate_full,
        share_up_full,
        share_down_full,
    ) = gathered
    attn_gain = attn_gain.astype(jnp.float32)
    ffn_gain = ffn_gain.astype(jnp.float32)
    first_row = exp_index * row_count
    slot_index = first_row // SLOT
    offset = first_row % SLOT
    positions = offset + jnp.arange(row_count, dtype=jnp.int32)
    length = jnp.sum(
        jnp.where(jnp.arange(lengths.shape[0], dtype=jnp.int32) == slot_index, lengths, 0)
    )
    valid_rows = (positions < length).astype(jnp.float32)
    cosine, sine_table = rope_tables(positions, head_dim)
    input_rows = tokens.astype(jnp.float32)
    inverse_first = norm_scale(input_rows)
    normed_first = (input_rows * inverse_first * attn_gain).astype(jnp.bfloat16)
    query_lin = product(normed_first, query_full) + query_bias.astype(jnp.float32)
    key_lin = product(normed_first, key_full) + key_bias.astype(jnp.float32)
    value_lin = product(normed_first, value_full) + value_bias.astype(jnp.float32)
    query_rot = rotate(
        query_lin.reshape(row_count, heads_here, head_dim), cosine, sine_table
    ).astype(jnp.bfloat16)
    key_rot = rotate(key_lin.reshape(row_count, heads_here, head_dim), cosine, sine_table).astype(
        jnp.bfloat16
    )
    value_low = value_lin.reshape(row_count, heads_here, head_dim).astype(jnp.bfloat16)
    key_list = [key_rot]
    value_list = [value_low]
    for distance in range(1, group_size):
        earlier_keys, earlier_values = shifted((key_rot, value_low), "exp", distance)
        key_list.append(earlier_keys)
        value_list.append(earlier_values)
    all_keys = jnp.concatenate(key_list, axis=0)
    all_values = jnp.concatenate(value_list, axis=0)
    key_index = jnp.arange(group_size * row_count, dtype=jnp.int32)
    key_pos = offset - key_index // row_count * row_count + key_index % row_count
    allowed = (
        (key_pos[None, :] >= 0)
        & (key_pos[None, :] <= positions[:, None])
        & (key_pos[None, :] < length)
    )
    scores = (
        jnp.einsum("qhd,khd->hqk", query_rot, all_keys, preferred_element_type=jnp.float32) * scale
    )
    scores = jnp.where(allowed[None, :, :], scores, MASKED)
    peak_score = jnp.max(scores, axis=2, keepdims=True)
    weights = jnp.exp(scores - peak_score)
    total_weight = jnp.sum(weights, axis=2, keepdims=True)
    log_total = peak_score + jnp.log(total_weight)
    attn_probs = (weights / total_weight).astype(jnp.bfloat16)
    attended = jnp.einsum(
        "hqk,khd->qhd", attn_probs, all_values, preferred_element_type=jnp.float32
    )
    attended = attended.reshape(row_count, heads_here * head_dim).astype(jnp.bfloat16)
    attn_sum = lax.psum(product(attended, out_full).astype(jnp.bfloat16), "tp").astype(jnp.float32)
    hidden_state = input_rows + attn_sum
    inverse_second = norm_scale(hidden_state)
    normed = (hidden_state * inverse_second * ffn_gain).astype(jnp.bfloat16)
    logits = product(normed, router_full)
    router_probs = jax.nn.softmax(logits, axis=1)
    chosen = (
        routes[:, :, None] == jnp.arange(expert_count, dtype=jnp.int32)[None, None, :]
    ).astype(jnp.float32)
    gates = jnp.sum(chosen * router_probs[:, None, :], axis=2)
    share_weight = jax.nn.sigmoid(product(normed, share_vector))
    share_pre = product(normed, share_gate_full)
    share_lin = product(normed, share_up_full)
    share_hidden = (jax.nn.silu(share_pre) * share_lin).astype(jnp.bfloat16)
    share_out = product(share_hidden, share_down_full)
    flat_routes = routes.reshape(-1)
    pair_count = row_count * top_count
    pick_table = (
        flat_routes[:, None] == jnp.arange(expert_count, dtype=jnp.int32)[None, :]
    ).astype(jnp.int32)
    rank_in_expert = jnp.sum((jnp.cumsum(pick_table, axis=0) - 1) * pick_table, axis=1)
    target = flat_routes * capacity + rank_in_expert
    slot_pair = (
        jnp.full((expert_count * capacity,), pair_count, jnp.int32)
        .at[target]
        .set(jnp.arange(pair_count, dtype=jnp.int32))
    )
    slot_token = jnp.where(slot_pair < pair_count, slot_pair // top_count, row_count)
    padded_rows = jnp.concatenate([normed, jnp.zeros((1, model_width), jnp.bfloat16)], axis=0)
    outgoing = padded_rows[slot_token].reshape(exp_count, local_experts, capacity, model_width)
    sending = own_slots(outgoing)
    working = lax.all_gather(
        lax.all_to_all(sending, "exp", split_axis=0, concat_axis=0, tiled=True),
        "tp",
        axis=2,
        tiled=True,
    )
    gate_pre = jnp.einsum(
        "sxcd,xdf->sxcf", working, expert_gate, preferred_element_type=jnp.float32
    )
    up_pre = jnp.einsum("sxcd,xdf->sxcf", working, expert_up, preferred_element_type=jnp.float32)
    inner = (jax.nn.silu(gate_pre) * up_pre).astype(jnp.bfloat16)
    result_rows = jnp.einsum(
        "sxcf,xfd->sxcd", inner, expert_down, preferred_element_type=jnp.float32
    )
    result_rows = lax.psum_scatter(
        result_rows.astype(jnp.bfloat16), "tp", scatter_dimension=2, tiled=True
    ).astype(jnp.float32)
    back_rows = lax.all_to_all(
        result_rows.astype(jnp.bfloat16), "exp", split_axis=0, concat_axis=0, tiled=True
    ).astype(result_rows.dtype)
    returned = back_rows
    returned = place_slots(returned)
    expert_rows = returned.reshape(expert_count * capacity, model_width)[target].reshape(
        row_count, top_count, model_width
    )
    mixture = jnp.einsum("tk,tkd->td", gates, expert_rows) + share_weight[:, None] * share_out
    mixture = lax.psum(mixture.astype(jnp.bfloat16), "tp").astype(jnp.float32)
    output = valid_rows[:, None] * (hidden_state + mixture)
    grad_out = cotangent.astype(jnp.float32) * valid_rows[:, None]
    share_grad = (grad_out * share_weight[:, None]).astype(jnp.bfloat16)
    grad_share_hidden = (
        product_bt(share_grad, share_down_full).astype(jnp.bfloat16).astype(jnp.float32)
    )
    grad_share_pre = (grad_share_hidden * share_lin * silu_grad(share_pre)).astype(jnp.bfloat16)
    grad_share_lin = (grad_share_hidden * jax.nn.silu(share_pre)).astype(jnp.bfloat16)
    d_shared_down = product_at(share_hidden, share_grad)
    d_shared_gate = product_at(normed, grad_share_pre)
    d_shared_up = product_at(normed, grad_share_lin)
    back_normed = product_bt(grad_share_pre, share_gate_full) + product_bt(
        grad_share_lin, share_up_full
    )
    gate_part = jnp.einsum("td,tkd->tk", grad_out, expert_rows)
    share_part = jnp.sum(grad_out * share_out, axis=1)
    pair_grads = (
        (grad_out[:, None, :] * gates[:, :, None])
        .astype(jnp.bfloat16)
        .reshape(pair_count, model_width)
    )
    padded_grads = jnp.concatenate([pair_grads, jnp.zeros((1, model_width), jnp.bfloat16)], axis=0)
    outgoing_grads = padded_grads[slot_pair].reshape(
        exp_count, local_experts, capacity, model_width
    )
    sending_grads = own_slots(outgoing_grads)
    arrived_grads, arrived_rows = (
        lax.all_to_all(sending_grads, "exp", split_axis=0, concat_axis=0, tiled=True),
        lax.all_to_all(sending, "exp", split_axis=0, concat_axis=0, tiled=True),
    )
    arrived_grads, arrived_rows = (
        lax.all_gather(arrived_grads, "tp", axis=2, tiled=True),
        lax.all_gather(arrived_rows, "tp", axis=2, tiled=True),
    )
    gate_pre = jnp.einsum(
        "sxcd,xdf->sxcf", arrived_rows, expert_gate, preferred_element_type=jnp.float32
    )
    up_pre = jnp.einsum(
        "sxcd,xdf->sxcf", arrived_rows, expert_up, preferred_element_type=jnp.float32
    )
    inner = (jax.nn.silu(gate_pre) * up_pre).astype(jnp.bfloat16)
    grad_inner = jnp.einsum(
        "sxcd,xfd->sxcf", arrived_grads, expert_down, preferred_element_type=jnp.float32
    )
    grad_inner = grad_inner.astype(jnp.bfloat16).astype(jnp.float32)
    grad_gate_pre = (grad_inner * up_pre * silu_grad(gate_pre)).astype(jnp.bfloat16)
    grad_up_pre = (grad_inner * jax.nn.silu(gate_pre)).astype(jnp.bfloat16)
    rows_back = jnp.einsum(
        "sxcf,xdf->sxcd", grad_gate_pre, expert_gate, preferred_element_type=jnp.float32
    )
    rows_back = rows_back + jnp.einsum(
        "sxcf,xdf->sxcd", grad_up_pre, expert_up, preferred_element_type=jnp.float32
    )
    rows_back = lax.psum_scatter(
        rows_back.astype(jnp.bfloat16), "tp", scatter_dimension=2, tiled=True
    ).astype(jnp.float32)
    returned_grads = lax.all_to_all(
        rows_back.astype(jnp.bfloat16), "exp", split_axis=0, concat_axis=0, tiled=True
    ).astype(rows_back.dtype)
    returned_grads = place_slots(returned_grads)
    d_expert_gate = jnp.einsum(
        "sxcd,sxcf->xdf", arrived_rows, grad_gate_pre, preferred_element_type=jnp.float32
    )
    d_expert_up = jnp.einsum(
        "sxcd,sxcf->xdf", arrived_rows, grad_up_pre, preferred_element_type=jnp.float32
    )
    d_expert_down = jnp.einsum(
        "sxcf,sxcd->xfd", inner, arrived_grads, preferred_element_type=jnp.float32
    )
    grad_rows = returned_grads.reshape(expert_count * capacity, model_width)[target].reshape(
        row_count, top_count, model_width
    )
    back_normed = back_normed + jnp.sum(grad_rows, axis=1)
    scalar_part = jnp.concatenate([gate_part, share_part[:, None]], axis=1)
    summed_normed, scalar_sum = (
        lax.psum(back_normed.astype(jnp.bfloat16), "tp").astype(jnp.float32),
        lax.psum(scalar_part.astype(jnp.bfloat16), "tp").astype(jnp.float32),
    )
    grad_gates = scalar_sum[:, :top_count]
    grad_share_weight = scalar_sum[:, top_count]
    grad_router_probs = jnp.einsum("tk,tke->te", grad_gates, chosen)
    grad_logits = (
        router_probs
        * (grad_router_probs - jnp.sum(grad_router_probs * router_probs, axis=1, keepdims=True))
    ).astype(jnp.bfloat16)
    grad_share_logit = (grad_share_weight * share_weight * (1.0 - share_weight)).astype(
        jnp.bfloat16
    )
    d_router = product_at(normed, grad_logits)
    d_share_vector = product(grad_share_logit, normed)
    grad_normed = (
        summed_normed
        + product_bt(grad_logits, router_full)
        + grad_share_logit.astype(jnp.float32)[:, None] * share_vector.astype(jnp.float32)[None, :]
    )
    norm_rows, d_gain_experts = norm_back(grad_normed, hidden_state, inverse_second, ffn_gain)
    grad_hidden = grad_out + norm_rows
    grad_hidden_low = grad_hidden.astype(jnp.bfloat16)
    d_out_weight = product_at(attended, grad_hidden_low)
    grad_attended = (
        product_bt(grad_hidden_low, out_full)
        .astype(jnp.bfloat16)
        .reshape(row_count, heads_here, head_dim)
    )
    scores = (
        jnp.einsum("qhd,khd->hqk", query_rot, all_keys, preferred_element_type=jnp.float32) * scale
    )
    scores = jnp.where(allowed[None, :, :], scores, MASKED)
    probs_again = jnp.exp(scores - log_total)
    probs_low = probs_again.astype(jnp.bfloat16)
    grad_values = jnp.einsum(
        "hqk,qhd->khd", probs_low, grad_attended, preferred_element_type=jnp.float32
    )
    grad_probs = jnp.einsum(
        "qhd,khd->hqk", grad_attended, all_values, preferred_element_type=jnp.float32
    )
    grad_scores = (
        probs_again * (grad_probs - jnp.sum(probs_again * grad_probs, axis=2, keepdims=True))
    ).astype(jnp.bfloat16)
    grad_query = (
        jnp.einsum("hqk,khd->qhd", grad_scores, all_keys, preferred_element_type=jnp.float32)
        * scale
    )
    grad_keys = (
        jnp.einsum("hqk,qhd->khd", grad_scores, query_rot, preferred_element_type=jnp.float32)
        * scale
    )
    own_key_grads = grad_keys[:row_count]
    own_value_grads = grad_values[:row_count]
    for distance in range(1, group_size):
        lower_row = distance * row_count
        later_keys, later_values = (
            shifted(
                grad_keys[lower_row : lower_row + row_count].astype(jnp.bfloat16), "exp", -distance
            ).astype(jnp.float32),
            shifted(
                grad_values[lower_row : lower_row + row_count].astype(jnp.bfloat16),
                "exp",
                -distance,
            ).astype(jnp.float32),
        )
        own_key_grads = own_key_grads + later_keys
        own_value_grads = own_value_grads + later_values
    grad_query_lin = (
        rotate_back(grad_query, cosine, sine_table)
        .reshape(row_count, heads_here * head_dim)
        .astype(jnp.bfloat16)
    )
    grad_key_lin = (
        rotate_back(own_key_grads, cosine, sine_table)
        .reshape(row_count, heads_here * head_dim)
        .astype(jnp.bfloat16)
    )
    grad_value_lin = own_value_grads.reshape(row_count, heads_here * head_dim).astype(jnp.bfloat16)
    d_query = product_at(normed_first, grad_query_lin)
    d_key = product_at(normed_first, grad_key_lin)
    d_value = product_at(normed_first, grad_value_lin)
    d_query_bias = jnp.sum(grad_query_lin.astype(jnp.float32), axis=0)
    d_key_bias = jnp.sum(grad_key_lin.astype(jnp.float32), axis=0)
    d_value_bias = jnp.sum(grad_value_lin.astype(jnp.float32), axis=0)
    back_first = (
        product_bt(grad_query_lin, query_full)
        + product_bt(grad_key_lin, key_full)
        + product_bt(grad_value_lin, value_full)
    )
    back_first = lax.psum(back_first.astype(jnp.bfloat16), "tp").astype(jnp.float32)
    first_rows, d_gain_attention = norm_back(back_first, input_rows, inverse_first, attn_gain)
    grad_input = grad_hidden + first_rows
    reduced = (
        lax.psum_scatter(
            d_query.astype(jnp.bfloat16), "exp", scatter_dimension=0, tiled=True
        ).astype(jnp.float32),
        lax.psum_scatter(d_key.astype(jnp.bfloat16), "exp", scatter_dimension=0, tiled=True).astype(
            jnp.float32
        ),
        lax.psum_scatter(
            d_value.astype(jnp.bfloat16), "exp", scatter_dimension=0, tiled=True
        ).astype(jnp.float32),
        lax.psum_scatter(
            d_out_weight.astype(jnp.bfloat16), "exp", scatter_dimension=1, tiled=True
        ).astype(jnp.float32),
        lax.psum_scatter(
            d_query_bias.astype(jnp.bfloat16), "exp", scatter_dimension=0, tiled=True
        ).astype(jnp.float32),
        lax.psum_scatter(
            d_key_bias.astype(jnp.bfloat16), "exp", scatter_dimension=0, tiled=True
        ).astype(jnp.float32),
        lax.psum_scatter(
            d_value_bias.astype(jnp.bfloat16), "exp", scatter_dimension=0, tiled=True
        ).astype(jnp.float32),
        lax.psum_scatter(
            d_gain_attention.astype(jnp.bfloat16), "exp", scatter_dimension=0, tiled=True
        ).astype(jnp.float32),
        lax.psum_scatter(
            d_gain_experts.astype(jnp.bfloat16), "exp", scatter_dimension=0, tiled=True
        ).astype(jnp.float32),
        lax.psum_scatter(
            d_router.astype(jnp.bfloat16), "exp", scatter_dimension=0, tiled=True
        ).astype(jnp.float32),
        lax.psum_scatter(
            d_share_vector.astype(jnp.bfloat16), "exp", scatter_dimension=0, tiled=True
        ).astype(jnp.float32),
        lax.psum_scatter(
            d_shared_gate.astype(jnp.bfloat16), "exp", scatter_dimension=0, tiled=True
        ).astype(jnp.float32),
        lax.psum_scatter(
            d_shared_up.astype(jnp.bfloat16), "exp", scatter_dimension=0, tiled=True
        ).astype(jnp.float32),
        lax.psum_scatter(
            d_shared_down.astype(jnp.bfloat16), "exp", scatter_dimension=1, tiled=True
        ).astype(jnp.float32),
    )
    square_sums = lax.psum((jnp.sum(output * output), jnp.sum(grad_input * grad_input)), "exp")
    count_cells = jnp.sum(lengths).astype(jnp.float32) * model_width
    rms_output = jnp.sqrt(square_sums[0] / count_cells)
    rms_grad = jnp.sqrt(square_sums[1] / count_cells)
    return (
        output.astype(jnp.bfloat16),
        grad_input.astype(jnp.bfloat16),
        reduced[0],
        reduced[1],
        reduced[2],
        reduced[3],
        reduced[4],
        reduced[5],
        reduced[6],
        reduced[7],
        reduced[8],
        reduced[9],
        reduced[10],
        reduced[11],
        reduced[12],
        reduced[13],
        d_expert_gate,
        d_expert_up,
        d_expert_down,
        rms_output,
        rms_grad,
    )


def flat(pieces):
    return jnp.concatenate([p.reshape(-1) for p in pieces])


def key_window(info_ref, block, keys):
    return lax.rem(block + info_ref[0], 2), pl.ds(pl.multiple_of(block // 2 * keys, keys), keys)


def attend_back_kernel(
    info_ref, q_ref, kv_ref, do_ref, o_ref, lse_ref, dq_ref, dk_ref, dv_ref, *, tile, keys, rows
):
    step = pl.program_id(0)
    per_block = rows // tile
    base = (2 * (step // per_block) + info_ref[0]) * rows + (step % per_block) * tile

    @pl.when(step == 0)
    def _():
        dk_ref[...] = jnp.zeros_like(dk_ref)
        dv_ref[...] = jnp.zeros_like(dv_ref)

    query = q_ref[...]
    grad = do_ref[...]
    log_total = lse_ref[:, 0:1]
    delta = jnp.sum(grad.astype(jnp.float32) * o_ref[...], axis=1, keepdims=True)
    row_pos = base + lax.broadcasted_iota(jnp.int32, (tile, 1), 0)
    limit = jnp.minimum(row_pos, info_ref[1] - 1)
    column = lax.broadcasted_iota(jnp.int32, (tile, keys), 1)

    def body(j, acc):
        side, window = key_window(info_ref, j, keys)
        key = kv_ref[side, window, :HEAD_DIM]
        scores = product_bt(query, key) * (1.0 / HEAD_DIM**0.5)
        scores = jnp.where(column <= limit - j * keys, scores, MASKED)
        probs = jnp.exp(scores - log_total)
        dv_ref[side, window, :] += product_at(probs.astype(jnp.bfloat16), grad)
        grad_probs = product_bt(grad, kv_ref[side, window, HEAD_DIM:])
        grad_scores = (probs * (grad_probs - delta)).astype(jnp.bfloat16)
        dk_ref[side, window, :] += product_at(grad_scores, query)
        return acc + product(grad_scores, key)

    count = (base + tile + keys - 1) // keys
    dq_ref[...] = lax.fori_loop(0, count, body, jnp.zeros((tile, HEAD_DIM), jnp.float32))


def attend_back(info, query, key_values, grad, out, log_total, rows):
    count = query.shape[0]
    tile = 256
    half = key_values.shape[:2] + (HEAD_DIM,)
    whole = pl.BlockSpec(half, lambda i: (0, 0, 0))
    both = pl.BlockSpec(key_values.shape, lambda i: (0, 0, 0))
    part = pl.BlockSpec((tile, HEAD_DIM), lambda i: (i, 0))
    return pl.pallas_call(
        functools.partial(attend_back_kernel, tile=tile, keys=rows, rows=rows),
        grid=(count // tile,),
        in_specs=[pl.BlockSpec(memory_space=pltpu.SMEM), part, both, part, part, part],
        out_specs=[part, whole, whole],
        out_shape=[
            jax.ShapeDtypeStruct((count, HEAD_DIM), jnp.float32),
            jax.ShapeDtypeStruct(half, jnp.float32),
            jax.ShapeDtypeStruct(half, jnp.float32),
        ],
        compiler_params=pltpu.CompilerParams(vmem_limit_bytes=40 * 2**20),
        cost_estimate=pl.CostEstimate(
            flops=10 * count * count * HEAD_DIM,
            bytes_accessed=12 * 2**20,
            transcendentals=count * count,
        ),
    )(info, query, key_values, grad, out, log_total)


ROW_AXES = ("z", "x")
COLUMN_AXES = ("y", "c")
ALL_AXES = ("z", "x", "y", "c")
CHUNK_AXES = ("c", "y", "x", "z")
SAME_X = ("c", "y", "z")


def front_kernel(
    own_ref,
    parts_ref,
    leaving_ref,
    rows_ref,
    weights_ref,
    all_ref,
    send,
    send_z,
    recv,
    send_w,
    recv_w,
    send_g,
    recv_g,
    here,
):
    z, x, y, c = (lax.axis_index(name) for name in ALL_AXES)
    z_count = lax.axis_size("z")
    chunks = own_ref.shape[0]
    half = own_ref.shape[2] // 2
    left, right = pl.ds(0, half), pl.ds(half, leaving_ref.shape[2] - half)
    flip = {"x": {"x": 1 - x}, "y": {"y": 1 - y}, "c": {"c": 1 - c}}

    def up(distance):
        return {"z": lax.rem(z + distance, z_count)}

    def remote(src, dst, send_sem, recv_sem, device):
        return pltpu.make_async_remote_copy(
            src_ref=src,
            dst_ref=dst,
            send_sem=send_sem,
            recv_sem=recv_sem,
            device_id=device,
            device_id_type=pl.DeviceIdType.MESH,
        )

    def spread_z(k, d):
        block = rows_ref.at[c, y, z, k]
        return remote(own_ref.at[k], block, send_z.at[d - 1, k], recv.at[1 + d, k], up(d))

    def spread_y(k):
        block = rows_ref.at[c, y, :, k]
        return remote(block, block, send.at[0, k], recv.at[0, k], flip["y"])

    def spread_c(k):
        block = rows_ref.at[c, :, :, k]
        return remote(block, block, send.at[1, k], recv.at[1, k], flip["c"])

    def weights_z(d):
        there = lax.rem(z + d, z_count)
        return remote(
            parts_ref.at[there], weights_ref.at[z, x], send_w.at[d], recv_w.at[d], up(d)
        )

    def weights_x():
        block = weights_ref.at[:, x]
        return remote(block, block, send_w.at[0], recv_w.at[0], flip["x"])

    def grads(slot, k, src, dst, device):
        return remote(src, dst, send_g.at[slot, k], recv_g.at[slot, k], device)

    def grads_z(k):
        return [
            grads(4 + d, k, leaving_ref.at[k], all_ref.at[c, y, x, z, k], up(d))
            for d in range(1, 4)
        ]

    def grads_2(k):
        a = all_ref.at[c, y, x, :, k, :, left]
        b = all_ref.at[c, y, x, :, k, :, right]
        return grads(0, k, a, a, flip["x"]), grads(1, k, b, b, flip["y"])

    def grads_3(k):
        a = all_ref.at[c, y, :, :, k, :, left]
        b = all_ref.at[c, :, x, :, k, :, right]
        return grads(2, k, a, a, flip["y"]), grads(3, k, b, b, flip["x"])

    def grads_c(k):
        a = all_ref.at[c, :, :, :, k]
        return (grads(4, k, a, a, flip["c"]),)

    def start(copies):
        for copy in copies:
            copy.start()

    def finish(copies):
        for copy in copies:
            copy.wait()

    barrier = pltpu.get_barrier_semaphore()
    for device in (flip["x"], flip["y"], flip["c"], up(1), up(2), up(3)):
        pl.semaphore_signal(
            barrier, inc=1, device_id=device, device_id_type=pl.DeviceIdType.MESH
        )
    keep = [
        pltpu.make_async_copy(own_ref, rows_ref.at[c, y, z], here.at[0]),
        pltpu.make_async_copy(parts_ref.at[z], weights_ref.at[z, x], here.at[1]),
        pltpu.make_async_copy(leaving_ref, all_ref.at[c, y, x, z], here.at[2]),
    ]
    start(keep)
    pl.semaphore_wait(barrier, 6)
    def first_z(k):
        return [spread_z(k, d) for d in range(1, 4)]

    def all_weights_z():
        return [weights_z(d) for d in range(1, 4)]

    waiting = [first_z(k) for k in range(2, chunks)] + [grads_z(k) for k in range(chunks)]
    start(first_z(0))
    start(first_z(1))
    finish(keep)
    for k in range(chunks):
        finish(first_z(k))
        if k == 0:
            start(all_weights_z())
        start(waiting.pop(0))
        spread_y(k).start()
        if k == 2:
            finish(all_weights_z())
            weights_x().start()
        if k > 0:
            spread_y(k - 1).wait()
            spread_c(k - 1).start()
    for k in range(chunks):
        finish(grads_z(k))
        if waiting:
            start(waiting.pop(0))
        start(grads_2(k))
        if k == 0:
            spread_y(chunks - 1).wait()
            spread_c(chunks - 1).start()
        if k > 0:
            finish(grads_2(k - 1))
            start(grads_3(k - 1))
        if k > 1:
            finish(grads_3(k - 2))
            start(grads_c(k - 2))
    finish(grads_2(chunks - 1))
    start(grads_3(chunks - 1))
    for k in (chunks - 2, chunks - 1):
        finish(grads_3(k))
        start(grads_c(k))
    for k in range(chunks):
        spread_c(k).wait()
        finish(grads_c(k))
    weights_x().wait()


def front(rows, parts, leaving, chunks=4):
    own, model = rows.shape
    wide = leaving.shape[1]
    piece = own // chunks
    zs = lax.axis_size("z")
    anywhere = pl.BlockSpec(memory_space=pl.ANY)
    dma = pltpu.SemaphoreType.DMA
    gathered, weights, spread = pl.pallas_call(
        front_kernel,
        in_specs=[anywhere] * 3,
        out_specs=[anywhere] * 3,
        out_shape=[
            jax.ShapeDtypeStruct((2, 2, zs, chunks, piece, model), rows.dtype),
            jax.ShapeDtypeStruct((zs, 2) + parts.shape[1:], parts.dtype),
            jax.ShapeDtypeStruct((2, 2, 2, zs, chunks, piece, wide), rows.dtype),
        ],
        scratch_shapes=[
            dma((2, chunks)),
            dma((3, chunks)),
            dma((5, chunks)),
            dma((4,)),
            dma((4,)),
            dma((8, chunks)),
            dma((8, chunks)),
            dma((3,)),
        ],
        compiler_params=pltpu.CompilerParams(
            collective_id=0, has_side_effects=True, vmem_limit_bytes=16 * 2**20
        ),
    )(rows.reshape(chunks, piece, model), parts, leaving.reshape(chunks, piece, wide))
    return (
        gathered.reshape(4 * zs * own, model),
        weights,
        spread.reshape(8 * zs * own, wide),
    )


def middle_kernel(
    length_ref,
    rows_ref,
    w_ref,
    row_ref,
    block_ref,
    sh_ref,
    q_ref,
    kv_ref,
    att_ref,
    lse_ref,
    part_ref,
    joined_ref,
    shared_ref,
    peaks,
    totals,
    once,
    once_in,
    here,
    *,
    rows,
):
    z, x, y, c = (lax.axis_index(name) for name in ALL_AXES)
    z_count = lax.axis_size("z")
    e_count = 2 * z_count
    head = HEAD_DIM
    count, model = rows_ref.shape
    block = model // e_count
    own = rows // 4
    tile = 2 * own
    flip = {"x": {"x": 1 - x}, "y": {"y": 1 - y}, "c": {"c": 1 - c}}

    def up(distance):
        return {"z": lax.rem(z + distance, z_count)}

    def copy_to(src, dst, send_sem, recv_sem, device):
        return pltpu.make_async_remote_copy(
            src_ref=src,
            dst_ref=dst,
            send_sem=send_sem,
            recv_sem=recv_sem,
            device_id=device,
            device_id_type=pl.DeviceIdType.MESH,
        )

    def share(d, other):
        z_to, x_to = lax.rem(z + d, z_count), 1 - x if other else x
        i = d + z_count if other else d
        return copy_to(
            sh_ref.at[2 * z_to + x_to],
            shared_ref.at[2 * z + x],
            once.at[i],
            once_in.at[i],
            {"z": z_to, "x": x_to},
        )

    def key_values():
        return copy_to(kv_ref.at[0], kv_ref.at[1], once.at[0], once_in.at[0], flip["x"])

    def start(copies):
        for copy in copies:
            copy.start()

    def finish(copies):
        for copy in copies:
            copy.wait()

    barrier = pltpu.get_barrier_semaphore()
    partners = [flip["x"], flip["y"], flip["c"], up(1), up(2), up(3)]
    partners += [{"z": lax.rem(z + d, z_count), "x": 1 - x} for d in range(1, 4)]
    for device in partners:
        pl.semaphore_signal(
            barrier, inc=1, device_id=device, device_id_type=pl.DeviceIdType.MESH
        )
    keep_share = pltpu.make_async_copy(
        sh_ref.at[2 * z + x], shared_ref.at[2 * z + x], here.at[0]
    )
    keep_share.start()
    for i in range(z_count):
        for j in range(2):
            e = 2 * i + j
            joined_ref[e * block : (e + 1) * block] = w_ref[i, j, :block]
    bias = w_ref[z, 0, pl.ds(block, 16)].astype(jnp.float32) + w_ref[
        z, 1, pl.ds(block, 16)
    ].astype(jnp.float32)
    bias = bias[0:1, : 3 * head]
    lane = lax.broadcasted_iota(jnp.int32, (1, head), 1)
    sign = jnp.where(lane < head // 2, -1.0, 1.0)
    pl.semaphore_wait(barrier, 9)
    shares = [share(d, other) for d in range(4) for other in (False, True) if d or other]

    def project(t, carry):
        lin = product(rows_ref[pl.ds(t * tile, tile), :], joined_ref[:, : 3 * head]) + bias
        for h in range(2):
            s = 2 * t + h
            z_of, y_of, c_of = lax.rem(s, 4), lax.rem(s // 4, 2), s // 8
            place = pl.ds(pl.multiple_of((z_of * 4 + y_of * 2 + c_of) * own, own), own)
            block_cos, block_sin = block_ref[x, 0, pl.ds(s, 1)], block_ref[x, 1, pl.ds(s, 1)]
            cosine = block_cos * row_ref[0] - block_sin * row_ref[1]
            sine = (block_sin * row_ref[0] + block_cos * row_ref[1]) * sign
            part = lin[h * own : (h + 1) * own]
            query, key = part[:, :head], part[:, head : 2 * head]
            query = query * cosine + pltpu.roll(query, head // 2, 1) * sine
            key = key * cosine + pltpu.roll(key, head // 2, 1) * sine
            q_ref[place, :] = query.astype(jnp.bfloat16)
            kv_ref[0, place, :head] = key.astype(jnp.bfloat16)
            kv_ref[0, place, head:] = part[:, 2 * head :].astype(jnp.bfloat16)
        return carry

    lax.fori_loop(0, count // tile, project, 0)
    key_values().start()
    start(shares)
    column = lax.broadcasted_iota(jnp.int32, (tile, rows), 1)

    def scan(i, side, blocks, carry):
        query = q_ref[pl.ds(pl.multiple_of(i * tile, tile), tile), :]
        base = (2 * (i // 2) + x) * rows + lax.rem(i, 2) * tile
        row_pos = base + lax.broadcasted_iota(jnp.int32, (tile, 1), 0)
        limit = jnp.minimum(row_pos, length_ref[0] - 1)
        parity = x if side == 0 else 1 - x

        def body(m, carry):
            peak, total, acc = carry
            window = pl.ds(pl.multiple_of(m * rows, rows), rows)
            scores = product_bt(query, kv_ref[side, window, :head]) * (1.0 / head**0.5)
            scores = jnp.where(column <= limit - (2 * m + parity) * rows, scores, MASKED)
            new_peak = jnp.maximum(peak, jnp.max(scores, axis=1, keepdims=True))
            weights = jnp.exp(scores - new_peak)
            shrink = jnp.exp(peak - new_peak)
            total = shrink * total + jnp.sum(weights, axis=1, keepdims=True)
            acc = shrink * acc + product(
                weights.astype(jnp.bfloat16), kv_ref[side, window, head:]
            )
            return (new_peak, total, acc)

        return lax.fori_loop(0, blocks, body, carry)

    def first_pass(i, carry):
        peak, total, acc = scan(
            i,
            0,
            i // 2 + 1,
            (
                jnp.full((tile, 1), MASKED, jnp.float32),
                jnp.zeros((tile, 1), jnp.float32),
                jnp.zeros((tile, head), jnp.float32),
            ),
        )
        place = pl.ds(pl.multiple_of(i * tile, tile), tile)
        peaks[place, :] = jnp.broadcast_to(peak, (tile, head))
        totals[place, :] = jnp.broadcast_to(total, (tile, head))
        att_ref[place, :] = acc
        return carry

    lax.fori_loop(0, count // tile, first_pass, 0)
    key_values().wait()

    def second_pass(i, carry):
        place = pl.ds(pl.multiple_of(i * tile, tile), tile)
        peak, total, acc = scan(
            i, 1, i // 2 + x, (peaks[place, 0:1], totals[place, 0:1], att_ref[place, :])
        )
        acc = acc / total
        att_ref[place, :] = acc
        lse_ref[place, :] = jnp.broadcast_to(peak + jnp.log(total), (tile, head))
        part = product_bt(acc.astype(jnp.bfloat16), joined_ref[:, 3 * head :]).astype(
            jnp.bfloat16
        )
        for h in range(2):
            z_of, y_of, c_of = i // 2, lax.rem(i, 2), h
            part_ref[c_of * 8 + y_of * 4 + z_of] = part[h * own : (h + 1) * own]
        return carry

    lax.fori_loop(0, count // tile, second_pass, 0)
    finish(shares)
    keep_share.wait()


def middle(length, gathered, weights, row_table, block_table, shared, rows):
    own = rows // 4
    count, model = gathered.shape
    head = HEAD_DIM
    bf16, f32 = jnp.bfloat16, jnp.float32
    anywhere = pl.BlockSpec(memory_space=pl.ANY)
    inside = pl.BlockSpec(memory_space=pltpu.VMEM)
    vm, dma = pltpu.VMEM, pltpu.SemaphoreType.DMA
    shape = jax.ShapeDtypeStruct
    results = pl.pallas_call(
        functools.partial(middle_kernel, rows=rows),
        in_specs=[pl.BlockSpec(memory_space=pltpu.SMEM)] + [inside] * 4 + [anywhere],
        out_specs=[inside] * 6 + [anywhere],
        out_shape=[
            shape((count, head), bf16),
            shape((2, count, 2 * head), bf16),
            shape((count, head), f32),
            shape((count, head), f32),
            shape((count // own, own, model), bf16),
            shape((model, 4 * head), bf16),
            shape(shared.shape, bf16),
        ],
        scratch_shapes=[
            vm((count, head), f32),
            vm((count, head), f32),
            dma((8,)),
            dma((8,)),
            dma((1,)),
        ],
        compiler_params=pltpu.CompilerParams(
            collective_id=3, has_side_effects=True, vmem_limit_bytes=56 * 2**20
        ),
        cost_estimate=pl.CostEstimate(
            flops=10 * count * model * head, bytes_accessed=60 * 2**20, transcendentals=count * count
        ),
    )(
        length,
        gathered,
        weights,
        row_table,
        block_table,
        shared,
    )
    query, key_values, attended, log_total, partial, joined, shared = results
    return (
        query,
        key_values,
        attended,
        log_total,
        partial.reshape(count, model),
        joined,
        shared,
    )


def expert_rows(first, normed, grads, routes, w_ref, d_ref, s_ref, units, experts):
    width = d_ref.shape[0]
    rows = normed.shape[0]
    pre = product_bt(normed, w_ref[...])
    gate_pre = pre[:, :width]
    up_pre = pre[:, width:]
    lane = lax.broadcasted_iota(jnp.int32, (rows, 128), 1)
    router_lane = lane - (128 - experts)
    logits = jnp.where(router_lane >= 0, gate_pre[:, width - 128 :], MASKED)
    expo = jnp.exp(logits - jnp.max(logits, axis=1, keepdims=True))
    probs = expo / jnp.sum(expo, axis=1, keepdims=True)

    def gate_of(expert):
        picked = jnp.sum((routes == expert).astype(jnp.float32), axis=1, keepdims=True)
        return picked * jnp.sum(
            jnp.where(router_lane == expert, probs, 0.0), axis=1, keepdims=True
        )

    share = jax.nn.sigmoid(
        jnp.sum(jnp.where(router_lane == 0, up_pre[:, width - 128 :], 0.0), axis=1, keepdims=True)
    )
    column = lax.broadcasted_iota(jnp.int32, (rows, width), 1)
    scale = jnp.where(column < width - experts, share, 0.0)
    for index in reversed(range(2)):
        scale = jnp.where(column < (index + 1) * units, gate_of(first + index), scale)
    sigma = jax.nn.sigmoid(gate_pre)
    swish = gate_pre * sigma
    hidden = swish * up_pre
    scaled = (hidden * scale).astype(jnp.bfloat16)
    mixture = product(scaled, d_ref[...]).astype(jnp.bfloat16)
    back = product_bt(grads, d_ref[...])
    gate_sums = product((back * hidden).astype(jnp.bfloat16), s_ref[...]).astype(jnp.bfloat16)
    back = back * scale
    grad_gate = (back * up_pre * (sigma * (1.0 + gate_pre * (1.0 - sigma)))).astype(jnp.bfloat16)
    grad_up = (back * swish).astype(jnp.bfloat16)
    pushed = product(grad_gate, w_ref[:width]) + product(grad_up, w_ref[width:])
    return scaled, grad_gate, grad_up, mixture, pushed.astype(jnp.bfloat16), gate_sums


def add_low(*terms):
    total = terms[0].astype(jnp.float32)
    for term in terms[1:]:
        total = total + term.astype(jnp.float32)
    return total.astype(jnp.bfloat16)


def stream_kernel(
    part_ref,
    x_ref,
    gain_ref,
    g_ref,
    eg_ref,
    eu_ref,
    ed_ref,
    sh_ref,
    router_ref,
    s_ref,
    all_ref,
    hs_ref,
    dgu_ref,
    out_ref,
    hidden_ref,
    own_ref,
    lrc_ref,
    lr2_ref,
    lr3_ref,
    lca_ref,
    lcb_ref,
    l2a_ref,
    l2b_ref,
    l3a_ref,
    l3b_ref,
    lza_ref,
    lzb_ref,
    w_ref,
    d_ref,
    n_buf,
    g_buf,
    pa,
    pb,
    ca,
    cb,
    da,
    db,
    ea,
    eb,
    fa,
    fb,
    qa,
    qb,
    sa,
    sb,
    ta,
    tb,
    hs_buf,
    dgu_buf,
    ra,
    rb,
    rc,
    rd,
    re,
    rf,
    send,
    send_z,
    send_r,
    send_c,
    recv_c,
    recv,
    here,
    weigh,
    *,
    units,
    experts,
):
    z, x, y, c = (lax.axis_index(name) for name in ALL_AXES)
    z_count = lax.axis_size("z")
    chunks = x_ref.shape[0]
    model = x_ref.shape[2]
    width = d_ref.shape[0]
    cut = pa.shape[-1]
    half = model // 2
    left, right = pl.ds(0, half), pl.ds(half, half)
    first = 2 * (2 * z + x)
    flip = {"x": {"x": 1 - x}, "y": {"y": 1 - y}, "c": {"c": 1 - c}}

    def up(distance):
        return {"z": lax.rem(z + distance, z_count)}

    def remote(slot, k, src, dst, device):
        return pltpu.make_async_remote_copy(
            src_ref=src,
            dst_ref=dst,
            send_sem=send.at[slot, lax.rem(k, 2)],
            recv_sem=recv.at[slot, k],
            device_id=device,
            device_id_type=pl.DeviceIdType.MESH,
        )

    def spread_z(k, d):
        return pltpu.make_async_remote_copy(
            src_ref=own_ref.at[k],
            dst_ref=all_ref.at[c, y, x, z, k],
            send_sem=send_z.at[d - 1, k],
            recv_sem=recv.at[20 + d, k],
            device_id=up(d),
            device_id_type=pl.DeviceIdType.MESH,
        )

    def heads_c(k):
        return pltpu.make_async_remote_copy(
            src_ref=part_ref.at[1 - c, :, :, k],
            dst_ref=lrc_ref.at[k],
            send_sem=send_r.at[k],
            recv_sem=recv.at[24, k],
            device_id=flip["c"],
            device_id_type=pl.DeviceIdType.MESH,
        )

    def heads_y(k):
        return (remote(17, k, rc.at[lax.rem(k, 2), 1 - y], lr2_ref.at[k], flip["y"]),)

    def heads_z(k):
        copies = []
        for d in range(1, 4):
            there = lax.rem(z + d, z_count)
            copies.append(remote(17 + d, k, re.at[lax.rem(k, 2), there], lr3_ref.at[k, d - 1], up(d)))
        return copies

    def load_hc(k):
        return (
            pltpu.make_async_copy(part_ref.at[c, :, :, k], ra, here.at[15]),
            pltpu.make_async_copy(lrc_ref.at[k], rb, here.at[16]),
        )

    def load_hy(k):
        return (pltpu.make_async_copy(lr2_ref.at[k], rd, here.at[17]),)

    def load_hz(k):
        return (pltpu.make_async_copy(lr3_ref.at[k], rf, here.at[18]),)

    def keep(k):
        return pltpu.make_async_copy(own_ref.at[k], all_ref.at[c, y, x, z, k], here.at[19 + lax.rem(k, 2)])

    def spread_2(k):
        a = all_ref.at[c, y, x, :, k, :, left]
        b = all_ref.at[c, y, x, :, k, :, right]
        return remote(0, k, a, a, flip["x"]), remote(1, k, b, b, flip["y"])

    def spread_3(k):
        a = all_ref.at[c, y, :, :, k, :, left]
        b = all_ref.at[c, :, x, :, k, :, right]
        return remote(2, k, a, a, flip["y"]), remote(3, k, b, b, flip["x"])

    def across(slot, k, src, dst):
        return pltpu.make_async_remote_copy(
            src_ref=src,
            dst_ref=dst,
            send_sem=send_c.at[slot, lax.rem(k, 2)],
            recv_sem=recv_c.at[slot, k],
            device_id=flip["c"],
            device_id_type=pl.DeviceIdType.MESH,
        )

    def spread_c(k):
        copies = []
        for j in range(2):
            for m in range(2):
                a = all_ref.at[c, j, m, :, k]
                copies.append(across(2 * j + m, k, a, a))
        return copies

    def sum_c(k):
        slot = lax.rem(k, 2)
        copies = []
        for j in range(2):
            for m in range(2):
                i = 4 + 2 * j + m
                copies.append(across(i, k, pa.at[slot, 1 - c, j, m], lca_ref.at[k, j, m]))
                copies.append(across(4 + i, k, pb.at[slot, 1 - c, j, m], lcb_ref.at[k, j, m]))
        return copies

    def sum_2(k):
        return (
            remote(7, k, qa.at[lax.rem(k, 2), 1 - y], l2a_ref.at[k], flip["y"]),
            remote(8, k, qb.at[lax.rem(k, 2), :, 1 - x], l2b_ref.at[k], flip["x"]),
        )

    def sum_3(k):
        return (
            remote(9, k, sa.at[lax.rem(k, 2), 1 - x], l3a_ref.at[k], flip["x"]),
            remote(10, k, sb.at[lax.rem(k, 2), 1 - y], l3b_ref.at[k], flip["y"]),
        )

    def sum_z(k):
        copies = []
        for d in range(1, 4):
            there = lax.rem(z + d, z_count)
            copies.append(remote(10 + d, k, ta.at[lax.rem(k, 2), there], lza_ref.at[k, d - 1], up(d)))
            copies.append(remote(13 + d, k, tb.at[lax.rem(k, 2), there], lzb_ref.at[k, d - 1], up(d)))
        return copies

    def load_rows(k):
        slot = lax.rem(k, 2)
        return (
            pltpu.make_async_copy(all_ref.at[:, :, :, :, k], n_buf.at[slot], here.at[slot]),
            pltpu.make_async_copy(g_ref.at[:, :, :, :, k], g_buf.at[slot], here.at[13 + slot]),
        )

    def load_c(k):
        return (
            pltpu.make_async_copy(lca_ref.at[k], ca, here.at[2]),
            pltpu.make_async_copy(lcb_ref.at[k], cb, here.at[3]),
        )

    def load_2(k):
        return (
            pltpu.make_async_copy(l2a_ref.at[k], da, here.at[4]),
            pltpu.make_async_copy(l2b_ref.at[k], db, here.at[5]),
        )

    def load_3(k):
        return (
            pltpu.make_async_copy(l3a_ref.at[k], ea, here.at[6]),
            pltpu.make_async_copy(l3b_ref.at[k], eb, here.at[7]),
        )

    def load_z(k):
        return (
            pltpu.make_async_copy(lza_ref.at[k], fa, here.at[8]),
            pltpu.make_async_copy(lzb_ref.at[k], fb, here.at[9]),
        )

    def store_rows(k):
        return (
            pltpu.make_async_copy(hs_buf, hs_ref.at[:, :, :, :, k], here.at[10]),
            pltpu.make_async_copy(dgu_buf, dgu_ref.at[:, :, :, :, k], here.at[11]),
        )

    def start(copies):
        for copy in copies:
            copy.start()

    def finish(copies):
        for copy in copies:
            copy.wait()

    def at(k, body):
        pl.when((k >= 0) & (k < chunks))(lambda: body(k))

    barrier = pltpu.get_barrier_semaphore()
    for device in (flip["x"], flip["y"], flip["c"], up(1), up(2), up(3)):
        pl.semaphore_signal(
            barrier, inc=1, device_id=device, device_id_type=pl.DeviceIdType.MESH
        )
    pl.semaphore_wait(barrier, 6)

    def first_sends(k, carry):
        heads_c(k).start()
        return carry

    lax.fori_loop(0, chunks, first_sends, 0)
    routed, share = eg_ref.shape[0], sh_ref.shape[1] // 3
    low = pl.ds(routed, share)
    high = pl.ds(width + routed, share)

    def weight_copies():
        pairs = [
            (eg_ref, w_ref.at[pl.ds(0, routed)]),
            (eu_ref, w_ref.at[pl.ds(width, routed)]),
            (ed_ref, d_ref.at[pl.ds(0, routed)]),
            (router_ref.at[0], w_ref.at[pl.ds(width - experts, experts)]),
            (router_ref.at[1], w_ref.at[pl.ds(2 * width - experts, experts)]),
        ]
        cells = model // sh_ref.shape[0]
        for e in range(sh_ref.shape[0]):
            columns = pl.ds(e * cells, cells)
            pairs.append((sh_ref.at[e, pl.ds(0, share)], w_ref.at[low, columns]))
            pairs.append((sh_ref.at[e, pl.ds(share, share)], w_ref.at[high, columns]))
            pairs.append((sh_ref.at[e, pl.ds(2 * share, share)], d_ref.at[low, columns]))
        return [
            pltpu.make_async_copy(src, dst, weigh.at[i]) for i, (src, dst) in enumerate(pairs)
        ]

    start(weight_copies())
    d_ref[pl.ds(width - experts, experts), :] = jnp.zeros((experts, model), jnp.bfloat16)

    def arrive_hc(k):
        heads_c(k).wait()
        start(load_hc(k))

    def arrive_hy(k):
        finish(heads_y(k))
        start(load_hy(k))

    def arrive_hz(k):
        finish(heads_z(k))
        start(load_hz(k))

    def close_hc(k):
        finish(load_hc(k))
        slot = lax.rem(k, 2)

        def each(i, carry):
            for j in range(2):
                rc[slot, j, i] = add_low(ra[j, i], rb[j, i])
            return carry

        lax.fori_loop(0, z_count, each, 0)
        start(heads_y(k))

    def close_hy(k):
        finish(load_hy(k))
        slot = lax.rem(k, 2)
        for i in range(4):
            re[slot, i] = add_low(rc[slot, y, i], rd[i])
        start(heads_z(k))

    def close_hz(k):
        finish(load_hz(k))
        total = re[lax.rem(k, 2), z].astype(jnp.float32)
        for d in range(3):
            total = total + rf[d].astype(jnp.float32)
        hidden = x_ref[k].astype(jnp.float32) + total
        inverse = lax.rsqrt(jnp.mean(hidden * hidden, axis=1, keepdims=True) + EPSILON)
        hidden_ref[k] = hidden
        own_ref[k] = (hidden * inverse * gain_ref[...]).astype(jnp.bfloat16)
        keep(k).start()
        for d in range(1, 4):
            spread_z(k, d).start()

    def gather_2(k):
        keep(k).wait()
        for d in range(1, 4):
            spread_z(k, d).wait()
        start(spread_2(k))

    def gather_3(k):
        finish(spread_2(k))
        start(spread_3(k))

    def gather_c(k):
        finish(spread_3(k))
        start(spread_c(k))

    def gathered(k):
        finish(spread_c(k))
        start(load_rows(k))

    def work(k, part):
        slot = lax.rem(k, 2)
        rows = 256
        normed = n_buf[slot, part].reshape(rows, model)
        grads = g_buf[slot, part].reshape(rows, model + 128)
        routes = grads[:, model : model + 128].astype(jnp.int32)
        grads = grads[:, :model]
        scaled, grad_gate, grad_up, mixture, pushed, gate_sums = expert_rows(
            first, normed, grads, routes, w_ref, d_ref, s_ref, units, experts
        )
        shape = (2, 2, z_count, 16)
        hs_buf[part] = scaled.reshape(shape + (width,))
        dgu_buf[part, :, :, :, :, :width] = grad_gate.reshape(shape + (width,))
        dgu_buf[part, :, :, :, :, width:] = grad_up.reshape(shape + (width,))
        pa[slot, part] = mixture[:, :cut].reshape(shape + (cut,))
        rest = model - cut
        if rest:
            pb[slot, part, :, :, :, :, :rest] = mixture[:, cut:].reshape(shape + (rest,))
        pb[slot, part, :, :, :, :, rest : rest + model] = pushed.reshape(shape + (model,))
        pb[slot, part, :, :, :, :, rest + model :] = gate_sums.reshape(shape + (128,))

    def work_first(k):
        finish(load_rows(k))
        at(k - 1, lambda j: finish(store_rows(j)))
        work(k, 0)

    def work_second(k):
        work(k, 1)
        start(store_rows(k))

    def arrive_c(k):
        finish(sum_c(k))
        start(load_c(k))

    def arrive_2(k):
        finish(sum_2(k))
        start(load_2(k))

    def arrive_3(k):
        finish(sum_3(k))
        start(load_3(k))

    def arrive_z(k):
        finish(sum_z(k))
        start(load_z(k))

    def close_z(k):
        finish(load_z(k))
        slot = lax.rem(k, 2)
        own_a = ta[slot, z].astype(jnp.float32)
        own_b = tb[slot, z].astype(jnp.float32)
        for d in range(3):
            own_a = own_a + fa[d].astype(jnp.float32)
            own_b = own_b + fb[d].astype(jnp.float32)
        out_ref[k, :, :cut] = own_a
        out_ref[k, :, cut:] = own_b

    def close_3(k):
        finish(load_3(k))
        slot = lax.rem(k, 2)

        def each(i, carry):
            ta[slot, i] = add_low(sa[slot, x, i], ea[i])
            tb[slot, i] = add_low(sb[slot, y, i], eb[i])
            return carry

        lax.fori_loop(0, z_count, each, 0)
        start(sum_z(k))

    def close_2(k):
        finish(load_2(k))
        slot = lax.rem(k, 2)

        def each(i, carry):
            for j in range(2):
                sa[slot, j, i] = add_low(qa[slot, y, j, i], da[j, i])
                sb[slot, j, i] = add_low(qb[slot, j, x, i], db[j, i])
            return carry

        lax.fori_loop(0, z_count, each, 0)
        start(sum_3(k))

    def close_c(k):
        finish(load_c(k))
        slot = lax.rem(k, 2)

        def each(i, carry):
            for j in range(2):
                for m in range(2):
                    qa[slot, j, m, i] = add_low(pa[slot, c, j, m, i], ca[j, m, i])
                    qb[slot, j, m, i] = add_low(pb[slot, c, j, m, i], cb[j, m, i])
            return carry

        lax.fori_loop(0, z_count, each, 0)
        start(sum_2(k))

    def tick(i, carry):
        at(i - 11, gathered)
        at(i - 10, gather_c)
        at(i - 8, gather_3)
        at(i - 6, gather_2)
        pl.when(i == 12)(lambda: finish(weight_copies()))
        at(i - 12, work_first)
        at(i - 19, arrive_z)
        at(i - 17, arrive_3)
        at(i - 15, arrive_2)
        at(i - 13, arrive_c)
        at(i - 4, arrive_hz)
        at(i - 2, arrive_hy)
        at(i, arrive_hc)
        at(i - 12, work_second)
        at(i - 4, close_hz)
        at(i - 2, close_hy)
        at(i, close_hc)
        at(i - 19, close_z)
        at(i - 17, close_3)
        at(i - 15, close_2)
        at(i - 13, close_c)
        at(i - 12, lambda k: start(sum_c(k)))
        return carry

    lax.fori_loop(0, chunks + 19, tick, 0)
    finish(store_rows(chunks - 1))


def stream(
    partial, tokens, gain, grads, gates, ups, downs, shared, router, segments, units, experts, chunks
):
    own, model = tokens.shape
    width = segments.shape[0]
    piece = own // chunks
    zs = lax.axis_size("z")
    lead = (2, 2, 2, zs)
    partial = partial.reshape((2, 2, zs, chunks, piece, model))
    grads = grads.reshape(lead + (chunks, piece, model + 128))
    tokens = tokens.reshape(chunks, piece, model)
    cut = model
    extra = 2 * model + 128 - cut
    bf16 = jnp.bfloat16
    shapes = [
        (lead + (chunks, piece, model), bf16),
        (lead + (chunks, piece, width), bf16),
        (lead + (chunks, piece, 2 * width), bf16),
        ((chunks, piece, 2 * model + 128), jnp.float32),
        ((chunks, piece, model), jnp.float32),
        ((chunks, piece, model), bf16),
        ((chunks, 2, zs, piece, model), bf16),
        ((chunks, zs, piece, model), bf16),
        ((chunks, 3, piece, model), bf16),
        ((chunks, 2, 2, zs, piece, cut), bf16),
        ((chunks, 2, 2, zs, piece, extra), bf16),
        ((chunks, 2, zs, piece, cut), bf16),
        ((chunks, 2, zs, piece, extra), bf16),
        ((chunks, zs, piece, cut), bf16),
        ((chunks, zs, piece, extra), bf16),
        ((chunks, 3, piece, cut), bf16),
        ((chunks, 3, piece, extra), bf16),
    ]
    anywhere = pl.BlockSpec(memory_space=pl.ANY)
    inside = pl.BlockSpec(memory_space=pltpu.VMEM)
    vm = pltpu.VMEM
    dma = pltpu.SemaphoreType.DMA
    scratch = [
        vm((2 * width, model), bf16),
        vm((width, model), bf16),
        vm((2,) + lead + (piece, model), bf16),
        vm((2,) + lead + (piece, model + 128), bf16),
        vm((2,) + lead + (piece, cut), bf16),
        vm((2,) + lead + (piece, extra), bf16),
        vm((2, 2, zs, piece, cut), bf16),
        vm((2, 2, zs, piece, extra), bf16),
        vm((2, zs, piece, cut), bf16),
        vm((2, zs, piece, extra), bf16),
        vm((zs, piece, cut), bf16),
        vm((zs, piece, extra), bf16),
        vm((3, piece, cut), bf16),
        vm((3, piece, extra), bf16),
        vm((2, 2, 2, zs, piece, cut), bf16),
        vm((2, 2, 2, zs, piece, extra), bf16),
        vm((2, 2, zs, piece, cut), bf16),
        vm((2, 2, zs, piece, extra), bf16),
        vm((2, zs, piece, cut), bf16),
        vm((2, zs, piece, extra), bf16),
        vm(lead + (piece, width), bf16),
        vm(lead + (piece, 2 * width), bf16),
        vm((2, zs, piece, model), bf16),
        vm((2, zs, piece, model), bf16),
        vm((2, 2, zs, piece, model), bf16),
        vm((zs, piece, model), bf16),
        vm((2, zs, piece, model), bf16),
        vm((3, piece, model), bf16),
        dma((21, 2)),
        dma((3, chunks)),
        dma((chunks,)),
        dma((12, 2)),
        dma((12, chunks)),
        dma((25, chunks)),
        dma((21,)),
        dma((5 + 3 * shared.shape[0],)),
    ]
    rows = own * 8 * zs
    results = pl.pallas_call(
        functools.partial(stream_kernel, units=units, experts=experts),
        in_specs=[anywhere, inside, inside] + [anywhere] * 6 + [inside],
        out_specs=[anywhere] * 3 + [inside] * 3 + [anywhere] * 11,
        out_shape=[jax.ShapeDtypeStruct(s, t) for s, t in shapes],
        scratch_shapes=scratch,
        compiler_params=pltpu.CompilerParams(
            collective_id=1, has_side_effects=True, vmem_limit_bytes=61 * 2**20
        ),
        cost_estimate=pl.CostEstimate(
            flops=12 * rows * model * width,
            bytes_accessed=rows * (14 * model + 6 * width),
            transcendentals=rows * width,
        ),
    )(partial, tokens, gain, grads, gates, ups, downs, shared, router, segments)
    gathered, scaled, slopes, sums, hidden, normed = results[:6]
    return (
        gathered.reshape(rows, model),
        scaled.reshape(rows, width),
        slopes.reshape(rows, 2 * width),
        sums.reshape(own, 2 * model + 128),
        hidden.reshape(own, model),
        normed.reshape(own, model),
    )


def finish_kernel(
    part_ref,
    grads_ref,
    x_ref,
    wp_ref,
    bp_ref,
    w_ref,
    e_ref,
    scale_ref,
    rows_ref,
    dq_ref,
    dk_ref,
    dv_ref,
    do_ref,
    bias_ref,
    gain_ref,
    square_ref,
    extra_ref,
    lc,
    ly,
    lz,
    rc,
    re,
    gt,
    wl,
    bl,
    ws,
    heads_ref,
    gs,
    gl,
    ss,
    sl,
    ls,
    ll,
    lx,
    lu,
    lv,
    send,
    send_k,
    recv,
    once,
    once_in,
    here,
):
    z, x, y, c = (lax.axis_index(name) for name in ALL_AXES)
    z_count = lax.axis_size("z")
    chunks, _, model = x_ref.shape
    head = HEAD_DIM
    flip = {"x": {"x": 1 - x}, "y": {"y": 1 - y}, "c": {"c": 1 - c}}

    def up(distance):
        return {"z": lax.rem(z + distance, z_count)}

    def copy_to(src, dst, send_sem, recv_sem, device):
        return pltpu.make_async_remote_copy(
            src_ref=src,
            dst_ref=dst,
            send_sem=send_sem,
            recv_sem=recv_sem,
            device_id=device,
            device_id_type=pl.DeviceIdType.MESH,
        )

    def heads_c(k):
        return copy_to(
            part_ref.at[1 - c, :, :, k], lc.at[k], send_k.at[k], recv.at[0, k], flip["c"]
        )

    def heads_y(k):
        return copy_to(rc.at[lax.rem(k, 2), 1 - y], ly.at[k], send.at[0, lax.rem(k, 2)], recv.at[1, k], flip["y"])

    def heads_z(k, d):
        there = lax.rem(z + d, z_count)
        return copy_to(
            re.at[lax.rem(k, 2), there], lz.at[k, d - 1], send.at[d, lax.rem(k, 2)], recv.at[1 + d, k], up(d)
        )

    def keep(k):
        return pltpu.make_async_copy(gt.at[k], rows_ref.at[y, c, k], here.at[lax.rem(k, 2)])

    def rows_y(k):
        return copy_to(gt.at[k], rows_ref.at[y, c, k], send.at[4, lax.rem(k, 2)], recv.at[5, k], flip["y"])

    def rows_c(k):
        block = rows_ref.at[:, c, k]
        return copy_to(block, block, send.at[5, lax.rem(k, 2)], recv.at[6, k], flip["c"])

    def single(i, src, dst, device):
        return copy_to(src, dst, once.at[i], once_in.at[i], device)

    def weights_x():
        return (
            single(0, wp_ref.at[1 - x], wl, flip["x"]),
            single(1, bp_ref.at[1 - x], bl, flip["x"]),
        )

    def weights_z(d):
        return single(1 + d, ws.at[lax.rem(z + d, z_count)], heads_ref.at[z], up(d))

    def at(k, body):
        pl.when((k >= 0) & (k < chunks))(lambda: body(k))

    barrier = pltpu.get_barrier_semaphore()
    for device in (flip["x"], flip["y"], flip["c"], up(1), up(2), up(3)):
        pl.semaphore_signal(
            barrier, inc=1, device_id=device, device_id_type=pl.DeviceIdType.MESH
        )
    square_ref[...] = jnp.zeros_like(square_ref)
    pl.semaphore_wait(barrier, 6)

    def first_sends(k, carry):
        heads_c(k).start()
        return carry

    lax.fori_loop(0, chunks, first_sends, 0)
    for copy in weights_x():
        copy.start()

    def close_c(k):
        heads_c(k).wait()
        slot = lax.rem(k, 2)

        def each(i, carry):
            for j in range(2):
                rc[slot, j, i] = add_low(part_ref[c, j, i, k], lc[k, j, i])
            return carry

        lax.fori_loop(0, z_count, each, 0)
        heads_y(k).start()

    def close_y(k):
        heads_y(k).wait()
        slot = lax.rem(k, 2)
        for i in range(4):
            re[slot, i] = add_low(rc[slot, y, i], ly[k, i])
        for d in range(1, 4):
            heads_z(k, d).start()

    def close_z(k):
        for d in range(1, 4):
            heads_z(k, d).wait()
        pushed = re[lax.rem(k, 2), z].astype(jnp.float32)
        for d in range(3):
            pushed = pushed + lz[k, d].astype(jnp.float32)
        values = x_ref[k].astype(jnp.float32)
        inverse = lax.rsqrt(jnp.mean(values * values, axis=1, keepdims=True) + EPSILON)
        scaled = values * inverse
        total = grads_ref[k] + inverse * (
            pushed - scaled * jnp.mean(pushed * scaled, axis=1, keepdims=True)
        )
        gt[k] = total.astype(jnp.bfloat16)
        squares = total * total
        squares = squares[:8] + squares[8:]
        lanes = squares[:, :128]
        for j in range(1, model // 128):
            lanes = lanes + squares[:, j * 128 : (j + 1) * 128]
        square_ref[...] += lanes
        keep(k).start()
        rows_y(k).start()

    def close_rows(k):
        keep(k).wait()
        rows_y(k).wait()
        rows_c(k).start()

    def close_all(k):
        rows_c(k).wait()

    def weights_sum():
        for copy in weights_x():
            copy.wait()
        bias_ref[...] = bp_ref[x].astype(jnp.float32) + bl[...].astype(jnp.float32)

        def each(i, carry):
            ws[i] = add_low(wp_ref[x, i], wl[i])
            return carry

        lax.fori_loop(0, z_count, each, 0)
        heads_ref[z] = ws[z]
        for d in range(1, 4):
            weights_z(d).start()

    def extra_c():
        return single(13, e_ref, ll.at[0], flip["c"])

    def extra_y():
        return single(14, ls, ll.at[1], flip["y"])

    def extra_x():
        return single(15, lx.at[1 - x], lu, flip["x"])

    def extra_z(d):
        return single(15 + d, lx.at[x, lax.rem(z + d, z_count)], lv.at[d - 1], up(d))

    def extra_sum_c():
        extra_c().wait()
        ls[...] = e_ref[...] + ll[0]
        extra_y().start()

    def extra_sum_y():
        extra_y().wait()
        lx[...] = ls[...] + ll[1]
        extra_x().start()

    def extra_sum_x():
        extra_x().wait()
        lx[x] = lx[x] + lu[...]
        for d in range(1, 4):
            extra_z(d).start()

    def gain_y():
        return single(6, gs.at[0], gl.at[0], flip["y"])

    def gain_c():
        return single(8, gs.at[1], gl.at[1], flip["c"])

    def weights_done():
        for d in range(1, 4):
            weights_z(d).wait()
        total = jnp.zeros(gain_ref.shape, jnp.float32)
        scale = scale_ref[...]
        for i in range(4):
            place = slice(i * head, (i + 1) * head)
            for j, ref in enumerate((dq_ref, dk_ref, dv_ref)):
                columns = slice(j * head, (j + 1) * head)
                values = heads_ref[i, :, columns].astype(jnp.float32)
                total = total + w_ref[i, :, columns].astype(jnp.float32) * values
                ref[:, place] = values * scale
            do_ref[place, :] = heads_ref[i, :, 3 * head :].astype(jnp.float32).T
        gs[0] = total
        gain_y().start()

    def gain_sum():
        gain_y().wait()
        gs[1] = gs[0] + gl[0]
        gain_c().start()

    extra_c().start()

    def tick(i, carry):
        at(i - 7, close_all)
        at(i - 6, close_rows)
        at(i - 4, close_z)
        at(i - 2, close_y)
        at(i, close_c)
        pl.when(i == 2)(weights_sum)
        pl.when(i == 2)(extra_sum_c)
        pl.when(i == 4)(extra_sum_y)
        pl.when(i == 6)(extra_sum_x)
        pl.when(i == 7)(weights_done)
        pl.when(i == 9)(gain_sum)
        return carry

    lax.fori_loop(0, chunks + 7, tick, 0)
    for d in range(1, 4):
        extra_z(d).wait()
    extra_ref[...] = lx[x, z] + lv[0] + lv[1] + lv[2]
    ss[0] = square_ref[...]
    squares_c = single(5, ss.at[0], sl.at[0], flip["c"])
    squares_c.start()
    squares_c.wait()
    ss[1] = ss[0] + sl[0]
    squares_y = single(7, ss.at[1], sl.at[1], flip["y"])
    squares_y.start()
    squares_y.wait()
    ss[2] = ss[1] + sl[1]
    squares_x = single(9, ss.at[2], sl.at[2], flip["x"])
    squares_x.start()
    squares_x.wait()
    ss[3] = ss[2] + sl[2]
    squares_z = [single(9 + d, ss.at[3], sl.at[2 + d], up(d)) for d in range(1, 4)]
    for copy in squares_z:
        copy.start()
    gain_c().wait()
    gain_ref[...] = gs[1] + gl[1]
    for copy in squares_z:
        copy.wait()
    square_ref[...] = ss[3] + sl[3] + sl[4] + sl[5]


def finish(partial, grads, tokens, weight_parts, bias_parts, weights, extras, scale, chunks):
    own, model = tokens.shape
    piece = own // chunks
    zs = lax.axis_size("z")
    bf16, f32 = jnp.bfloat16, jnp.float32
    block, wide = weight_parts.shape[2:]
    anywhere = pl.BlockSpec(memory_space=pl.ANY)
    inside = pl.BlockSpec(memory_space=pltpu.VMEM)
    vm = pltpu.VMEM
    dma = pltpu.SemaphoreType.DMA
    rows, d_query, d_key, d_value, d_out, bias, gain, square, extra = pl.pallas_call(
        finish_kernel,
        in_specs=[inside] * 8,
        out_specs=[anywhere] + [inside] * 8,
        out_shape=[
            jax.ShapeDtypeStruct((2, 2, chunks, piece, model), bf16),
            jax.ShapeDtypeStruct((block, wide), f32),
            jax.ShapeDtypeStruct((block, wide), f32),
            jax.ShapeDtypeStruct((block, wide), f32),
            jax.ShapeDtypeStruct((wide, block), f32),
            jax.ShapeDtypeStruct(bias_parts.shape[1:], f32),
            jax.ShapeDtypeStruct((block, 128), f32),
            jax.ShapeDtypeStruct((8, 128), f32),
            jax.ShapeDtypeStruct(extras.shape[2:], f32),
        ],
        scratch_shapes=[
            vm((chunks, 2, zs, piece, model), bf16),
            vm((chunks, zs, piece, model), bf16),
            vm((chunks, 3, piece, model), bf16),
            vm((2, 2, zs, piece, model), bf16),
            vm((2, zs, piece, model), bf16),
            vm((chunks, piece, model), bf16),
            vm((zs, block, wide), bf16),
            vm(bias_parts.shape[1:], bf16),
            vm((zs, block, wide), bf16),
            vm((zs, block, wide), bf16),
            vm((2, block, 128), f32),
            vm((2, block, 128), f32),
            vm((4, 8, 128), f32),
            vm((6, 8, 128), f32),
            vm(extras.shape, f32),
            vm((2,) + extras.shape, f32),
            vm(extras.shape, f32),
            vm(extras.shape[1:], f32),
            vm((3,) + extras.shape[2:], f32),
            dma((6, 2)),
            dma((chunks,)),
            dma((7, chunks)),
            dma((19,)),
            dma((19,)),
            dma((2,)),
        ],
        compiler_params=pltpu.CompilerParams(
            collective_id=2, has_side_effects=True, vmem_limit_bytes=48 * 2**20
        ),
        cost_estimate=pl.CostEstimate(
            flops=100 * own * model, bytes_accessed=40 * 2**20, transcendentals=0
        ),
    )(
        partial.reshape(2, 2, zs, chunks, piece, model),
        grads.reshape(chunks, piece, model),
        tokens.reshape(chunks, piece, model),
        weight_parts,
        bias_parts,
        weights,
        extras,
        scale,
    )
    return rows.reshape(4 * own, model), d_query, d_key, d_value, d_out, bias, gain, square, extra


def weight_grads_kernel(
    n_ref, g_ref, slopes_ref, scaled_ref, gate_ref, up_ref, down_ref, sh_ref, *, units, share
):
    width = scaled_ref.shape[1]
    low = 2 * units
    first = product_at(n_ref[...], slopes_ref[...]).T
    second = product_at(g_ref[...], scaled_ref[...]).T
    for ref, rows in ((gate_ref, first[:width]), (up_ref, first[width:]), (down_ref, second)):
        for i in range(2):
            ref[i] = rows[i * units : (i + 1) * units]
    for i, rows in enumerate((first[:width], first[width:], second)):
        sh_ref[0, i * share : (i + 1) * share] = rows[low : low + share].astype(jnp.bfloat16)


def weight_grads(normed, grads, slopes, scaled, units, share, blocks):
    count, model = normed.shape
    width = scaled.shape[1]
    block = model // blocks
    one = pl.Buffered(1)
    f32, bf16 = jnp.float32, jnp.bfloat16
    rows = pl.BlockSpec((2, units, block), lambda i: (0, 0, i))
    return pl.pallas_call(
        functools.partial(weight_grads_kernel, units=units, share=share),
        grid=(blocks,),
        in_specs=[
            pl.BlockSpec((count, block), lambda i: (0, i)),
            pl.BlockSpec((count, block), lambda i: (0, i)),
            pl.BlockSpec(slopes.shape, lambda i: (0, 0), pipeline_mode=one),
            pl.BlockSpec(scaled.shape, lambda i: (0, 0), pipeline_mode=one),
        ],
        out_specs=[rows, rows, rows, pl.BlockSpec((1, 3 * share, block), lambda i: (i, 0, 0))],
        out_shape=[jax.ShapeDtypeStruct((2, units, model), f32)] * 3
        + [jax.ShapeDtypeStruct((blocks, 3 * share, block), bf16)],
        compiler_params=pltpu.CompilerParams(vmem_limit_bytes=56 * 2**20),
        cost_estimate=pl.CostEstimate(
            flops=6 * count * model * width,
            bytes_accessed=count * (4 * model + 6 * width) + 12 * model * width,
            transcendentals=0,
        ),
    )(normed, grads, slopes, scaled)


def head_grads_kernel(first_ref, hidden_ref, qkv_ref, att_ref, out_ref):
    wide = qkv_ref.shape[1]
    out_ref[0, 0, :, :wide] = product_at(first_ref[...], qkv_ref[...]).astype(jnp.bfloat16)
    out_ref[0, 0, :, wide:] = product_at(hidden_ref[...], att_ref[...]).astype(jnp.bfloat16)


def head_grads(first, hidden, grad_qkv, attended, block):
    count, model = first.shape
    wide = grad_qkv.shape[1] + attended.shape[1]
    blocks = model // block
    return pl.pallas_call(
        head_grads_kernel,
        grid=(blocks,),
        in_specs=[
            pl.BlockSpec((count, block), lambda i: (0, i)),
            pl.BlockSpec((count, block), lambda i: (0, i)),
            pl.BlockSpec(grad_qkv.shape, lambda i: (0, 0)),
            pl.BlockSpec(attended.shape, lambda i: (0, 0)),
        ],
        out_specs=pl.BlockSpec((1, 1, block, wide), lambda i: (i % 2, i // 2, 0, 0)),
        out_shape=jax.ShapeDtypeStruct((2, blocks // 2, block, wide), jnp.bfloat16),
        compiler_params=pltpu.CompilerParams(vmem_limit_bytes=32 * 2**20),
        cost_estimate=pl.CostEstimate(
            flops=2 * count * model * wide, bytes_accessed=5 * count * model, transcendentals=0
        ),
    )(first, hidden, grad_qkv, attended)


def packed(
    tokens,
    cotangent,
    lengths,
    routes,
    w_query,
    w_key,
    w_value,
    w_out,
    b_query,
    b_key,
    b_value,
    gain_attention,
    gain_experts,
    w_router,
    w_shared_gate,
    shared_gate,
    shared_up,
    shared_down,
    expert_gate,
    expert_up,
    expert_down,
    chunks=8,
):
    f32, bf16 = jnp.float32, jnp.bfloat16
    heads_z = lax.axis_size("z")
    exp_count = heads_z * lax.axis_size("x")
    tp_count = lax.axis_size("y") * lax.axis_size("c")
    z_index, x_index = lax.axis_index("z"), lax.axis_index("x")
    exp_index = z_index * lax.axis_size("x") + x_index
    tp_index = lax.axis_index("y") * lax.axis_size("c") + lax.axis_index("c")
    rows, model = tokens.shape
    total_rows = rows * exp_count
    own = rows // tp_count
    block = model // exp_count
    local_experts, _, units = expert_gate.shape
    experts = local_experts * exp_count
    shared_units = shared_gate.shape[1] // exp_count
    head = HEAD_DIM
    length = lengths[0]

    def my_rows(array):
        return lax.dynamic_slice_in_dim(array, tp_index * own, own, 0)

    own_tokens = my_rows(tokens).astype(f32)
    normed_first = (own_tokens * norm_scale(own_tokens)).astype(bf16)
    gain_rows = gain_attention.astype(f32)
    attn_gain_own = gain_rows[:, None]
    query_part, key_part, value_part = (
        (w.astype(f32) * attn_gain_own).astype(bf16).reshape(block, heads_z, head)
        for w in (w_query, w_key, w_value)
    )
    out_part = w_out.reshape(heads_z, head, block).transpose(2, 0, 1)
    attn_parts = jnp.concatenate([query_part, key_part, value_part, out_part], axis=2)
    half_dim = head // 2
    side = x_index * half_dim
    bias_row = jnp.zeros((3, head), bf16)
    bias_row = lax.dynamic_update_slice(
        bias_row, jnp.stack([b_query, b_key, b_value]), (jnp.zeros_like(side), side)
    )
    small = flat([gain_experts, w_router.T, w_shared_gate])
    small = jnp.pad(small, (0, 15 * 4 * head - small.shape[0])).reshape(15, 4 * head)
    small = jnp.concatenate([jnp.pad(bias_row.reshape(1, 3 * head), ((0, 0), (0, head))), small])
    attn_parts = jnp.concatenate(
        [
            attn_parts.transpose(1, 0, 2),
            jnp.broadcast_to(small[None], (heads_z, 16, 4 * head)),
        ],
        axis=1,
    )
    own_first = exp_index * rows + tp_index * own
    own_positions = own_first + jnp.arange(own, dtype=jnp.int32)
    valid = (own_positions < length).astype(f32)[:, None]
    grad_out_low = (my_rows(cotangent).astype(f32) * valid).astype(bf16)
    own_routes = my_rows(routes)
    leaving = jnp.concatenate(
        [grad_out_low, jnp.pad(own_routes.astype(bf16), ((0, 0), (0, 124)), constant_values=-1.0)],
        axis=1,
    )
    first_half, arrived_weights, grad_all = front(normed_first, attn_parts, leaving)
    small = arrived_weights[:, :, block + 1 :].reshape(exp_count, 15 * 4 * head)
    shared_parts = jnp.concatenate(
        [
            w.reshape(exp_count, shared_units, block)
            for w in (shared_gate.T, shared_up.T, shared_down)
        ],
        axis=1,
    )
    place = 0
    ffn_gain = small[:, place : place + block].reshape(model).astype(f32)
    place += block
    router_rows = (
        small[:, place : place + block * experts]
        .reshape(exp_count, experts, block)
        .transpose(1, 0, 2)
        .reshape(experts, model)
    )
    place += block * experts
    share_vector = small[:, place : place + block].reshape(model)

    frequency = np.tile(ROPE_BASE ** (-np.arange(half_dim) * 2.0 / head), 2)
    row_angle = np.arange(own)[:, None] * frequency
    starts = (
        np.arange(2)[:, None, None, None] * rows
        + np.arange(2)[None, :, None, None] * own
        + np.arange(2)[None, None, :, None] * 2 * own
        + np.arange(heads_z)[None, None, None, :] * 2 * rows
    )
    block_angle = starts.reshape(2, -1, 1) * frequency
    row_table = np.stack([np.cos(row_angle), np.sin(row_angle)]).astype(np.float32)
    block_table = np.stack([np.cos(block_angle), np.sin(block_angle)], axis=1).astype(np.float32)
    row_cos, row_sin = jnp.asarray(row_table[:, None, :, :half_dim])
    block_both = lax.dynamic_index_in_dim(jnp.asarray(block_table), x_index, 0, keepdims=False)
    block_cos, block_sin = block_both[:, :, None, :half_dim]
    cosine = (block_cos * row_cos - block_sin * row_sin).reshape(heads_z * rows, half_dim)
    sine = (block_sin * row_cos + block_cos * row_sin).reshape(heads_z * rows, half_dim)

    def rope_back(values):
        one, two = values[:, :half_dim], values[:, half_dim:]
        return jnp.concatenate([one * cosine + two * sine, two * cosine - one * sine], axis=1)

    def by_position(array):
        return (
            array.reshape((2, 2, heads_z, own) + array.shape[1:])
            .transpose(2, 1, 0, 3, 4)
            .reshape(array.shape)
        )

    def by_owner(array):
        return (
            array.reshape((heads_z, 2, 2, own) + array.shape[1:])
            .transpose(2, 1, 0, 3, 4)
            .reshape(array.shape)
        )

    flip = [(0, 1), (1, 0)]
    query_rot, key_values, attended, log_total, attn_part, attn_weights, shared_parts = (
        middle(
            lengths,
            first_half,
            arrived_weights,
            jnp.asarray(row_table),
            jnp.asarray(block_table),
            shared_parts,
            rows,
        )
    )
    info = jnp.stack([x_index, length]).astype(jnp.int32)
    attended_low = by_owner(attended.astype(bf16))
    out_weight = attn_weights[:, 3 * head :]

    width = local_experts * units + shared_units + experts
    router_pair = jnp.stack(
        [router_rows, jnp.pad(share_vector[None, :], ((0, experts - 1), (0, 0)))]
    )
    unit = jnp.arange(width, dtype=jnp.int32)
    segment = jnp.where(
        unit < local_experts * units, exp_index * local_experts + unit // units, experts
    )
    segments = (
        (segment[:, None] == jnp.arange(128, dtype=jnp.int32)[None, :])
        & (unit < width - experts)[:, None]
    ).astype(bf16)
    normed_all, scaled_all, slope_all, mixed_sum, hidden_state, normed = stream(
        attn_part,
        my_rows(tokens),
        ffn_gain[None, :],
        grad_all,
        expert_gate.transpose(0, 2, 1).reshape(local_experts * units, model),
        expert_up.transpose(0, 2, 1).reshape(local_experts * units, model),
        expert_down.reshape(local_experts * units, model),
        shared_parts,
        router_pair,
        segments,
        units,
        experts,
        chunks,
    )
    inverse_second = norm_scale(hidden_state)
    d_expert_gate, d_expert_up, d_expert_down, d_shared = weight_grads(
        normed_all, grad_all, slope_all, scaled_all, units, shared_units, exp_count
    )

    output = valid * (hidden_state + mixed_sum[:, :model])
    mixed = lax.all_gather(output.astype(bf16), COLUMN_AXES, axis=0, tiled=True)

    router_probs = jax.nn.softmax(product_bt(normed, router_rows), axis=1)
    share_weight = jax.nn.sigmoid(product(normed, share_vector))
    chosen = jnp.sum(
        (own_routes[:, :, None] == jnp.arange(experts, dtype=jnp.int32)[None, None, :]).astype(f32),
        axis=1,
    )
    grad_router_probs = chosen * mixed_sum[:, 2 * model : 2 * model + experts]
    grad_share_weight = mixed_sum[:, 2 * model + experts]
    grad_logits = (
        router_probs
        * (grad_router_probs - jnp.sum(grad_router_probs * router_probs, axis=1, keepdims=True))
    ).astype(bf16)
    grad_share_logit = (grad_share_weight * share_weight * (1.0 - share_weight)).astype(bf16)
    grad_normed = (
        mixed_sum[:, model : 2 * model]
        + product(grad_logits, router_rows)
        + grad_share_logit.astype(f32)[:, None] * share_vector.astype(f32)[None, :]
    )
    norm_rows, d_gain_experts = norm_back(grad_normed, hidden_state, inverse_second, ffn_gain)
    grad_hidden = grad_out_low.astype(f32) + norm_rows
    hidden_half = lax.all_gather(grad_hidden.astype(bf16), SAME_X, axis=0, tiled=True)
    router_grads = product_at(
        jnp.concatenate([grad_logits, grad_share_logit[:, None]], axis=1), normed
    )
    extras = jnp.concatenate(
        [
            router_grads,
            d_gain_experts[None, :],
            jnp.broadcast_to(jnp.sum(output * output), (1, model)),
            jnp.zeros((5, model), f32),
        ]
    )
    extras = extras.reshape(-1, heads_z, 2, block).transpose(2, 1, 0, 3)
    hidden_half, d_shared = lax.optimization_barrier((hidden_half, d_shared))
    arrived = lax.all_to_all(d_shared, ROW_AXES, 0, 0, tiled=True).astype(f32)
    d_shared_gate, d_shared_up, d_shared_down = (
        arrived[:, k * shared_units : (k + 1) * shared_units].reshape(
            exp_count * shared_units, block
        )
        for k in range(3)
    )
    d_shared_gate, d_shared_up = d_shared_gate.T, d_shared_up.T
    grad_attended = product(hidden_half, out_weight).astype(bf16)
    scale = 1.0 / head**0.5
    grad_query, grad_key, grad_value = attend_back(
        info, query_rot, key_values, by_position(grad_attended), attended, log_total, rows
    )
    grad_kv = jnp.concatenate([grad_key, grad_value], axis=2).astype(bf16)
    away = lax.ppermute(grad_kv[1], "x", flip)
    grad_kv = by_owner(
        jnp.concatenate([grad_key[0], grad_value[0]], axis=1) + away.astype(f32)
    )
    grad_qkv = jnp.concatenate(
        [
            rope_back(by_owner(grad_query)) * scale,
            rope_back(grad_kv[:, :head]) * scale,
            grad_kv[:, head:],
        ],
        axis=1,
    ).astype(bf16)
    d_attn = head_grads(first_half, hidden_half, grad_qkv, attended_low, block)
    d_biases = jnp.sum(grad_qkv.astype(f32), axis=0).astype(bf16).reshape(3, 2, head // 2)
    d_biases = jnp.pad(
        d_biases.transpose(1, 0, 2).reshape(2, 1, 3 * head // 2),
        ((0, 0), (0, 15), (0, 4 * head - 3 * head // 2)),
    )
    raw = jnp.concatenate(
        [w.reshape(block, heads_z, head) for w in (w_query, w_key, w_value)], axis=2
    ).transpose(1, 0, 2)
    grad_tokens, d_query, d_key, d_value, d_out, d_bias_row, d_gain_attention, squares, extras = finish(
        product_bt(grad_qkv, attn_weights[:, : 3 * head]).astype(bf16),
        grad_hidden,
        my_rows(tokens),
        d_attn,
        d_biases,
        raw,
        extras,
        attn_gain_own,
        chunks,
    )
    d_bias_row = d_bias_row[0]
    d_gain_attention = jnp.sum(d_gain_attention, axis=1)
    half_head = head // 2

    d_router, d_share_vector = extras[:experts].T, extras[experts]
    d_gain_experts = extras[experts + 1]
    cells = length.astype(f32) * model
    rms_output = jnp.sqrt(extras[experts + 2, 0] / cells)
    rms_grad = jnp.sqrt(jnp.sum(squares) / cells)
    return (
        mixed,
        grad_tokens,
        d_query,
        d_key,
        d_value,
        d_out,
        d_bias_row[:half_head],
        d_bias_row[half_head : 2 * half_head],
        d_bias_row[2 * half_head : 3 * half_head],
        d_gain_attention,
        d_gain_experts,
        d_router,
        d_share_vector,
        d_shared_gate,
        d_shared_up,
        d_shared_down,
        d_expert_gate.transpose(0, 2, 1),
        d_expert_up.transpose(0, 2, 1),
        d_expert_down,
        rms_output,
        rms_grad,
    )


def specs(row, column):
    both = column + row
    ins = (
        P(row, None),
        P(row, None),
        P(),
        P(row, None),
        P(row, column),
        P(row, column),
        P(row, column),
        P(column, row),
        P(both),
        P(both),
        P(both),
        P(row),
        P(row),
        P(row, None),
        P(row),
        P(row, column),
        P(row, column),
        P(column, row),
        P(row, None, column),
        P(row, None, column),
        P(row, column, None),
    )
    outs = (
        P(row, None),
        P(row, None),
        P(row, column),
        P(row, column),
        P(row, column),
        P(column, row),
        P(both),
        P(both),
        P(both),
        P(row),
        P(row),
        P(row, None),
        P(row),
        P(row, column),
        P(row, column),
        P(column, row),
        P(row, None, column),
        P(row, None, column),
        P(row, column, None),
        P(),
        P(),
    )
    return ins, outs


def solution(mesh):
    if (mesh.shape["exp"], mesh.shape["tp"]) == (8, 4):
        body, row, column = packed, ROW_AXES, COLUMN_AXES
        mesh = Mesh(mesh.devices.reshape(4, 2, 2, 2), ALL_AXES)
    else:
        body, row, column = general, ("exp",), ("tp",)
    ins, outs = specs(row, column)
    return jax.shard_map(body, mesh=mesh, in_specs=ins, out_specs=outs, check_vma=False)
```

```python
import functools

import jax
import jax.numpy as jnp
import numpy as np
from jax import lax
from jax.experimental import pallas as pl
from jax.experimental.pallas import tpu as pltpu
from jax.sharding import Mesh
from jax.sharding import PartitionSpec as P

HEAD_DIM = 128
SLOT = 4096


EPSILON = 1e-06
ROPE_BASE = 1000000.0
MASKED = -1e30


def shifted(shard, axis, by):
    length = lax.axis_size(axis)
    pairs = [(i, i + by) for i in range(length) if 0 <= i + by < length]
    return lax.ppermute(shard, axis, pairs)


def rope_tables(positions, head_dim):
    half_dim = head_dim // 2
    frequency = ROPE_BASE ** (-(jnp.arange(half_dim, dtype=jnp.float32) * 2.0) / head_dim)
    angles = positions.astype(jnp.float32)[:, None] * frequency[None, :]
    cosine = jnp.concatenate([jnp.cos(angles), jnp.cos(angles)], axis=1)
    sine_table = jnp.concatenate([jnp.sin(angles), jnp.sin(angles)], axis=1)
    return (cosine, sine_table)


def rotate(values, cosine, sine_table):
    half_dim = values.shape[-1] // 2
    turned = jnp.concatenate([-values[..., half_dim:], values[..., :half_dim]], axis=-1)
    return values * cosine[:, None, :] + turned * sine_table[:, None, :]


def rotate_back(grads, cosine, sine_table):
    half_dim = grads.shape[-1] // 2
    moved = grads * sine_table[:, None, :]
    return grads * cosine[:, None, :] + jnp.concatenate(
        [moved[..., half_dim:], -moved[..., :half_dim]], axis=-1
    )


def product(left, right):
    return jnp.dot(left, right, preferred_element_type=jnp.float32)


def product_bt(left, right):
    return lax.dot_general(
        left, right, (((1,), (1,)), ((), ())), preferred_element_type=jnp.float32
    )


def product_at(left, right):
    return lax.dot_general(
        left, right, (((0,), (0,)), ((), ())), preferred_element_type=jnp.float32
    )


def norm_scale(values):
    return lax.rsqrt(jnp.mean(values * values, axis=1, keepdims=True) + EPSILON)


def norm_back(grad_normed, values, inverse, gain):
    scaled = values * inverse
    pushed = grad_normed * gain
    back_rows = inverse * (pushed - scaled * jnp.mean(pushed * scaled, axis=1, keepdims=True))
    return (back_rows, jnp.sum(grad_normed * scaled, axis=0))


def silu_grad(values):
    sigma = jax.nn.sigmoid(values)
    return sigma * (1.0 + values * (1.0 - sigma))


def general(
    tokens,
    cotangent,
    lengths,
    routes,
    w_query,
    w_key,
    w_value,
    w_out,
    b_query,
    b_key,
    b_value,
    gain_attention,
    gain_experts,
    w_router,
    w_shared_gate,
    shared_gate,
    shared_up,
    shared_down,
    expert_gate,
    expert_up,
    expert_down,
):
    exp_count = lax.axis_size("exp")
    exp_index = lax.axis_index("exp")
    tp_count = lax.axis_size("tp")
    tp_index = lax.axis_index("tp")
    row_count, model_width = tokens.shape
    local_experts = expert_gate.shape[0]
    expert_count = local_experts * exp_count
    top_count = routes.shape[1]
    capacity = 2 * row_count * top_count // expert_count
    quarter = capacity // tp_count
    head_dim = HEAD_DIM
    heads_here = w_query.shape[1] // head_dim
    group_size = SLOT // row_count
    scale = 1.0 / head_dim**0.5

    def own_slots(whole_rows):
        return lax.dynamic_slice_in_dim(whole_rows, tp_index * quarter, quarter, 2)

    def place_slots(part_rows):
        empty_rows = jnp.zeros((exp_count, local_experts, capacity, model_width), part_rows.dtype)
        return lax.dynamic_update_slice_in_dim(empty_rows, part_rows, tp_index * quarter, 2)

    gathered = (
        lax.all_gather(w_query, "exp", axis=0, tiled=True),
        lax.all_gather(w_key, "exp", axis=0, tiled=True),
        lax.all_gather(w_value, "exp", axis=0, tiled=True),
        lax.all_gather(w_out, "exp", axis=1, tiled=True),
        lax.all_gather(b_query, "exp", axis=0, tiled=True),
        lax.all_gather(b_key, "exp", axis=0, tiled=True),
        lax.all_gather(b_value, "exp", axis=0, tiled=True),
        lax.all_gather(gain_attention, "exp", axis=0, tiled=True),
        lax.all_gather(gain_experts, "exp", axis=0, tiled=True),
        lax.all_gather(w_router, "exp", axis=0, tiled=True),
        lax.all_gather(w_shared_gate, "exp", axis=0, tiled=True),
        lax.all_gather(shared_gate, "exp", axis=0, tiled=True),
        lax.all_gather(shared_up, "exp", axis=0, tiled=True),
        lax.all_gather(shared_down, "exp", axis=1, tiled=True),
    )
    (
        query_full,
        key_full,
        value_full,
        out_full,
        query_bias,
        key_bias,
        value_bias,
        attn_gain,
        ffn_gain,
        router_full,
        share_vector,
        share_gate_full,
        share_up_full,
        share_down_full,
    ) = gathered
    attn_gain = attn_gain.astype(jnp.float32)
    ffn_gain = ffn_gain.astype(jnp.float32)
    first_row = exp_index * row_count
    slot_index = first_row // SLOT
    offset = first_row % SLOT
    positions = offset + jnp.arange(row_count, dtype=jnp.int32)
    length = jnp.sum(
        jnp.where(jnp.arange(lengths.shape[0], dtype=jnp.int32) == slot_index, lengths, 0)
    )
    valid_rows = (positions < length).astype(jnp.float32)
    cosine, sine_table = rope_tables(positions, head_dim)
    input_rows = tokens.astype(jnp.float32)
    inverse_first = norm_scale(input_rows)
    normed_first = (input_rows * inverse_first * attn_gain).astype(jnp.bfloat16)
    query_lin = product(normed_first, query_full) + query_bias.astype(jnp.float32)
    key_lin = product(normed_first, key_full) + key_bias.astype(jnp.float32)
    value_lin = product(normed_first, value_full) + value_bias.astype(jnp.float32)
    query_rot = rotate(
        query_lin.reshape(row_count, heads_here, head_dim), cosine, sine_table
    ).astype(jnp.bfloat16)
    key_rot = rotate(key_lin.reshape(row_count, heads_here, head_dim), cosine, sine_table).astype(
        jnp.bfloat16
    )
    value_low = value_lin.reshape(row_count, heads_here, head_dim).astype(jnp.bfloat16)
    key_list = [key_rot]
    value_list = [value_low]
    for distance in range(1, group_size):
        earlier_keys, earlier_values = shifted((key_rot, value_low), "exp", distance)
        key_list.append(earlier_keys)
        value_list.append(earlier_values)
    all_keys = jnp.concatenate(key_list, axis=0)
    all_values = jnp.concatenate(value_list, axis=0)
    key_index = jnp.arange(group_size * row_count, dtype=jnp.int32)
    key_pos = offset - key_index // row_count * row_count + key_index % row_count
    allowed = (
        (key_pos[None, :] >= 0)
        & (key_pos[None, :] <= positions[:, None])
        & (key_pos[None, :] < length)
    )
    scores = (
        jnp.einsum("qhd,khd->hqk", query_rot, all_keys, preferred_element_type=jnp.float32) * scale
    )
    scores = jnp.where(allowed[None, :, :], scores, MASKED)
    peak_score = jnp.max(scores, axis=2, keepdims=True)
    weights = jnp.exp(scores - peak_score)
    total_weight = jnp.sum(weights, axis=2, keepdims=True)
    log_total = peak_score + jnp.log(total_weight)
    attn_probs = (weights / total_weight).astype(jnp.bfloat16)
    attended = jnp.einsum(
        "hqk,khd->qhd", attn_probs, all_values, preferred_element_type=jnp.float32
    )
    attended = attended.reshape(row_count, heads_here * head_dim).astype(jnp.bfloat16)
    attn_sum = lax.psum(product(attended, out_full).astype(jnp.bfloat16), "tp").astype(jnp.float32)
    hidden_state = input_rows + attn_sum
    inverse_second = norm_scale(hidden_state)
    normed = (hidden_state * inverse_second * ffn_gain).astype(jnp.bfloat16)
    logits = product(normed, router_full)
    router_probs = jax.nn.softmax(logits, axis=1)
    chosen = (
        routes[:, :, None] == jnp.arange(expert_count, dtype=jnp.int32)[None, None, :]
    ).astype(jnp.float32)
    gates = jnp.sum(chosen * router_probs[:, None, :], axis=2)
    share_weight = jax.nn.sigmoid(product(normed, share_vector))
    share_pre = product(normed, share_gate_full)
    share_lin = product(normed, share_up_full)
    share_hidden = (jax.nn.silu(share_pre) * share_lin).astype(jnp.bfloat16)
    share_out = product(share_hidden, share_down_full)
    flat_routes = routes.reshape(-1)
    pair_count = row_count * top_count
    pick_table = (
        flat_routes[:, None] == jnp.arange(expert_count, dtype=jnp.int32)[None, :]
    ).astype(jnp.int32)
    rank_in_expert = jnp.sum((jnp.cumsum(pick_table, axis=0) - 1) * pick_table, axis=1)
    target = flat_routes * capacity + rank_in_expert
    slot_pair = (
        jnp.full((expert_count * capacity,), pair_count, jnp.int32)
        .at[target]
        .set(jnp.arange(pair_count, dtype=jnp.int32))
    )
    slot_token = jnp.where(slot_pair < pair_count, slot_pair // top_count, row_count)
    padded_rows = jnp.concatenate([normed, jnp.zeros((1, model_width), jnp.bfloat16)], axis=0)
    outgoing = padded_rows[slot_token].reshape(exp_count, local_experts, capacity, model_width)
    sending = own_slots(outgoing)
    working = lax.all_gather(
        lax.all_to_all(sending, "exp", split_axis=0, concat_axis=0, tiled=True),
        "tp",
        axis=2,
        tiled=True,
    )
    gate_pre = jnp.einsum(
        "sxcd,xdf->sxcf", working, expert_gate, preferred_element_type=jnp.float32
    )
    up_pre = jnp.einsum("sxcd,xdf->sxcf", working, expert_up, preferred_element_type=jnp.float32)
    inner = (jax.nn.silu(gate_pre) * up_pre).astype(jnp.bfloat16)
    result_rows = jnp.einsum(
        "sxcf,xfd->sxcd", inner, expert_down, preferred_element_type=jnp.float32
    )
    result_rows = lax.psum_scatter(
        result_rows.astype(jnp.bfloat16), "tp", scatter_dimension=2, tiled=True
    ).astype(jnp.float32)
    back_rows = lax.all_to_all(
        result_rows.astype(jnp.bfloat16), "exp", split_axis=0, concat_axis=0, tiled=True
    ).astype(result_rows.dtype)
    returned = back_rows
    returned = place_slots(returned)
    expert_rows = returned.reshape(expert_count * capacity, model_width)[target].reshape(
        row_count, top_count, model_width
    )
    mixture = jnp.einsum("tk,tkd->td", gates, expert_rows) + share_weight[:, None] * share_out
    mixture = lax.psum(mixture.astype(jnp.bfloat16), "tp").astype(jnp.float32)
    output = valid_rows[:, None] * (hidden_state + mixture)
    grad_out = cotangent.astype(jnp.float32) * valid_rows[:, None]
    share_grad = (grad_out * share_weight[:, None]).astype(jnp.bfloat16)
    grad_share_hidden = (
        product_bt(share_grad, share_down_full).astype(jnp.bfloat16).astype(jnp.float32)
    )
    grad_share_pre = (grad_share_hidden * share_lin * silu_grad(share_pre)).astype(jnp.bfloat16)
    grad_share_lin = (grad_share_hidden * jax.nn.silu(share_pre)).astype(jnp.bfloat16)
    d_shared_down = product_at(share_hidden, share_grad)
    d_shared_gate = product_at(normed, grad_share_pre)
    d_shared_up = product_at(normed, grad_share_lin)
    back_normed = product_bt(grad_share_pre, share_gate_full) + product_bt(
        grad_share_lin, share_up_full
    )
    gate_part = jnp.einsum("td,tkd->tk", grad_out, expert_rows)
    share_part = jnp.sum(grad_out * share_out, axis=1)
    pair_grads = (
        (grad_out[:, None, :] * gates[:, :, None])
        .astype(jnp.bfloat16)
        .reshape(pair_count, model_width)
    )
    padded_grads = jnp.concatenate([pair_grads, jnp.zeros((1, model_width), jnp.bfloat16)], axis=0)
    outgoing_grads = padded_grads[slot_pair].reshape(
        exp_count, local_experts, capacity, model_width
    )
    sending_grads = own_slots(outgoing_grads)
    arrived_grads, arrived_rows = (
        lax.all_to_all(sending_grads, "exp", split_axis=0, concat_axis=0, tiled=True),
        lax.all_to_all(sending, "exp", split_axis=0, concat_axis=0, tiled=True),
    )
    arrived_grads, arrived_rows = (
        lax.all_gather(arrived_grads, "tp", axis=2, tiled=True),
        lax.all_gather(arrived_rows, "tp", axis=2, tiled=True),
    )
    gate_pre = jnp.einsum(
        "sxcd,xdf->sxcf", arrived_rows, expert_gate, preferred_element_type=jnp.float32
    )
    up_pre = jnp.einsum(
        "sxcd,xdf->sxcf", arrived_rows, expert_up, preferred_element_type=jnp.float32
    )
    inner = (jax.nn.silu(gate_pre) * up_pre).astype(jnp.bfloat16)
    grad_inner = jnp.einsum(
        "sxcd,xfd->sxcf", arrived_grads, expert_down, preferred_element_type=jnp.float32
    )
    grad_inner = grad_inner.astype(jnp.bfloat16).astype(jnp.float32)
    grad_gate_pre = (grad_inner * up_pre * silu_grad(gate_pre)).astype(jnp.bfloat16)
    grad_up_pre = (grad_inner * jax.nn.silu(gate_pre)).astype(jnp.bfloat16)
    rows_back = jnp.einsum(
        "sxcf,xdf->sxcd", grad_gate_pre, expert_gate, preferred_element_type=jnp.float32
    )
    rows_back = rows_back + jnp.einsum(
        "sxcf,xdf->sxcd", grad_up_pre, expert_up, preferred_element_type=jnp.float32
    )
    rows_back = lax.psum_scatter(
        rows_back.astype(jnp.bfloat16), "tp", scatter_dimension=2, tiled=True
    ).astype(jnp.float32)
    returned_grads = lax.all_to_all(
        rows_back.astype(jnp.bfloat16), "exp", split_axis=0, concat_axis=0, tiled=True
    ).astype(rows_back.dtype)
    returned_grads = place_slots(returned_grads)
    d_expert_gate = jnp.einsum(
        "sxcd,sxcf->xdf", arrived_rows, grad_gate_pre, preferred_element_type=jnp.float32
    )
    d_expert_up = jnp.einsum(
        "sxcd,sxcf->xdf", arrived_rows, grad_up_pre, preferred_element_type=jnp.float32
    )
    d_expert_down = jnp.einsum(
        "sxcf,sxcd->xfd", inner, arrived_grads, preferred_element_type=jnp.float32
    )
    grad_rows = returned_grads.reshape(expert_count * capacity, model_width)[target].reshape(
        row_count, top_count, model_width
    )
    back_normed = back_normed + jnp.sum(grad_rows, axis=1)
    scalar_part = jnp.concatenate([gate_part, share_part[:, None]], axis=1)
    summed_normed, scalar_sum = (
        lax.psum(back_normed.astype(jnp.bfloat16), "tp").astype(jnp.float32),
        lax.psum(scalar_part.astype(jnp.bfloat16), "tp").astype(jnp.float32),
    )
    grad_gates = scalar_sum[:, :top_count]
    grad_share_weight = scalar_sum[:, top_count]
    grad_router_probs = jnp.einsum("tk,tke->te", grad_gates, chosen)
    grad_logits = (
        router_probs
        * (grad_router_probs - jnp.sum(grad_router_probs * router_probs, axis=1, keepdims=True))
    ).astype(jnp.bfloat16)
    grad_share_logit = (grad_share_weight * share_weight * (1.0 - share_weight)).astype(
        jnp.bfloat16
    )
    d_router = product_at(normed, grad_logits)
    d_share_vector = product(grad_share_logit, normed)
    grad_normed = (
        summed_normed
        + product_bt(grad_logits, router_full)
        + grad_share_logit.astype(jnp.float32)[:, None] * share_vector.astype(jnp.float32)[None, :]
    )
    norm_rows, d_gain_experts = norm_back(grad_normed, hidden_state, inverse_second, ffn_gain)
    grad_hidden = grad_out + norm_rows
    grad_hidden_low = grad_hidden.astype(jnp.bfloat16)
    d_out_weight = product_at(attended, grad_hidden_low)
    grad_attended = (
        product_bt(grad_hidden_low, out_full)
        .astype(jnp.bfloat16)
        .reshape(row_count, heads_here, head_dim)
    )
    scores = (
        jnp.einsum("qhd,khd->hqk", query_rot, all_keys, preferred_element_type=jnp.float32) * scale
    )
    scores = jnp.where(allowed[None, :, :], scores, MASKED)
    probs_again = jnp.exp(scores - log_total)
    probs_low = probs_again.astype(jnp.bfloat16)
    grad_values = jnp.einsum(
        "hqk,qhd->khd", probs_low, grad_attended, preferred_element_type=jnp.float32
    )
    grad_probs = jnp.einsum(
        "qhd,khd->hqk", grad_attended, all_values, preferred_element_type=jnp.float32
    )
    grad_scores = (
        probs_again * (grad_probs - jnp.sum(probs_again * grad_probs, axis=2, keepdims=True))
    ).astype(jnp.bfloat16)
    grad_query = (
        jnp.einsum("hqk,khd->qhd", grad_scores, all_keys, preferred_element_type=jnp.float32)
        * scale
    )
    grad_keys = (
        jnp.einsum("hqk,qhd->khd", grad_scores, query_rot, preferred_element_type=jnp.float32)
        * scale
    )
    own_key_grads = grad_keys[:row_count]
    own_value_grads = grad_values[:row_count]
    for distance in range(1, group_size):
        lower_row = distance * row_count
        later_keys, later_values = (
            shifted(
                grad_keys[lower_row : lower_row + row_count].astype(jnp.bfloat16), "exp", -distance
            ).astype(jnp.float32),
            shifted(
                grad_values[lower_row : lower_row + row_count].astype(jnp.bfloat16),
                "exp",
                -distance,
            ).astype(jnp.float32),
        )
        own_key_grads = own_key_grads + later_keys
        own_value_grads = own_value_grads + later_values
    grad_query_lin = (
        rotate_back(grad_query, cosine, sine_table)
        .reshape(row_count, heads_here * head_dim)
        .astype(jnp.bfloat16)
    )
    grad_key_lin = (
        rotate_back(own_key_grads, cosine, sine_table)
        .reshape(row_count, heads_here * head_dim)
        .astype(jnp.bfloat16)
    )
    grad_value_lin = own_value_grads.reshape(row_count, heads_here * head_dim).astype(jnp.bfloat16)
    d_query = product_at(normed_first, grad_query_lin)
    d_key = product_at(normed_first, grad_key_lin)
    d_value = product_at(normed_first, grad_value_lin)
    d_query_bias = jnp.sum(grad_query_lin.astype(jnp.float32), axis=0)
    d_key_bias = jnp.sum(grad_key_lin.astype(jnp.float32), axis=0)
    d_value_bias = jnp.sum(grad_value_lin.astype(jnp.float32), axis=0)
    back_first = (
        product_bt(grad_query_lin, query_full)
        + product_bt(grad_key_lin, key_full)
        + product_bt(grad_value_lin, value_full)
    )
    back_first = lax.psum(back_first.astype(jnp.bfloat16), "tp").astype(jnp.float32)
    first_rows, d_gain_attention = norm_back(back_first, input_rows, inverse_first, attn_gain)
    grad_input = grad_hidden + first_rows
    reduced = (
        lax.psum_scatter(
            d_query.astype(jnp.bfloat16), "exp", scatter_dimension=0, tiled=True
        ).astype(jnp.float32),
        lax.psum_scatter(d_key.astype(jnp.bfloat16), "exp", scatter_dimension=0, tiled=True).astype(
            jnp.float32
        ),
        lax.psum_scatter(
            d_value.astype(jnp.bfloat16), "exp", scatter_dimension=0, tiled=True
        ).astype(jnp.float32),
        lax.psum_scatter(
            d_out_weight.astype(jnp.bfloat16), "exp", scatter_dimension=1, tiled=True
        ).astype(jnp.float32),
        lax.psum_scatter(
            d_query_bias.astype(jnp.bfloat16), "exp", scatter_dimension=0, tiled=True
        ).astype(jnp.float32),
        lax.psum_scatter(
            d_key_bias.astype(jnp.bfloat16), "exp", scatter_dimension=0, tiled=True
        ).astype(jnp.float32),
        lax.psum_scatter(
            d_value_bias.astype(jnp.bfloat16), "exp", scatter_dimension=0, tiled=True
        ).astype(jnp.float32),
        lax.psum_scatter(
            d_gain_attention.astype(jnp.bfloat16), "exp", scatter_dimension=0, tiled=True
        ).astype(jnp.float32),
        lax.psum_scatter(
            d_gain_experts.astype(jnp.bfloat16), "exp", scatter_dimension=0, tiled=True
        ).astype(jnp.float32),
        lax.psum_scatter(
            d_router.astype(jnp.bfloat16), "exp", scatter_dimension=0, tiled=True
        ).astype(jnp.float32),
        lax.psum_scatter(
            d_share_vector.astype(jnp.bfloat16), "exp", scatter_dimension=0, tiled=True
        ).astype(jnp.float32),
        lax.psum_scatter(
            d_shared_gate.astype(jnp.bfloat16), "exp", scatter_dimension=0, tiled=True
        ).astype(jnp.float32),
        lax.psum_scatter(
            d_shared_up.astype(jnp.bfloat16), "exp", scatter_dimension=0, tiled=True
        ).astype(jnp.float32),
        lax.psum_scatter(
            d_shared_down.astype(jnp.bfloat16), "exp", scatter_dimension=1, tiled=True
        ).astype(jnp.float32),
    )
    square_sums = lax.psum((jnp.sum(output * output), jnp.sum(grad_input * grad_input)), "exp")
    count_cells = jnp.sum(lengths).astype(jnp.float32) * model_width
    rms_output = jnp.sqrt(square_sums[0] / count_cells)
    rms_grad = jnp.sqrt(square_sums[1] / count_cells)
    return (
        output.astype(jnp.bfloat16),
        grad_input.astype(jnp.bfloat16),
        reduced[0],
        reduced[1],
        reduced[2],
        reduced[3],
        reduced[4],
        reduced[5],
        reduced[6],
        reduced[7],
        reduced[8],
        reduced[9],
        reduced[10],
        reduced[11],
        reduced[12],
        reduced[13],
        d_expert_gate,
        d_expert_up,
        d_expert_down,
        rms_output,
        rms_grad,
    )


def flat(pieces):
    return jnp.concatenate([p.reshape(-1) for p in pieces])


def key_window(info_ref, block, keys):
    return lax.rem(block + info_ref[0], 2), pl.ds(pl.multiple_of(block // 2 * keys, keys), keys)


def attend_back_kernel(
    info_ref, q_ref, kv_ref, do_ref, o_ref, lse_ref, dq_ref, dk_ref, dv_ref, *, tile, keys, rows
):
    step = pl.program_id(0)
    per_block = rows // tile
    base = (2 * (step // per_block) + info_ref[0]) * rows + (step % per_block) * tile

    @pl.when(step == 0)
    def _():
        dk_ref[...] = jnp.zeros_like(dk_ref)
        dv_ref[...] = jnp.zeros_like(dv_ref)

    query = q_ref[...]
    grad = do_ref[...]
    log_total = lse_ref[:, 0:1]
    delta = jnp.sum(grad.astype(jnp.float32) * o_ref[...], axis=1, keepdims=True)
    row_pos = base + lax.broadcasted_iota(jnp.int32, (tile, 1), 0)
    limit = jnp.minimum(row_pos, info_ref[1] - 1)
    column = lax.broadcasted_iota(jnp.int32, (tile, keys), 1)

    def body(j, acc):
        side, window = key_window(info_ref, j, keys)
        key = kv_ref[side, window, :HEAD_DIM]
        scores = product_bt(query, key) * (1.0 / HEAD_DIM**0.5)
        scores = jnp.where(column <= limit - j * keys, scores, MASKED)
        probs = jnp.exp(scores - log_total)
        dv_ref[side, window, :] += product_at(probs.astype(jnp.bfloat16), grad)
        grad_probs = product_bt(grad, kv_ref[side, window, HEAD_DIM:])
        grad_scores = (probs * (grad_probs - delta)).astype(jnp.bfloat16)
        dk_ref[side, window, :] += product_at(grad_scores, query)
        return acc + product(grad_scores, key)

    count = (base + tile + keys - 1) // keys
    dq_ref[...] = lax.fori_loop(0, count, body, jnp.zeros((tile, HEAD_DIM), jnp.float32))


def attend_back(info, query, key_values, grad, out, log_total, rows):
    count = query.shape[0]
    tile = 256
    half = key_values.shape[:2] + (HEAD_DIM,)
    whole = pl.BlockSpec(half, lambda i: (0, 0, 0))
    both = pl.BlockSpec(key_values.shape, lambda i: (0, 0, 0))
    part = pl.BlockSpec((tile, HEAD_DIM), lambda i: (i, 0))
    return pl.pallas_call(
        functools.partial(attend_back_kernel, tile=tile, keys=rows, rows=rows),
        grid=(count // tile,),
        in_specs=[pl.BlockSpec(memory_space=pltpu.SMEM), part, both, part, part, part],
        out_specs=[part, whole, whole],
        out_shape=[
            jax.ShapeDtypeStruct((count, HEAD_DIM), jnp.float32),
            jax.ShapeDtypeStruct(half, jnp.float32),
            jax.ShapeDtypeStruct(half, jnp.float32),
        ],
        compiler_params=pltpu.CompilerParams(vmem_limit_bytes=40 * 2**20),
        cost_estimate=pl.CostEstimate(
            flops=10 * count * count * HEAD_DIM,
            bytes_accessed=12 * 2**20,
            transcendentals=count * count,
        ),
    )(info, query, key_values, grad, out, log_total)


ROW_AXES = ("z", "x")
COLUMN_AXES = ("y", "c")
ALL_AXES = ("z", "x", "y", "c")
CHUNK_AXES = ("c", "y", "x", "z")
SAME_X = ("c", "y", "z")


def front_kernel(
    own_ref,
    parts_ref,
    leaving_ref,
    rows_ref,
    weights_ref,
    all_ref,
    send,
    send_z,
    recv,
    send_w,
    recv_w,
    send_g,
    recv_g,
    here,
):
    z, x, y, c = (lax.axis_index(name) for name in ALL_AXES)
    z_count = lax.axis_size("z")
    chunks = own_ref.shape[0]
    half = own_ref.shape[2] // 2
    left, right = pl.ds(0, half), pl.ds(half, leaving_ref.shape[2] - half)
    flip = {"x": {"x": 1 - x}, "y": {"y": 1 - y}, "c": {"c": 1 - c}}

    def up(distance):
        return {"z": lax.rem(z + distance, z_count)}

    def remote(src, dst, send_sem, recv_sem, device):
        return pltpu.make_async_remote_copy(
            src_ref=src,
            dst_ref=dst,
            send_sem=send_sem,
            recv_sem=recv_sem,
            device_id=device,
            device_id_type=pl.DeviceIdType.MESH,
        )

    def spread_z(k, d):
        block = rows_ref.at[c, y, z, k]
        return remote(own_ref.at[k], block, send_z.at[d - 1, k], recv.at[1 + d, k], up(d))

    def spread_y(k):
        block = rows_ref.at[c, y, :, k]
        return remote(block, block, send.at[0, k], recv.at[0, k], flip["y"])

    def spread_c(k):
        block = rows_ref.at[c, :, :, k]
        return remote(block, block, send.at[1, k], recv.at[1, k], flip["c"])

    def weights_z(d):
        there = lax.rem(z + d, z_count)
        return remote(
            parts_ref.at[there], weights_ref.at[z, x], send_w.at[d], recv_w.at[d], up(d)
        )

    def weights_x():
        block = weights_ref.at[:, x]
        return remote(block, block, send_w.at[0], recv_w.at[0], flip["x"])

    def grads(slot, k, src, dst, device):
        return remote(src, dst, send_g.at[slot, k], recv_g.at[slot, k], device)

    def grads_z(k):
        return [
            grads(4 + d, k, leaving_ref.at[k], all_ref.at[c, y, x, z, k], up(d))
            for d in range(1, 4)
        ]

    def grads_2(k):
        a = all_ref.at[c, y, x, :, k, :, left]
        b = all_ref.at[c, y, x, :, k, :, right]
        return grads(0, k, a, a, flip["x"]), grads(1, k, b, b, flip["y"])

    def grads_3(k):
        a = all_ref.at[c, y, :, :, k, :, left]
        b = all_ref.at[c, :, x, :, k, :, right]
        return grads(2, k, a, a, flip["y"]), grads(3, k, b, b, flip["x"])

    def grads_c(k):
        a = all_ref.at[c, :, :, :, k]
        return (grads(4, k, a, a, flip["c"]),)

    def start(copies):
        for copy in copies:
            copy.start()

    def finish(copies):
        for copy in copies:
            copy.wait()

    barrier = pltpu.get_barrier_semaphore()
    for device in (flip["x"], flip["y"], flip["c"], up(1), up(2), up(3)):
        pl.semaphore_signal(
            barrier, inc=1, device_id=device, device_id_type=pl.DeviceIdType.MESH
        )
    keep = [
        pltpu.make_async_copy(own_ref, rows_ref.at[c, y, z], here.at[0]),
        pltpu.make_async_copy(parts_ref.at[z], weights_ref.at[z, x], here.at[1]),
        pltpu.make_async_copy(leaving_ref, all_ref.at[c, y, x, z], here.at[2]),
    ]
    start(keep)
    pl.semaphore_wait(barrier, 6)
    def first_z(k):
        return [spread_z(k, d) for d in range(1, 4)]

    def all_weights_z():
        return [weights_z(d) for d in range(1, 4)]

    start(first_z(0))
    start(grads_z(0))
    finish(keep)
    for k in range(chunks):
        finish(first_z(k))
        if k + 1 < chunks:
            start(first_z(k + 1))
        spread_y(k).start()
        if k == 1:
            finish(all_weights_z())
            weights_x().start()
        if k > 0:
            spread_y(k - 1).wait()
            spread_c(k - 1).start()
        finish(grads_z(k))
        if k == 0:
            start(all_weights_z())
        if k + 1 < chunks:
            start(grads_z(k + 1))
        start(grads_2(k))
        if k > 0:
            finish(grads_2(k - 1))
            start(grads_3(k - 1))
        if k > 1:
            finish(grads_3(k - 2))
            start(grads_c(k - 2))
    spread_y(chunks - 1).wait()
    spread_c(chunks - 1).start()
    finish(grads_2(chunks - 1))
    start(grads_3(chunks - 1))
    for k in (chunks - 2, chunks - 1):
        finish(grads_3(k))
        start(grads_c(k))
    for k in range(chunks):
        spread_c(k).wait()
        finish(grads_c(k))
    weights_x().wait()


def front(rows, parts, leaving, chunks=4):
    own, model = rows.shape
    wide = leaving.shape[1]
    piece = own // chunks
    zs = lax.axis_size("z")
    anywhere = pl.BlockSpec(memory_space=pl.ANY)
    dma = pltpu.SemaphoreType.DMA
    gathered, weights, spread = pl.pallas_call(
        front_kernel,
        in_specs=[anywhere] * 3,
        out_specs=[anywhere] * 3,
        out_shape=[
            jax.ShapeDtypeStruct((2, 2, zs, chunks, piece, model), rows.dtype),
            jax.ShapeDtypeStruct((zs, 2) + parts.shape[1:], parts.dtype),
            jax.ShapeDtypeStruct((2, 2, 2, zs, chunks, piece, wide), rows.dtype),
        ],
        scratch_shapes=[
            dma((2, chunks)),
            dma((3, chunks)),
            dma((5, chunks)),
            dma((4,)),
            dma((4,)),
            dma((8, chunks)),
            dma((8, chunks)),
            dma((3,)),
        ],
        compiler_params=pltpu.CompilerParams(
            collective_id=0, has_side_effects=True, vmem_limit_bytes=16 * 2**20
        ),
    )(rows.reshape(chunks, piece, model), parts, leaving.reshape(chunks, piece, wide))
    return (
        gathered.reshape(4 * zs * own, model),
        weights,
        spread.reshape(8 * zs * own, wide),
    )


def middle_kernel(
    length_ref,
    rows_ref,
    w_ref,
    row_ref,
    block_ref,
    sh_ref,
    q_ref,
    kv_ref,
    att_ref,
    lse_ref,
    part_ref,
    joined_ref,
    shared_ref,
    peaks,
    totals,
    once,
    once_in,
    here,
    *,
    rows,
):
    z, x, y, c = (lax.axis_index(name) for name in ALL_AXES)
    z_count = lax.axis_size("z")
    e_count = 2 * z_count
    head = HEAD_DIM
    count, model = rows_ref.shape
    block = model // e_count
    own = rows // 4
    tile = 2 * own
    flip = {"x": {"x": 1 - x}, "y": {"y": 1 - y}, "c": {"c": 1 - c}}

    def up(distance):
        return {"z": lax.rem(z + distance, z_count)}

    def copy_to(src, dst, send_sem, recv_sem, device):
        return pltpu.make_async_remote_copy(
            src_ref=src,
            dst_ref=dst,
            send_sem=send_sem,
            recv_sem=recv_sem,
            device_id=device,
            device_id_type=pl.DeviceIdType.MESH,
        )

    def share(d, other):
        z_to, x_to = lax.rem(z + d, z_count), 1 - x if other else x
        i = d + z_count if other else d
        return copy_to(
            sh_ref.at[2 * z_to + x_to],
            shared_ref.at[2 * z + x],
            once.at[i],
            once_in.at[i],
            {"z": z_to, "x": x_to},
        )

    def key_values():
        return copy_to(kv_ref.at[0], kv_ref.at[1], once.at[0], once_in.at[0], flip["x"])

    def start(copies):
        for copy in copies:
            copy.start()

    def finish(copies):
        for copy in copies:
            copy.wait()

    barrier = pltpu.get_barrier_semaphore()
    partners = [flip["x"], flip["y"], flip["c"], up(1), up(2), up(3)]
    partners += [{"z": lax.rem(z + d, z_count), "x": 1 - x} for d in range(1, 4)]
    for device in partners:
        pl.semaphore_signal(
            barrier, inc=1, device_id=device, device_id_type=pl.DeviceIdType.MESH
        )
    keep_share = pltpu.make_async_copy(
        sh_ref.at[2 * z + x], shared_ref.at[2 * z + x], here.at[0]
    )
    keep_share.start()
    for i in range(z_count):
        for j in range(2):
            e = 2 * i + j
            joined_ref[e * block : (e + 1) * block] = w_ref[i, j, :block]
    bias = w_ref[z, 0, pl.ds(block, 16)].astype(jnp.float32) + w_ref[
        z, 1, pl.ds(block, 16)
    ].astype(jnp.float32)
    bias = bias[0:1, : 3 * head]
    lane = lax.broadcasted_iota(jnp.int32, (1, head), 1)
    sign = jnp.where(lane < head // 2, -1.0, 1.0)
    pl.semaphore_wait(barrier, 9)
    shares = [share(d, other) for d in range(4) for other in (False, True) if d or other]

    def project(t, carry):
        lin = product(rows_ref[pl.ds(t * tile, tile), :], joined_ref[:, : 3 * head]) + bias
        for h in range(2):
            s = 2 * t + h
            z_of, y_of, c_of = lax.rem(s, 4), lax.rem(s // 4, 2), s // 8
            place = pl.ds(pl.multiple_of((z_of * 4 + y_of * 2 + c_of) * own, own), own)
            block_cos, block_sin = block_ref[x, 0, pl.ds(s, 1)], block_ref[x, 1, pl.ds(s, 1)]
            cosine = block_cos * row_ref[0] - block_sin * row_ref[1]
            sine = (block_sin * row_ref[0] + block_cos * row_ref[1]) * sign
            part = lin[h * own : (h + 1) * own]
            query, key = part[:, :head], part[:, head : 2 * head]
            query = query * cosine + pltpu.roll(query, head // 2, 1) * sine
            key = key * cosine + pltpu.roll(key, head // 2, 1) * sine
            q_ref[place, :] = query.astype(jnp.bfloat16)
            kv_ref[0, place, :head] = key.astype(jnp.bfloat16)
            kv_ref[0, place, head:] = part[:, 2 * head :].astype(jnp.bfloat16)
        return carry

    lax.fori_loop(0, count // tile, project, 0)
    key_values().start()
    start(shares)
    column = lax.broadcasted_iota(jnp.int32, (tile, rows), 1)

    def scan(i, side, blocks, carry):
        query = q_ref[pl.ds(pl.multiple_of(i * tile, tile), tile), :]
        base = (2 * (i // 2) + x) * rows + lax.rem(i, 2) * tile
        row_pos = base + lax.broadcasted_iota(jnp.int32, (tile, 1), 0)
        limit = jnp.minimum(row_pos, length_ref[0] - 1)
        parity = x if side == 0 else 1 - x

        def body(m, carry):
            peak, total, acc = carry
            window = pl.ds(pl.multiple_of(m * rows, rows), rows)
            scores = product_bt(query, kv_ref[side, window, :head]) * (1.0 / head**0.5)
            scores = jnp.where(column <= limit - (2 * m + parity) * rows, scores, MASKED)
            new_peak = jnp.maximum(peak, jnp.max(scores, axis=1, keepdims=True))
            weights = jnp.exp(scores - new_peak)
            shrink = jnp.exp(peak - new_peak)
            total = shrink * total + jnp.sum(weights, axis=1, keepdims=True)
            acc = shrink * acc + product(
                weights.astype(jnp.bfloat16), kv_ref[side, window, head:]
            )
            return (new_peak, total, acc)

        return lax.fori_loop(0, blocks, body, carry)

    def first_pass(i, carry):
        peak, total, acc = scan(
            i,
            0,
            i // 2 + 1,
            (
                jnp.full((tile, 1), MASKED, jnp.float32),
                jnp.zeros((tile, 1), jnp.float32),
                jnp.zeros((tile, head), jnp.float32),
            ),
        )
        place = pl.ds(pl.multiple_of(i * tile, tile), tile)
        peaks[place, :] = jnp.broadcast_to(peak, (tile, head))
        totals[place, :] = jnp.broadcast_to(total, (tile, head))
        att_ref[place, :] = acc
        return carry

    lax.fori_loop(0, count // tile, first_pass, 0)
    key_values().wait()

    def second_pass(i, carry):
        place = pl.ds(pl.multiple_of(i * tile, tile), tile)
        peak, total, acc = scan(
            i, 1, i // 2 + x, (peaks[place, 0:1], totals[place, 0:1], att_ref[place, :])
        )
        acc = acc / total
        att_ref[place, :] = acc
        lse_ref[place, :] = jnp.broadcast_to(peak + jnp.log(total), (tile, head))
        part = product_bt(acc.astype(jnp.bfloat16), joined_ref[:, 3 * head :]).astype(
            jnp.bfloat16
        )
        for h in range(2):
            z_of, y_of, c_of = i // 2, lax.rem(i, 2), h
            part_ref[c_of * 8 + y_of * 4 + z_of] = part[h * own : (h + 1) * own]
        return carry

    lax.fori_loop(0, count // tile, second_pass, 0)
    finish(shares)
    keep_share.wait()


def middle(length, gathered, weights, row_table, block_table, shared, rows):
    own = rows // 4
    count, model = gathered.shape
    head = HEAD_DIM
    bf16, f32 = jnp.bfloat16, jnp.float32
    anywhere = pl.BlockSpec(memory_space=pl.ANY)
    inside = pl.BlockSpec(memory_space=pltpu.VMEM)
    vm, dma = pltpu.VMEM, pltpu.SemaphoreType.DMA
    shape = jax.ShapeDtypeStruct
    results = pl.pallas_call(
        functools.partial(middle_kernel, rows=rows),
        in_specs=[pl.BlockSpec(memory_space=pltpu.SMEM)] + [inside] * 4 + [anywhere],
        out_specs=[inside] * 6 + [anywhere],
        out_shape=[
            shape((count, head), bf16),
            shape((2, count, 2 * head), bf16),
            shape((count, head), f32),
            shape((count, head), f32),
            shape((count // own, own, model), bf16),
            shape((model, 4 * head), bf16),
            shape(shared.shape, bf16),
        ],
        scratch_shapes=[
            vm((count, head), f32),
            vm((count, head), f32),
            dma((8,)),
            dma((8,)),
            dma((1,)),
        ],
        compiler_params=pltpu.CompilerParams(
            collective_id=3, has_side_effects=True, vmem_limit_bytes=56 * 2**20
        ),
        cost_estimate=pl.CostEstimate(
            flops=10 * count * model * head, bytes_accessed=60 * 2**20, transcendentals=count * count
        ),
    )(
        length,
        gathered,
        weights,
        row_table,
        block_table,
        shared,
    )
    query, key_values, attended, log_total, partial, joined, shared = results
    return (
        query,
        key_values,
        attended,
        log_total,
        partial.reshape(count, model),
        joined,
        shared,
    )


def expert_rows(first, normed, grads, routes, w_ref, d_ref, s_ref, units, experts):
    width = d_ref.shape[0]
    rows = normed.shape[0]
    pre = product_bt(normed, w_ref[...])
    gate_pre = pre[:, :width]
    up_pre = pre[:, width:]
    lane = lax.broadcasted_iota(jnp.int32, (rows, 128), 1)
    router_lane = lane - (128 - experts)
    logits = jnp.where(router_lane >= 0, gate_pre[:, width - 128 :], MASKED)
    expo = jnp.exp(logits - jnp.max(logits, axis=1, keepdims=True))
    probs = expo / jnp.sum(expo, axis=1, keepdims=True)

    def gate_of(expert):
        picked = jnp.sum((routes == expert).astype(jnp.float32), axis=1, keepdims=True)
        return picked * jnp.sum(
            jnp.where(router_lane == expert, probs, 0.0), axis=1, keepdims=True
        )

    share = jax.nn.sigmoid(
        jnp.sum(jnp.where(router_lane == 0, up_pre[:, width - 128 :], 0.0), axis=1, keepdims=True)
    )
    column = lax.broadcasted_iota(jnp.int32, (rows, width), 1)
    scale = jnp.where(column < width - experts, share, 0.0)
    for index in reversed(range(2)):
        scale = jnp.where(column < (index + 1) * units, gate_of(first + index), scale)
    sigma = jax.nn.sigmoid(gate_pre)
    swish = gate_pre * sigma
    hidden = swish * up_pre
    scaled = (hidden * scale).astype(jnp.bfloat16)
    mixture = product(scaled, d_ref[...]).astype(jnp.bfloat16)
    back = product_bt(grads, d_ref[...])
    gate_sums = product((back * hidden).astype(jnp.bfloat16), s_ref[...]).astype(jnp.bfloat16)
    back = back * scale
    grad_gate = (back * up_pre * (sigma * (1.0 + gate_pre * (1.0 - sigma)))).astype(jnp.bfloat16)
    grad_up = (back * swish).astype(jnp.bfloat16)
    pushed = product(grad_gate, w_ref[:width]) + product(grad_up, w_ref[width:])
    return scaled, grad_gate, grad_up, mixture, pushed.astype(jnp.bfloat16), gate_sums


def add_low(*terms):
    total = terms[0].astype(jnp.float32)
    for term in terms[1:]:
        total = total + term.astype(jnp.float32)
    return total.astype(jnp.bfloat16)


def stream_kernel(
    part_ref,
    x_ref,
    gain_ref,
    g_ref,
    eg_ref,
    eu_ref,
    ed_ref,
    sh_ref,
    router_ref,
    s_ref,
    all_ref,
    hs_ref,
    dgu_ref,
    out_ref,
    hidden_ref,
    own_ref,
    lrc_ref,
    lr2_ref,
    lr3_ref,
    lca_ref,
    lcb_ref,
    l2a_ref,
    l2b_ref,
    l3a_ref,
    l3b_ref,
    lza_ref,
    lzb_ref,
    w_ref,
    d_ref,
    n_buf,
    g_buf,
    pa,
    pb,
    ca,
    cb,
    da,
    db,
    ea,
    eb,
    fa,
    fb,
    qa,
    qb,
    sa,
    sb,
    ta,
    tb,
    hs_buf,
    dgu_buf,
    ra,
    rb,
    rc,
    rd,
    re,
    rf,
    send,
    send_z,
    send_r,
    send_c,
    recv_c,
    recv,
    here,
    weigh,
    *,
    units,
    experts,
):
    z, x, y, c = (lax.axis_index(name) for name in ALL_AXES)
    z_count = lax.axis_size("z")
    chunks = x_ref.shape[0]
    model = x_ref.shape[2]
    width = d_ref.shape[0]
    cut = pa.shape[-1]
    half = model // 2
    left, right = pl.ds(0, half), pl.ds(half, half)
    first = 2 * (2 * z + x)
    flip = {"x": {"x": 1 - x}, "y": {"y": 1 - y}, "c": {"c": 1 - c}}

    def up(distance):
        return {"z": lax.rem(z + distance, z_count)}

    def remote(slot, k, src, dst, device):
        return pltpu.make_async_remote_copy(
            src_ref=src,
            dst_ref=dst,
            send_sem=send.at[slot, lax.rem(k, 2)],
            recv_sem=recv.at[slot, k],
            device_id=device,
            device_id_type=pl.DeviceIdType.MESH,
        )

    def spread_z(k, d):
        return pltpu.make_async_remote_copy(
            src_ref=own_ref.at[k],
            dst_ref=all_ref.at[c, y, x, z, k],
            send_sem=send_z.at[d - 1, k],
            recv_sem=recv.at[20 + d, k],
            device_id=up(d),
            device_id_type=pl.DeviceIdType.MESH,
        )

    def heads_c(k):
        return pltpu.make_async_remote_copy(
            src_ref=part_ref.at[1 - c, :, :, k],
            dst_ref=lrc_ref.at[k],
            send_sem=send_r.at[k],
            recv_sem=recv.at[24, k],
            device_id=flip["c"],
            device_id_type=pl.DeviceIdType.MESH,
        )

    def heads_y(k):
        return (remote(17, k, rc.at[lax.rem(k, 2), 1 - y], lr2_ref.at[k], flip["y"]),)

    def heads_z(k):
        copies = []
        for d in range(1, 4):
            there = lax.rem(z + d, z_count)
            copies.append(remote(17 + d, k, re.at[lax.rem(k, 2), there], lr3_ref.at[k, d - 1], up(d)))
        return copies

    def load_hc(k):
        return (
            pltpu.make_async_copy(part_ref.at[c, :, :, k], ra, here.at[15]),
            pltpu.make_async_copy(lrc_ref.at[k], rb, here.at[16]),
        )

    def load_hy(k):
        return (pltpu.make_async_copy(lr2_ref.at[k], rd, here.at[17]),)

    def load_hz(k):
        return (pltpu.make_async_copy(lr3_ref.at[k], rf, here.at[18]),)

    def keep(k):
        return pltpu.make_async_copy(own_ref.at[k], all_ref.at[c, y, x, z, k], here.at[19 + lax.rem(k, 2)])

    def spread_2(k):
        a = all_ref.at[c, y, x, :, k, :, left]
        b = all_ref.at[c, y, x, :, k, :, right]
        return remote(0, k, a, a, flip["x"]), remote(1, k, b, b, flip["y"])

    def spread_3(k):
        a = all_ref.at[c, y, :, :, k, :, left]
        b = all_ref.at[c, :, x, :, k, :, right]
        return remote(2, k, a, a, flip["y"]), remote(3, k, b, b, flip["x"])

    def across(slot, k, src, dst):
        return pltpu.make_async_remote_copy(
            src_ref=src,
            dst_ref=dst,
            send_sem=send_c.at[slot, lax.rem(k, 2)],
            recv_sem=recv_c.at[slot, k],
            device_id=flip["c"],
            device_id_type=pl.DeviceIdType.MESH,
        )

    def spread_c(k):
        copies = []
        for j in range(2):
            for m in range(2):
                a = all_ref.at[c, j, m, :, k]
                copies.append(across(2 * j + m, k, a, a))
        return copies

    def sum_c(k):
        slot = lax.rem(k, 2)
        copies = []
        for j in range(2):
            for m in range(2):
                i = 4 + 2 * j + m
                copies.append(across(i, k, pa.at[slot, 1 - c, j, m], lca_ref.at[k, j, m]))
                copies.append(across(4 + i, k, pb.at[slot, 1 - c, j, m], lcb_ref.at[k, j, m]))
        return copies

    def sum_2(k):
        return (
            remote(7, k, qa.at[lax.rem(k, 2), 1 - y], l2a_ref.at[k], flip["y"]),
            remote(8, k, qb.at[lax.rem(k, 2), :, 1 - x], l2b_ref.at[k], flip["x"]),
        )

    def sum_3(k):
        return (
            remote(9, k, sa.at[lax.rem(k, 2), 1 - x], l3a_ref.at[k], flip["x"]),
            remote(10, k, sb.at[lax.rem(k, 2), 1 - y], l3b_ref.at[k], flip["y"]),
        )

    def sum_z(k):
        copies = []
        for d in range(1, 4):
            there = lax.rem(z + d, z_count)
            copies.append(remote(10 + d, k, ta.at[lax.rem(k, 2), there], lza_ref.at[k, d - 1], up(d)))
            copies.append(remote(13 + d, k, tb.at[lax.rem(k, 2), there], lzb_ref.at[k, d - 1], up(d)))
        return copies

    def load_rows(k):
        slot = lax.rem(k, 2)
        return (
            pltpu.make_async_copy(all_ref.at[:, :, :, :, k], n_buf.at[slot], here.at[slot]),
            pltpu.make_async_copy(g_ref.at[:, :, :, :, k], g_buf.at[slot], here.at[13 + slot]),
        )

    def load_c(k):
        return (
            pltpu.make_async_copy(lca_ref.at[k], ca, here.at[2]),
            pltpu.make_async_copy(lcb_ref.at[k], cb, here.at[3]),
        )

    def load_2(k):
        return (
            pltpu.make_async_copy(l2a_ref.at[k], da, here.at[4]),
            pltpu.make_async_copy(l2b_ref.at[k], db, here.at[5]),
        )

    def load_3(k):
        return (
            pltpu.make_async_copy(l3a_ref.at[k], ea, here.at[6]),
            pltpu.make_async_copy(l3b_ref.at[k], eb, here.at[7]),
        )

    def load_z(k):
        return (
            pltpu.make_async_copy(lza_ref.at[k], fa, here.at[8]),
            pltpu.make_async_copy(lzb_ref.at[k], fb, here.at[9]),
        )

    def store_rows(k):
        return (
            pltpu.make_async_copy(hs_buf, hs_ref.at[:, :, :, :, k], here.at[10]),
            pltpu.make_async_copy(dgu_buf, dgu_ref.at[:, :, :, :, k], here.at[11]),
        )

    def start(copies):
        for copy in copies:
            copy.start()

    def finish(copies):
        for copy in copies:
            copy.wait()

    def at(k, body):
        pl.when((k >= 0) & (k < chunks))(lambda: body(k))

    barrier = pltpu.get_barrier_semaphore()
    for device in (flip["x"], flip["y"], flip["c"], up(1), up(2), up(3)):
        pl.semaphore_signal(
            barrier, inc=1, device_id=device, device_id_type=pl.DeviceIdType.MESH
        )
    pl.semaphore_wait(barrier, 6)

    def first_sends(k, carry):
        heads_c(k).start()
        return carry

    lax.fori_loop(0, chunks, first_sends, 0)
    routed, share = eg_ref.shape[0], sh_ref.shape[1] // 3
    low = pl.ds(routed, share)
    high = pl.ds(width + routed, share)

    def weight_copies():
        pairs = [
            (eg_ref, w_ref.at[pl.ds(0, routed)]),
            (eu_ref, w_ref.at[pl.ds(width, routed)]),
            (ed_ref, d_ref.at[pl.ds(0, routed)]),
            (router_ref.at[0], w_ref.at[pl.ds(width - experts, experts)]),
            (router_ref.at[1], w_ref.at[pl.ds(2 * width - experts, experts)]),
        ]
        cells = model // sh_ref.shape[0]
        for e in range(sh_ref.shape[0]):
            columns = pl.ds(e * cells, cells)
            pairs.append((sh_ref.at[e, pl.ds(0, share)], w_ref.at[low, columns]))
            pairs.append((sh_ref.at[e, pl.ds(share, share)], w_ref.at[high, columns]))
            pairs.append((sh_ref.at[e, pl.ds(2 * share, share)], d_ref.at[low, columns]))
        return [
            pltpu.make_async_copy(src, dst, weigh.at[i]) for i, (src, dst) in enumerate(pairs)
        ]

    start(weight_copies())
    d_ref[pl.ds(width - experts, experts), :] = jnp.zeros((experts, model), jnp.bfloat16)

    def arrive_hc(k):
        heads_c(k).wait()
        start(load_hc(k))

    def arrive_hy(k):
        finish(heads_y(k))
        start(load_hy(k))

    def arrive_hz(k):
        finish(heads_z(k))
        start(load_hz(k))

    def close_hc(k):
        finish(load_hc(k))
        slot = lax.rem(k, 2)

        def each(i, carry):
            for j in range(2):
                rc[slot, j, i] = add_low(ra[j, i], rb[j, i])
            return carry

        lax.fori_loop(0, z_count, each, 0)
        start(heads_y(k))

    def close_hy(k):
        finish(load_hy(k))
        slot = lax.rem(k, 2)
        for i in range(4):
            re[slot, i] = add_low(rc[slot, y, i], rd[i])
        start(heads_z(k))

    def close_hz(k):
        finish(load_hz(k))
        total = re[lax.rem(k, 2), z].astype(jnp.float32)
        for d in range(3):
            total = total + rf[d].astype(jnp.float32)
        hidden = x_ref[k].astype(jnp.float32) + total
        inverse = lax.rsqrt(jnp.mean(hidden * hidden, axis=1, keepdims=True) + EPSILON)
        hidden_ref[k] = hidden
        own_ref[k] = (hidden * inverse * gain_ref[...]).astype(jnp.bfloat16)
        keep(k).start()
        for d in range(1, 4):
            spread_z(k, d).start()

    def gather_2(k):
        keep(k).wait()
        for d in range(1, 4):
            spread_z(k, d).wait()
        start(spread_2(k))

    def gather_3(k):
        finish(spread_2(k))
        start(spread_3(k))

    def gather_c(k):
        finish(spread_3(k))
        start(spread_c(k))

    def gathered(k):
        finish(spread_c(k))
        start(load_rows(k))

    def work(k, part):
        slot = lax.rem(k, 2)
        rows = 256
        normed = n_buf[slot, part].reshape(rows, model)
        grads = g_buf[slot, part].reshape(rows, model + 128)
        routes = grads[:, model : model + 128].astype(jnp.int32)
        grads = grads[:, :model]
        scaled, grad_gate, grad_up, mixture, pushed, gate_sums = expert_rows(
            first, normed, grads, routes, w_ref, d_ref, s_ref, units, experts
        )
        shape = (2, 2, z_count, 16)
        hs_buf[part] = scaled.reshape(shape + (width,))
        dgu_buf[part, :, :, :, :, :width] = grad_gate.reshape(shape + (width,))
        dgu_buf[part, :, :, :, :, width:] = grad_up.reshape(shape + (width,))
        pa[slot, part] = mixture[:, :cut].reshape(shape + (cut,))
        rest = model - cut
        if rest:
            pb[slot, part, :, :, :, :, :rest] = mixture[:, cut:].reshape(shape + (rest,))
        pb[slot, part, :, :, :, :, rest : rest + model] = pushed.reshape(shape + (model,))
        pb[slot, part, :, :, :, :, rest + model :] = gate_sums.reshape(shape + (128,))

    def work_first(k):
        finish(load_rows(k))
        at(k - 1, lambda j: finish(store_rows(j)))
        work(k, 0)

    def work_second(k):
        work(k, 1)
        start(store_rows(k))

    def arrive_c(k):
        finish(sum_c(k))
        start(load_c(k))

    def arrive_2(k):
        finish(sum_2(k))
        start(load_2(k))

    def arrive_3(k):
        finish(sum_3(k))
        start(load_3(k))

    def arrive_z(k):
        finish(sum_z(k))
        start(load_z(k))

    def close_z(k):
        finish(load_z(k))
        slot = lax.rem(k, 2)
        own_a = ta[slot, z].astype(jnp.float32)
        own_b = tb[slot, z].astype(jnp.float32)
        for d in range(3):
            own_a = own_a + fa[d].astype(jnp.float32)
            own_b = own_b + fb[d].astype(jnp.float32)
        out_ref[k, :, :cut] = own_a
        out_ref[k, :, cut:] = own_b

    def close_3(k):
        finish(load_3(k))
        slot = lax.rem(k, 2)

        def each(i, carry):
            ta[slot, i] = add_low(sa[slot, x, i], ea[i])
            tb[slot, i] = add_low(sb[slot, y, i], eb[i])
            return carry

        lax.fori_loop(0, z_count, each, 0)
        start(sum_z(k))

    def close_2(k):
        finish(load_2(k))
        slot = lax.rem(k, 2)

        def each(i, carry):
            for j in range(2):
                sa[slot, j, i] = add_low(qa[slot, y, j, i], da[j, i])
                sb[slot, j, i] = add_low(qb[slot, j, x, i], db[j, i])
            return carry

        lax.fori_loop(0, z_count, each, 0)
        start(sum_3(k))

    def close_c(k):
        finish(load_c(k))
        slot = lax.rem(k, 2)

        def each(i, carry):
            for j in range(2):
                for m in range(2):
                    qa[slot, j, m, i] = add_low(pa[slot, c, j, m, i], ca[j, m, i])
                    qb[slot, j, m, i] = add_low(pb[slot, c, j, m, i], cb[j, m, i])
            return carry

        lax.fori_loop(0, z_count, each, 0)
        start(sum_2(k))

    def tick(i, carry):
        at(i - 11, gathered)
        at(i - 10, gather_c)
        at(i - 8, gather_3)
        at(i - 6, gather_2)
        pl.when(i == 12)(lambda: finish(weight_copies()))
        at(i - 12, work_first)
        at(i - 19, arrive_z)
        at(i - 17, arrive_3)
        at(i - 15, arrive_2)
        at(i - 13, arrive_c)
        at(i - 4, arrive_hz)
        at(i - 2, arrive_hy)
        at(i, arrive_hc)
        at(i - 12, work_second)
        at(i - 4, close_hz)
        at(i - 2, close_hy)
        at(i, close_hc)
        at(i - 19, close_z)
        at(i - 17, close_3)
        at(i - 15, close_2)
        at(i - 13, close_c)
        at(i - 12, lambda k: start(sum_c(k)))
        return carry

    lax.fori_loop(0, chunks + 19, tick, 0)
    finish(store_rows(chunks - 1))


def stream(
    partial, tokens, gain, grads, gates, ups, downs, shared, router, segments, units, experts, chunks
):
    own, model = tokens.shape
    width = segments.shape[0]
    piece = own // chunks
    zs = lax.axis_size("z")
    lead = (2, 2, 2, zs)
    partial = partial.reshape((2, 2, zs, chunks, piece, model))
    grads = grads.reshape(lead + (chunks, piece, model + 128))
    tokens = tokens.reshape(chunks, piece, model)
    cut = model
    extra = 2 * model + 128 - cut
    bf16 = jnp.bfloat16
    shapes = [
        (lead + (chunks, piece, model), bf16),
        (lead + (chunks, piece, width), bf16),
        (lead + (chunks, piece, 2 * width), bf16),
        ((chunks, piece, 2 * model + 128), jnp.float32),
        ((chunks, piece, model), jnp.float32),
        ((chunks, piece, model), bf16),
        ((chunks, 2, zs, piece, model), bf16),
        ((chunks, zs, piece, model), bf16),
        ((chunks, 3, piece, model), bf16),
        ((chunks, 2, 2, zs, piece, cut), bf16),
        ((chunks, 2, 2, zs, piece, extra), bf16),
        ((chunks, 2, zs, piece, cut), bf16),
        ((chunks, 2, zs, piece, extra), bf16),
        ((chunks, zs, piece, cut), bf16),
        ((chunks, zs, piece, extra), bf16),
        ((chunks, 3, piece, cut), bf16),
        ((chunks, 3, piece, extra), bf16),
    ]
    anywhere = pl.BlockSpec(memory_space=pl.ANY)
    inside = pl.BlockSpec(memory_space=pltpu.VMEM)
    vm = pltpu.VMEM
    dma = pltpu.SemaphoreType.DMA
    scratch = [
        vm((2 * width, model), bf16),
        vm((width, model), bf16),
        vm((2,) + lead + (piece, model), bf16),
        vm((2,) + lead + (piece, model + 128), bf16),
        vm((2,) + lead + (piece, cut), bf16),
        vm((2,) + lead + (piece, extra), bf16),
        vm((2, 2, zs, piece, cut), bf16),
        vm((2, 2, zs, piece, extra), bf16),
        vm((2, zs, piece, cut), bf16),
        vm((2, zs, piece, extra), bf16),
        vm((zs, piece, cut), bf16),
        vm((zs, piece, extra), bf16),
        vm((3, piece, cut), bf16),
        vm((3, piece, extra), bf16),
        vm((2, 2, 2, zs, piece, cut), bf16),
        vm((2, 2, 2, zs, piece, extra), bf16),
        vm((2, 2, zs, piece, cut), bf16),
        vm((2, 2, zs, piece, extra), bf16),
        vm((2, zs, piece, cut), bf16),
        vm((2, zs, piece, extra), bf16),
        vm(lead + (piece, width), bf16),
        vm(lead + (piece, 2 * width), bf16),
        vm((2, zs, piece, model), bf16),
        vm((2, zs, piece, model), bf16),
        vm((2, 2, zs, piece, model), bf16),
        vm((zs, piece, model), bf16),
        vm((2, zs, piece, model), bf16),
        vm((3, piece, model), bf16),
        dma((21, 2)),
        dma((3, chunks)),
        dma((chunks,)),
        dma((12, 2)),
        dma((12, chunks)),
        dma((25, chunks)),
        dma((21,)),
        dma((5 + 3 * shared.shape[0],)),
    ]
    rows = own * 8 * zs
    results = pl.pallas_call(
        functools.partial(stream_kernel, units=units, experts=experts),
        in_specs=[anywhere, inside, inside] + [anywhere] * 6 + [inside],
        out_specs=[anywhere] * 3 + [inside] * 3 + [anywhere] * 11,
        out_shape=[jax.ShapeDtypeStruct(s, t) for s, t in shapes],
        scratch_shapes=scratch,
        compiler_params=pltpu.CompilerParams(
            collective_id=1, has_side_effects=True, vmem_limit_bytes=61 * 2**20
        ),
        cost_estimate=pl.CostEstimate(
            flops=12 * rows * model * width,
            bytes_accessed=rows * (14 * model + 6 * width),
            transcendentals=rows * width,
        ),
    )(partial, tokens, gain, grads, gates, ups, downs, shared, router, segments)
    gathered, scaled, slopes, sums, hidden, normed = results[:6]
    return (
        gathered.reshape(rows, model),
        scaled.reshape(rows, width),
        slopes.reshape(rows, 2 * width),
        sums.reshape(own, 2 * model + 128),
        hidden.reshape(own, model),
        normed.reshape(own, model),
    )


def finish_kernel(
    part_ref,
    grads_ref,
    x_ref,
    wp_ref,
    bp_ref,
    w_ref,
    e_ref,
    scale_ref,
    rows_ref,
    dq_ref,
    dk_ref,
    dv_ref,
    do_ref,
    bias_ref,
    gain_ref,
    square_ref,
    extra_ref,
    lc,
    ly,
    lz,
    rc,
    re,
    gt,
    wl,
    bl,
    ws,
    heads_ref,
    gs,
    gl,
    ss,
    sl,
    ls,
    ll,
    lx,
    lu,
    lv,
    send,
    send_k,
    recv,
    once,
    once_in,
    here,
):
    z, x, y, c = (lax.axis_index(name) for name in ALL_AXES)
    z_count = lax.axis_size("z")
    chunks, _, model = x_ref.shape
    head = HEAD_DIM
    flip = {"x": {"x": 1 - x}, "y": {"y": 1 - y}, "c": {"c": 1 - c}}

    def up(distance):
        return {"z": lax.rem(z + distance, z_count)}

    def copy_to(src, dst, send_sem, recv_sem, device):
        return pltpu.make_async_remote_copy(
            src_ref=src,
            dst_ref=dst,
            send_sem=send_sem,
            recv_sem=recv_sem,
            device_id=device,
            device_id_type=pl.DeviceIdType.MESH,
        )

    def heads_c(k):
        return copy_to(
            part_ref.at[1 - c, :, :, k], lc.at[k], send_k.at[k], recv.at[0, k], flip["c"]
        )

    def heads_y(k):
        return copy_to(rc.at[lax.rem(k, 2), 1 - y], ly.at[k], send.at[0, lax.rem(k, 2)], recv.at[1, k], flip["y"])

    def heads_z(k, d):
        there = lax.rem(z + d, z_count)
        return copy_to(
            re.at[lax.rem(k, 2), there], lz.at[k, d - 1], send.at[d, lax.rem(k, 2)], recv.at[1 + d, k], up(d)
        )

    def keep(k):
        return pltpu.make_async_copy(gt.at[k], rows_ref.at[y, c, k], here.at[lax.rem(k, 2)])

    def rows_y(k):
        return copy_to(gt.at[k], rows_ref.at[y, c, k], send.at[4, lax.rem(k, 2)], recv.at[5, k], flip["y"])

    def rows_c(k):
        block = rows_ref.at[:, c, k]
        return copy_to(block, block, send.at[5, lax.rem(k, 2)], recv.at[6, k], flip["c"])

    def single(i, src, dst, device):
        return copy_to(src, dst, once.at[i], once_in.at[i], device)

    def weights_x():
        return (
            single(0, wp_ref.at[1 - x], wl, flip["x"]),
            single(1, bp_ref.at[1 - x], bl, flip["x"]),
        )

    def weights_z(d):
        return single(1 + d, ws.at[lax.rem(z + d, z_count)], heads_ref.at[z], up(d))

    def at(k, body):
        pl.when((k >= 0) & (k < chunks))(lambda: body(k))

    barrier = pltpu.get_barrier_semaphore()
    for device in (flip["x"], flip["y"], flip["c"], up(1), up(2), up(3)):
        pl.semaphore_signal(
            barrier, inc=1, device_id=device, device_id_type=pl.DeviceIdType.MESH
        )
    square_ref[...] = jnp.zeros_like(square_ref)
    pl.semaphore_wait(barrier, 6)

    def first_sends(k, carry):
        heads_c(k).start()
        return carry

    lax.fori_loop(0, chunks, first_sends, 0)
    for copy in weights_x():
        copy.start()

    def close_c(k):
        heads_c(k).wait()
        slot = lax.rem(k, 2)

        def each(i, carry):
            for j in range(2):
                rc[slot, j, i] = add_low(part_ref[c, j, i, k], lc[k, j, i])
            return carry

        lax.fori_loop(0, z_count, each, 0)
        heads_y(k).start()

    def close_y(k):
        heads_y(k).wait()
        slot = lax.rem(k, 2)
        for i in range(4):
            re[slot, i] = add_low(rc[slot, y, i], ly[k, i])
        for d in range(1, 4):
            heads_z(k, d).start()

    def close_z(k):
        for d in range(1, 4):
            heads_z(k, d).wait()
        pushed = re[lax.rem(k, 2), z].astype(jnp.float32)
        for d in range(3):
            pushed = pushed + lz[k, d].astype(jnp.float32)
        values = x_ref[k].astype(jnp.float32)
        inverse = lax.rsqrt(jnp.mean(values * values, axis=1, keepdims=True) + EPSILON)
        scaled = values * inverse
        total = grads_ref[k] + inverse * (
            pushed - scaled * jnp.mean(pushed * scaled, axis=1, keepdims=True)
        )
        gt[k] = total.astype(jnp.bfloat16)
        squares = total * total
        squares = squares[:8] + squares[8:]
        lanes = squares[:, :128]
        for j in range(1, model // 128):
            lanes = lanes + squares[:, j * 128 : (j + 1) * 128]
        square_ref[...] += lanes
        keep(k).start()
        rows_y(k).start()

    def close_rows(k):
        keep(k).wait()
        rows_y(k).wait()
        rows_c(k).start()

    def close_all(k):
        rows_c(k).wait()

    def weights_sum():
        for copy in weights_x():
            copy.wait()
        bias_ref[...] = bp_ref[x].astype(jnp.float32) + bl[...].astype(jnp.float32)

        def each(i, carry):
            ws[i] = add_low(wp_ref[x, i], wl[i])
            return carry

        lax.fori_loop(0, z_count, each, 0)
        heads_ref[z] = ws[z]
        for d in range(1, 4):
            weights_z(d).start()

    def extra_c():
        return single(13, e_ref, ll.at[0], flip["c"])

    def extra_y():
        return single(14, ls, ll.at[1], flip["y"])

    def extra_x():
        return single(15, lx.at[1 - x], lu, flip["x"])

    def extra_z(d):
        return single(15 + d, lx.at[x, lax.rem(z + d, z_count)], lv.at[d - 1], up(d))

    def extra_sum_c():
        extra_c().wait()
        ls[...] = e_ref[...] + ll[0]
        extra_y().start()

    def extra_sum_y():
        extra_y().wait()
        lx[...] = ls[...] + ll[1]
        extra_x().start()

    def extra_sum_x():
        extra_x().wait()
        lx[x] = lx[x] + lu[...]
        for d in range(1, 4):
            extra_z(d).start()

    def gain_y():
        return single(6, gs.at[0], gl.at[0], flip["y"])

    def gain_c():
        return single(8, gs.at[1], gl.at[1], flip["c"])

    def weights_done():
        for d in range(1, 4):
            weights_z(d).wait()
        total = jnp.zeros(gain_ref.shape, jnp.float32)
        scale = scale_ref[...]
        for i in range(4):
            place = slice(i * head, (i + 1) * head)
            for j, ref in enumerate((dq_ref, dk_ref, dv_ref)):
                columns = slice(j * head, (j + 1) * head)
                values = heads_ref[i, :, columns].astype(jnp.float32)
                total = total + w_ref[i, :, columns].astype(jnp.float32) * values
                ref[:, place] = values * scale
            do_ref[place, :] = heads_ref[i, :, 3 * head :].astype(jnp.float32).T
        gs[0] = total
        gain_y().start()

    def gain_sum():
        gain_y().wait()
        gs[1] = gs[0] + gl[0]
        gain_c().start()

    extra_c().start()

    def tick(i, carry):
        at(i - 7, close_all)
        at(i - 6, close_rows)
        at(i - 4, close_z)
        at(i - 2, close_y)
        at(i, close_c)
        pl.when(i == 2)(weights_sum)
        pl.when(i == 2)(extra_sum_c)
        pl.when(i == 4)(extra_sum_y)
        pl.when(i == 6)(extra_sum_x)
        pl.when(i == 7)(weights_done)
        pl.when(i == 9)(gain_sum)
        return carry

    lax.fori_loop(0, chunks + 7, tick, 0)
    for d in range(1, 4):
        extra_z(d).wait()
    extra_ref[...] = lx[x, z] + lv[0] + lv[1] + lv[2]
    ss[0] = square_ref[...]
    squares_c = single(5, ss.at[0], sl.at[0], flip["c"])
    squares_c.start()
    squares_c.wait()
    ss[1] = ss[0] + sl[0]
    squares_y = single(7, ss.at[1], sl.at[1], flip["y"])
    squares_y.start()
    squares_y.wait()
    ss[2] = ss[1] + sl[1]
    squares_x = single(9, ss.at[2], sl.at[2], flip["x"])
    squares_x.start()
    squares_x.wait()
    ss[3] = ss[2] + sl[2]
    squares_z = [single(9 + d, ss.at[3], sl.at[2 + d], up(d)) for d in range(1, 4)]
    for copy in squares_z:
        copy.start()
    gain_c().wait()
    gain_ref[...] = gs[1] + gl[1]
    for copy in squares_z:
        copy.wait()
    square_ref[...] = ss[3] + sl[3] + sl[4] + sl[5]


def finish(partial, grads, tokens, weight_parts, bias_parts, weights, extras, scale, chunks):
    own, model = tokens.shape
    piece = own // chunks
    zs = lax.axis_size("z")
    bf16, f32 = jnp.bfloat16, jnp.float32
    block, wide = weight_parts.shape[2:]
    anywhere = pl.BlockSpec(memory_space=pl.ANY)
    inside = pl.BlockSpec(memory_space=pltpu.VMEM)
    vm = pltpu.VMEM
    dma = pltpu.SemaphoreType.DMA
    rows, d_query, d_key, d_value, d_out, bias, gain, square, extra = pl.pallas_call(
        finish_kernel,
        in_specs=[inside] * 8,
        out_specs=[anywhere] + [inside] * 8,
        out_shape=[
            jax.ShapeDtypeStruct((2, 2, chunks, piece, model), bf16),
            jax.ShapeDtypeStruct((block, wide), f32),
            jax.ShapeDtypeStruct((block, wide), f32),
            jax.ShapeDtypeStruct((block, wide), f32),
            jax.ShapeDtypeStruct((wide, block), f32),
            jax.ShapeDtypeStruct(bias_parts.shape[1:], f32),
            jax.ShapeDtypeStruct((block, 128), f32),
            jax.ShapeDtypeStruct((8, 128), f32),
            jax.ShapeDtypeStruct(extras.shape[2:], f32),
        ],
        scratch_shapes=[
            vm((chunks, 2, zs, piece, model), bf16),
            vm((chunks, zs, piece, model), bf16),
            vm((chunks, 3, piece, model), bf16),
            vm((2, 2, zs, piece, model), bf16),
            vm((2, zs, piece, model), bf16),
            vm((chunks, piece, model), bf16),
            vm((zs, block, wide), bf16),
            vm(bias_parts.shape[1:], bf16),
            vm((zs, block, wide), bf16),
            vm((zs, block, wide), bf16),
            vm((2, block, 128), f32),
            vm((2, block, 128), f32),
            vm((4, 8, 128), f32),
            vm((6, 8, 128), f32),
            vm(extras.shape, f32),
            vm((2,) + extras.shape, f32),
            vm(extras.shape, f32),
            vm(extras.shape[1:], f32),
            vm((3,) + extras.shape[2:], f32),
            dma((6, 2)),
            dma((chunks,)),
            dma((7, chunks)),
            dma((19,)),
            dma((19,)),
            dma((2,)),
        ],
        compiler_params=pltpu.CompilerParams(
            collective_id=2, has_side_effects=True, vmem_limit_bytes=48 * 2**20
        ),
        cost_estimate=pl.CostEstimate(
            flops=100 * own * model, bytes_accessed=40 * 2**20, transcendentals=0
        ),
    )(
        partial.reshape(2, 2, zs, chunks, piece, model),
        grads.reshape(chunks, piece, model),
        tokens.reshape(chunks, piece, model),
        weight_parts,
        bias_parts,
        weights,
        extras,
        scale,
    )
    return rows.reshape(4 * own, model), d_query, d_key, d_value, d_out, bias, gain, square, extra


def weight_grads_kernel(
    n_ref, g_ref, slopes_ref, scaled_ref, gate_ref, up_ref, down_ref, sh_ref, *, units, share
):
    width = scaled_ref.shape[1]
    low = 2 * units
    first = product_at(n_ref[...], slopes_ref[...]).T
    second = product_at(g_ref[...], scaled_ref[...]).T
    for ref, rows in ((gate_ref, first[:width]), (up_ref, first[width:]), (down_ref, second)):
        for i in range(2):
            ref[i] = rows[i * units : (i + 1) * units]
    for i, rows in enumerate((first[:width], first[width:], second)):
        sh_ref[0, i * share : (i + 1) * share] = rows[low : low + share].astype(jnp.bfloat16)


def weight_grads(normed, grads, slopes, scaled, units, share, blocks):
    count, model = normed.shape
    width = scaled.shape[1]
    block = model // blocks
    one = pl.Buffered(1)
    f32, bf16 = jnp.float32, jnp.bfloat16
    rows = pl.BlockSpec((2, units, block), lambda i: (0, 0, i))
    return pl.pallas_call(
        functools.partial(weight_grads_kernel, units=units, share=share),
        grid=(blocks,),
        in_specs=[
            pl.BlockSpec((count, block), lambda i: (0, i)),
            pl.BlockSpec((count, block), lambda i: (0, i)),
            pl.BlockSpec(slopes.shape, lambda i: (0, 0), pipeline_mode=one),
            pl.BlockSpec(scaled.shape, lambda i: (0, 0), pipeline_mode=one),
        ],
        out_specs=[rows, rows, rows, pl.BlockSpec((1, 3 * share, block), lambda i: (i, 0, 0))],
        out_shape=[jax.ShapeDtypeStruct((2, units, model), f32)] * 3
        + [jax.ShapeDtypeStruct((blocks, 3 * share, block), bf16)],
        compiler_params=pltpu.CompilerParams(vmem_limit_bytes=56 * 2**20),
        cost_estimate=pl.CostEstimate(
            flops=6 * count * model * width,
            bytes_accessed=count * (4 * model + 6 * width) + 12 * model * width,
            transcendentals=0,
        ),
    )(normed, grads, slopes, scaled)


def head_grads_kernel(first_ref, hidden_ref, qkv_ref, att_ref, out_ref):
    wide = qkv_ref.shape[1]
    out_ref[0, 0, :, :wide] = product_at(first_ref[...], qkv_ref[...]).astype(jnp.bfloat16)
    out_ref[0, 0, :, wide:] = product_at(hidden_ref[...], att_ref[...]).astype(jnp.bfloat16)


def head_grads(first, hidden, grad_qkv, attended, block):
    count, model = first.shape
    wide = grad_qkv.shape[1] + attended.shape[1]
    blocks = model // block
    return pl.pallas_call(
        head_grads_kernel,
        grid=(blocks,),
        in_specs=[
            pl.BlockSpec((count, block), lambda i: (0, i)),
            pl.BlockSpec((count, block), lambda i: (0, i)),
            pl.BlockSpec(grad_qkv.shape, lambda i: (0, 0)),
            pl.BlockSpec(attended.shape, lambda i: (0, 0)),
        ],
        out_specs=pl.BlockSpec((1, 1, block, wide), lambda i: (i % 2, i // 2, 0, 0)),
        out_shape=jax.ShapeDtypeStruct((2, blocks // 2, block, wide), jnp.bfloat16),
        compiler_params=pltpu.CompilerParams(vmem_limit_bytes=32 * 2**20),
        cost_estimate=pl.CostEstimate(
            flops=2 * count * model * wide, bytes_accessed=5 * count * model, transcendentals=0
        ),
    )(first, hidden, grad_qkv, attended)


def packed(
    tokens,
    cotangent,
    lengths,
    routes,
    w_query,
    w_key,
    w_value,
    w_out,
    b_query,
    b_key,
    b_value,
    gain_attention,
    gain_experts,
    w_router,
    w_shared_gate,
    shared_gate,
    shared_up,
    shared_down,
    expert_gate,
    expert_up,
    expert_down,
    chunks=8,
):
    f32, bf16 = jnp.float32, jnp.bfloat16
    heads_z = lax.axis_size("z")
    exp_count = heads_z * lax.axis_size("x")
    tp_count = lax.axis_size("y") * lax.axis_size("c")
    z_index, x_index = lax.axis_index("z"), lax.axis_index("x")
    exp_index = z_index * lax.axis_size("x") + x_index
    tp_index = lax.axis_index("y") * lax.axis_size("c") + lax.axis_index("c")
    rows, model = tokens.shape
    total_rows = rows * exp_count
    own = rows // tp_count
    block = model // exp_count
    local_experts, _, units = expert_gate.shape
    experts = local_experts * exp_count
    shared_units = shared_gate.shape[1] // exp_count
    head = HEAD_DIM
    length = lengths[0]

    def my_rows(array):
        return lax.dynamic_slice_in_dim(array, tp_index * own, own, 0)

    own_tokens = my_rows(tokens).astype(f32)
    normed_first = (own_tokens * norm_scale(own_tokens)).astype(bf16)
    gain_rows = gain_attention.astype(f32)
    attn_gain_own = gain_rows[:, None]
    query_part, key_part, value_part = (
        (w.astype(f32) * attn_gain_own).astype(bf16).reshape(block, heads_z, head)
        for w in (w_query, w_key, w_value)
    )
    out_part = w_out.reshape(heads_z, head, block).transpose(2, 0, 1)
    attn_parts = jnp.concatenate([query_part, key_part, value_part, out_part], axis=2)
    half_dim = head // 2
    side = x_index * half_dim
    bias_row = jnp.zeros((3, head), bf16)
    bias_row = lax.dynamic_update_slice(
        bias_row, jnp.stack([b_query, b_key, b_value]), (jnp.zeros_like(side), side)
    )
    small = flat([gain_experts, w_router.T, w_shared_gate])
    small = jnp.pad(small, (0, 15 * 4 * head - small.shape[0])).reshape(15, 4 * head)
    small = jnp.concatenate([jnp.pad(bias_row.reshape(1, 3 * head), ((0, 0), (0, head))), small])
    attn_parts = jnp.concatenate(
        [
            attn_parts.transpose(1, 0, 2),
            jnp.broadcast_to(small[None], (heads_z, 16, 4 * head)),
        ],
        axis=1,
    )
    own_first = exp_index * rows + tp_index * own
    own_positions = own_first + jnp.arange(own, dtype=jnp.int32)
    valid = (own_positions < length).astype(f32)[:, None]
    grad_out_low = (my_rows(cotangent).astype(f32) * valid).astype(bf16)
    own_routes = my_rows(routes)
    leaving = jnp.concatenate(
        [grad_out_low, jnp.pad(own_routes.astype(bf16), ((0, 0), (0, 124)), constant_values=-1.0)],
        axis=1,
    )
    first_half, arrived_weights, grad_all = front(normed_first, attn_parts, leaving)
    small = arrived_weights[:, :, block + 1 :].reshape(exp_count, 15 * 4 * head)
    shared_parts = jnp.concatenate(
        [
            w.reshape(exp_count, shared_units, block)
            for w in (shared_gate.T, shared_up.T, shared_down)
        ],
        axis=1,
    )
    place = 0
    ffn_gain = small[:, place : place + block].reshape(model).astype(f32)
    place += block
    router_rows = (
        small[:, place : place + block * experts]
        .reshape(exp_count, experts, block)
        .transpose(1, 0, 2)
        .reshape(experts, model)
    )
    place += block * experts
    share_vector = small[:, place : place + block].reshape(model)

    frequency = np.tile(ROPE_BASE ** (-np.arange(half_dim) * 2.0 / head), 2)
    row_angle = np.arange(own)[:, None] * frequency
    starts = (
        np.arange(2)[:, None, None, None] * rows
        + np.arange(2)[None, :, None, None] * own
        + np.arange(2)[None, None, :, None] * 2 * own
        + np.arange(heads_z)[None, None, None, :] * 2 * rows
    )
    block_angle = starts.reshape(2, -1, 1) * frequency
    row_table = np.stack([np.cos(row_angle), np.sin(row_angle)]).astype(np.float32)
    block_table = np.stack([np.cos(block_angle), np.sin(block_angle)], axis=1).astype(np.float32)
    row_cos, row_sin = jnp.asarray(row_table[:, None, :, :half_dim])
    block_both = lax.dynamic_index_in_dim(jnp.asarray(block_table), x_index, 0, keepdims=False)
    block_cos, block_sin = block_both[:, :, None, :half_dim]
    cosine = (block_cos * row_cos - block_sin * row_sin).reshape(heads_z * rows, half_dim)
    sine = (block_sin * row_cos + block_cos * row_sin).reshape(heads_z * rows, half_dim)

    def rope_back(values):
        one, two = values[:, :half_dim], values[:, half_dim:]
        return jnp.concatenate([one * cosine + two * sine, two * cosine - one * sine], axis=1)

    def by_position(array):
        return (
            array.reshape((2, 2, heads_z, own) + array.shape[1:])
            .transpose(2, 1, 0, 3, 4)
            .reshape(array.shape)
        )

    def by_owner(array):
        return (
            array.reshape((heads_z, 2, 2, own) + array.shape[1:])
            .transpose(2, 1, 0, 3, 4)
            .reshape(array.shape)
        )

    flip = [(0, 1), (1, 0)]
    query_rot, key_values, attended, log_total, attn_part, attn_weights, shared_parts = (
        middle(
            lengths,
            first_half,
            arrived_weights,
            jnp.asarray(row_table),
            jnp.asarray(block_table),
            shared_parts,
            rows,
        )
    )
    info = jnp.stack([x_index, length]).astype(jnp.int32)
    attended_low = by_owner(attended.astype(bf16))
    out_weight = attn_weights[:, 3 * head :]

    width = local_experts * units + shared_units + experts
    router_pair = jnp.stack(
        [router_rows, jnp.pad(share_vector[None, :], ((0, experts - 1), (0, 0)))]
    )
    unit = jnp.arange(width, dtype=jnp.int32)
    segment = jnp.where(
        unit < local_experts * units, exp_index * local_experts + unit // units, experts
    )
    segments = (
        (segment[:, None] == jnp.arange(128, dtype=jnp.int32)[None, :])
        & (unit < width - experts)[:, None]
    ).astype(bf16)
    normed_all, scaled_all, slope_all, mixed_sum, hidden_state, normed = stream(
        attn_part,
        my_rows(tokens),
        ffn_gain[None, :],
        grad_all,
        expert_gate.transpose(0, 2, 1).reshape(local_experts * units, model),
        expert_up.transpose(0, 2, 1).reshape(local_experts * units, model),
        expert_down.reshape(local_experts * units, model),
        shared_parts,
        router_pair,
        segments,
        units,
        experts,
        chunks,
    )
    inverse_second = norm_scale(hidden_state)
    d_expert_gate, d_expert_up, d_expert_down, d_shared = weight_grads(
        normed_all, grad_all, slope_all, scaled_all, units, shared_units, exp_count
    )

    output = valid * (hidden_state + mixed_sum[:, :model])
    mixed = lax.all_gather(output.astype(bf16), COLUMN_AXES, axis=0, tiled=True)

    router_probs = jax.nn.softmax(product_bt(normed, router_rows), axis=1)
    share_weight = jax.nn.sigmoid(product(normed, share_vector))
    chosen = jnp.sum(
        (own_routes[:, :, None] == jnp.arange(experts, dtype=jnp.int32)[None, None, :]).astype(f32),
        axis=1,
    )
    grad_router_probs = chosen * mixed_sum[:, 2 * model : 2 * model + experts]
    grad_share_weight = mixed_sum[:, 2 * model + experts]
    grad_logits = (
        router_probs
        * (grad_router_probs - jnp.sum(grad_router_probs * router_probs, axis=1, keepdims=True))
    ).astype(bf16)
    grad_share_logit = (grad_share_weight * share_weight * (1.0 - share_weight)).astype(bf16)
    grad_normed = (
        mixed_sum[:, model : 2 * model]
        + product(grad_logits, router_rows)
        + grad_share_logit.astype(f32)[:, None] * share_vector.astype(f32)[None, :]
    )
    norm_rows, d_gain_experts = norm_back(grad_normed, hidden_state, inverse_second, ffn_gain)
    grad_hidden = grad_out_low.astype(f32) + norm_rows
    hidden_half = lax.all_gather(grad_hidden.astype(bf16), SAME_X, axis=0, tiled=True)
    router_grads = product_at(
        jnp.concatenate([grad_logits, grad_share_logit[:, None]], axis=1), normed
    )
    extras = jnp.concatenate(
        [
            router_grads,
            d_gain_experts[None, :],
            jnp.broadcast_to(jnp.sum(output * output), (1, model)),
            jnp.zeros((5, model), f32),
        ]
    )
    extras = extras.reshape(-1, heads_z, 2, block).transpose(2, 1, 0, 3)
    hidden_half, d_shared = lax.optimization_barrier((hidden_half, d_shared))
    arrived = lax.all_to_all(d_shared, ROW_AXES, 0, 0, tiled=True).astype(f32)
    d_shared_gate, d_shared_up, d_shared_down = (
        arrived[:, k * shared_units : (k + 1) * shared_units].reshape(
            exp_count * shared_units, block
        )
        for k in range(3)
    )
    d_shared_gate, d_shared_up = d_shared_gate.T, d_shared_up.T
    grad_attended = product(hidden_half, out_weight).astype(bf16)
    scale = 1.0 / head**0.5
    grad_query, grad_key, grad_value = attend_back(
        info, query_rot, key_values, by_position(grad_attended), attended, log_total, rows
    )
    grad_kv = jnp.concatenate([grad_key, grad_value], axis=2).astype(bf16)
    away = lax.ppermute(grad_kv[1], "x", flip)
    grad_kv = by_owner(
        jnp.concatenate([grad_key[0], grad_value[0]], axis=1) + away.astype(f32)
    )
    grad_qkv = jnp.concatenate(
        [
            rope_back(by_owner(grad_query)) * scale,
            rope_back(grad_kv[:, :head]) * scale,
            grad_kv[:, head:],
        ],
        axis=1,
    ).astype(bf16)
    d_attn = head_grads(first_half, hidden_half, grad_qkv, attended_low, block)
    d_biases = jnp.sum(grad_qkv.astype(f32), axis=0).astype(bf16).reshape(3, 2, head // 2)
    d_biases = jnp.pad(
        d_biases.transpose(1, 0, 2).reshape(2, 1, 3 * head // 2),
        ((0, 0), (0, 15), (0, 4 * head - 3 * head // 2)),
    )
    raw = jnp.concatenate(
        [w.reshape(block, heads_z, head) for w in (w_query, w_key, w_value)], axis=2
    ).transpose(1, 0, 2)
    grad_tokens, d_query, d_key, d_value, d_out, d_bias_row, d_gain_attention, squares, extras = finish(
        product_bt(grad_qkv, attn_weights[:, : 3 * head]).astype(bf16),
        grad_hidden,
        my_rows(tokens),
        d_attn,
        d_biases,
        raw,
        extras,
        attn_gain_own,
        chunks,
    )
    d_bias_row = d_bias_row[0]
    d_gain_attention = jnp.sum(d_gain_attention, axis=1)
    half_head = head // 2

    d_router, d_share_vector = extras[:experts].T, extras[experts]
    d_gain_experts = extras[experts + 1]
    cells = length.astype(f32) * model
    rms_output = jnp.sqrt(extras[experts + 2, 0] / cells)
    rms_grad = jnp.sqrt(jnp.sum(squares) / cells)
    return (
        mixed,
        grad_tokens,
        d_query,
        d_key,
        d_value,
        d_out,
        d_bias_row[:half_head],
        d_bias_row[half_head : 2 * half_head],
        d_bias_row[2 * half_head : 3 * half_head],
        d_gain_attention,
        d_gain_experts,
        d_router,
        d_share_vector,
        d_shared_gate,
        d_shared_up,
        d_shared_down,
        d_expert_gate.transpose(0, 2, 1),
        d_expert_up.transpose(0, 2, 1),
        d_expert_down,
        rms_output,
        rms_grad,
    )


def specs(row, column):
    both = column + row
    ins = (
        P(row, None),
        P(row, None),
        P(),
        P(row, None),
        P(row, column),
        P(row, column),
        P(row, column),
        P(column, row),
        P(both),
        P(both),
        P(both),
        P(row),
        P(row),
        P(row, None),
        P(row),
        P(row, column),
        P(row, column),
        P(column, row),
        P(row, None, column),
        P(row, None, column),
        P(row, column, None),
    )
    outs = (
        P(row, None),
        P(row, None),
        P(row, column),
        P(row, column),
        P(row, column),
        P(column, row),
        P(both),
        P(both),
        P(both),
        P(row),
        P(row),
        P(row, None),
        P(row),
        P(row, column),
        P(row, column),
        P(column, row),
        P(row, None, column),
        P(row, None, column),
        P(row, column, None),
        P(),
        P(),
    )
    return ins, outs


def solution(mesh):
    if (mesh.shape["exp"], mesh.shape["tp"]) == (8, 4):
        body, row, column = packed, ROW_AXES, COLUMN_AXES
        mesh = Mesh(mesh.devices.reshape(4, 2, 2, 2), ALL_AXES)
    else:
        body, row, column = general, ("exp",), ("tp",)
    ins, outs = specs(row, column)
    return jax.shard_map(body, mesh=mesh, in_specs=ins, out_specs=outs, check_vma=False)
```
